32 devices in a mesh: dp: 16 (over z, x, core), tensor: 2 (over y).
Axes of the slice: x: 2, y: 2, z: 4, core: 2. Of those that a mesh axis runs over, the one named last changes fastest.
Arguments:
- tokens: bfloat16 [4096, 2048], P('dp'), may hold values from -6 to 6
- cotangent: bfloat16 [4096, 2048], P('dp'), may hold values from -6 to 6
- dealing: int32 [4096], replicated, may hold values from 0 to 4095, as said below
- lengths: int32 [16, 4], P('dp'), may hold values from 1 to 128, 256 in all within a row
- routes: int32 [4096, 8], P('dp'), may hold values from 0 to 15, all different within a row; in each aligned block of 256 rows (0 to 255, 256 to 511, ...) at most 160 rows name the same one
- attention_gain: float32 [2048], P('dp'), may hold values from 0.25 to 1.75
- query_weight: float32 [2048, 2048], P('dp', 'tensor'), may hold values from -0.125 to 0.125
- key_weight: float32 [2048, 2048], P('dp', 'tensor'), may hold values from -0.125 to 0.125
- value_weight: float32 [2048, 2048], P('dp', 'tensor'), may hold values from -0.125 to 0.125
- output_weight: float32 [2048, 2048], P('tensor', 'dp'), may hold values from -0.5 to 0.5
- query_gain: float32 [2, 1024], P('tensor', 'dp'), may hold values from 0.25 to 1.75
- key_gain: float32 [2, 1024], P('tensor', 'dp'), may hold values from 0.25 to 1.75
- ffn_gain: float32 [2048], P('dp'), may hold values from 0.25 to 1.75
- router_weight: float32 [2048, 16], P('dp'), may hold values from -0.0625 to 0.0625
- gate_weight: float32 [16, 2048, 1024], P(None, 'dp', 'tensor'), may hold values from -0.125 to 0.125
- up_weight: float32 [16, 2048, 1024], P(None, 'dp', 'tensor'), may hold values from -0.125 to 0.125
- down_weight: float32 [16, 1024, 2048], P(None, 'tensor', 'dp'), may hold values from -1.5 to 1.5
Outputs:
- block_out: bfloat16 [4096, 2048], P('dp')
- token_grad: bfloat16 [4096, 2048], P('dp')
- attention_gain_grad: float32 [2048], P('dp')
- query_weight_grad: float32 [2048, 2048], P('dp', 'tensor')
- key_weight_grad: float32 [2048, 2048], P('dp', 'tensor')
- value_weight_grad: float32 [2048, 2048], P('dp', 'tensor')
- output_weight_grad: float32 [2048, 2048], P('tensor', 'dp')
- query_gain_grad: float32 [2, 1024], P('tensor', 'dp')
- key_gain_grad: float32 [2, 1024], P('tensor', 'dp')
- ffn_gain_grad: float32 [2048], P('dp')
- router_weight_grad: float32 [2048, 16], P('dp')
- gate_weight_grad: float32 [16, 2048, 1024], P(None, 'dp', 'tensor')
- up_weight_grad: float32 [16, 2048, 1024], P(None, 'dp', 'tensor')
- down_weight_grad: float32 [16, 1024, 2048], P(None, 'tensor', 'dp')
The draws below stay inside these ranges and needn't reach their ends.
Inputs may be any that keep to these rules, and one draw needn't show every extreme that they name: dealing is a permutation; the 256 processed rows of each block take exactly 16 given rows from each block of 256 given rows. `lengths`: each row sums to 256; the longest sequence of each block has 128 rows. `routes`: a row names 8 different experts; among the rows of one device no expert is named more than 160 times, and in some blocks one is named exactly 160 times.
All inputs are finite; a program needn't handle non-finite values.
Results may differ from the reference program's by a relative error of at most 0.018.
The reference program's roundings to bfloat16 on the way count: a program that leaves them out, or rounds other values in their place, can miss the bound.
Values may be sent and summed in bfloat16 or wider, within the bound.
No kernel may reach another device: no remote copies, remote signals or barrier semaphores. Data moves between devices by JAX's collectives and lax.ppermute only.
A program may use at most 320 MiB of HBM per device.

```python
import math
import jax
import jax.numpy as jnp
import numpy as np
from jax import lax

D = 2048
HEADS = 16
HEAD_DIM = 128
FF = 1024
EXPERTS = 16
TOPK = 8
SEQS_DEV = 4
TOK_DEV = 256
CAP = 160
TOKENS = 4096
N_TENSOR = 2


def draw_dealing(key, part):
    block_count = TOKENS // TOK_DEV
    per_peer = TOK_DEV // block_count
    source_key, target_key = jax.random.split(jax.random.fold_in(key, 7))
    source_perm = jax.vmap(lambda inner: jax.random.permutation(inner, TOK_DEV))(jax.random.split(source_key, block_count)).astype(jnp.int32)
    offsets = (jnp.arange(block_count, dtype=jnp.int32) * TOK_DEV)[:, None]
    leaving = (source_perm + offsets).reshape(block_count, block_count, per_peer)
    incoming = jnp.transpose(leaving, (1, 0, 2)).reshape(block_count, TOK_DEV)
    target_perm = jax.vmap(lambda inner: jax.random.permutation(inner, TOK_DEV))(jax.random.split(target_key, block_count)).astype(jnp.int32)
    return jnp.take_along_axis(incoming, target_perm, 1).reshape(TOKENS)


def block_scale(rng, dims, cuts, least, high):
    factor_of, own = 1.0, jax.random.fold_in(rng, 6)
    for axis_at, parts in cuts:
        steps = jnp.exp(jax.random.uniform(jax.random.fold_in(own, axis_at), (parts,), jnp.float32, least / len(cuts), high / len(cuts)))
        factor_of = factor_of * jnp.repeat(steps, dims[axis_at] // parts).reshape([-1 if axis == axis_at else 1 for axis in range(len(dims))])
    return factor_of


def split_up(number_of, total, reach, slope):
    weights = [(1 << 20) // math.isqrt(grade ** slope) + 1 for grade in range(2, number_of + 1)]
    spare, given = total - reach - (number_of - 1), [1] * (number_of - 1)
    while spare > 0:
        candidates = [i for i in range(number_of - 1) if given[i] < reach]
        mass, remaining = sum([weights[i] for i in candidates]), spare
        for i in candidates:
            more = min(reach - given[i], max(1, remaining * weights[i] // mass), spare)
            given[i] = given[i] + more
            spare = spare - more
    return np.array([reach] + given)


def ragged_sizes(stream_key, number_of, total, most, skew):
    if number_of == 2:
        one = jax.random.randint(stream_key, (), max(1, total - most), min(most, total - 1) + 1)
        return jnp.stack([one, total - one])
    tallies = jnp.asarray(split_up(number_of, total, most, skew), jnp.int32)
    twos = (number_of - 1) // 2
    source_of, sink = tallies[1:1 + 2 * twos:2], tallies[2:2 + 2 * twos:2]
    room = jnp.minimum(source_of - 1, most - sink)
    shifted = jax.random.randint(jax.random.fold_in(stream_key, 1), (twos,), 0, 1 << 20) % (room + 1)
    tallies = tallies.at[1:1 + 2 * twos:2].set(source_of - shifted).at[2:2 + 2 * twos:2].set(sink + shifted)
    return tallies[jax.random.permutation(jax.random.fold_in(stream_key, 2), number_of)]


def routed_block(rng, own, number, rows, amount, top, most, slope):
    ranking = jax.random.permutation(rng, amount)
    heavy_load, usual = portions_of(amount, rows * top, most, slope, True), portions_of(amount, rows * top, most, slope, False)
    places = jnp.arange(amount)

    def named(sizes, turn):
        used = int((sizes > 0).sum())
        fixed = max(1, used // 4)
        passed = fixed + (places - fixed + turn * (used - fixed)) % max(1, amount - fixed)
        return jnp.zeros((amount,), jnp.int32).at[ranking[jnp.where(places < fixed, places, passed)]].set(jnp.asarray(sizes, jnp.int32))

    sizes = jnp.where(number % 4 == 0, named(heavy_load, number // 4), named(usual, number - number // 4 - 1))
    mixed = jax.random.permutation(jax.random.fold_in(own, 3), amount)
    giver, sink = mixed[0:amount // 2 * 2:2], mixed[1:amount // 2 * 2:2]
    room = jnp.minimum(sizes[giver] - 1, most - sizes[sink]) // 2
    room = jnp.where((giver == ranking[0]) | (sink == ranking[0]) | (sizes[sink] == 0), 0, jnp.maximum(room, 0))
    passed = jax.random.randint(jax.random.fold_in(own, 4), (amount // 2,), 0, 1 << 20) % (room + 1)
    sizes = sizes.at[giver].add(-passed).at[sink].add(passed)
    items = jnp.searchsorted(jnp.cumsum(sizes), jnp.arange(rows * top), side="right").astype(jnp.int32)
    table = items.reshape(top, rows).T
    table = table[jax.random.permutation(jax.random.fold_in(own, 1), rows)]
    turn = jax.random.randint(jax.random.fold_in(own, 2), (rows, 1), 0, top)
    return jnp.take_along_axis(table, (jnp.arange(top)[None, :] + turn) % top, axis=1)


def portions_of(amount, total, reach, lean, full):
    weights = [(1 << 20) // math.isqrt(standing ** lean) + 1 for standing in range(1, amount + 1)]
    largest = reach if full else min(reach, max(-(-total // amount), total * weights[0] // sum(weights)))
    least = 1 if total - largest >= amount - 1 else 0
    holding, rest = [largest] + [least] * (amount - 1), total - largest - least * (amount - 1)
    while rest > 0:
        free = [i for i in range(1, amount) if holding[i] < largest] or [i for i in range(1, amount) if holding[i] < reach]
        mass, budget = sum([weights[i] for i in free]), rest
        for i in free:
            more = min(reach - holding[i], max(1, budget * weights[i] // mass), rest)
            holding[i] = holding[i] + more
            rest = rest - more
    return np.array(holding)


def normal_values(own_key, extent, scale, limit, cuts=(), held_as=jnp.bfloat16):
    array = jax.random.normal(own_key, extent, jnp.float32) * scale
    if len(cuts) > 0:
        array = block_scale(own_key, extent, cuts, -0.22, 0.18) * array
    return jnp.clip(array, min=-limit, max=limit).astype(held_as)


def setup_inputs(seed: int = 0) -> dict:
    keys = jax.random.split(jax.random.key(seed), 18)
    tokens = normal_values(keys[0], (TOKENS, D), 1.0, 6.0, ((0, 16),))
    cotangent = normal_values(keys[1], (TOKENS, D), 1.0, 6.0, ((0, 16),))
    dealing = draw_dealing(jax.random.fold_in(keys[17], 71), 0)
    lengths = jax.vmap(lambda own: ragged_sizes(own, SEQS_DEV, TOK_DEV, TOK_DEV // 2, 2))(jax.random.split(keys[3], (TOKENS // TOK_DEV))).reshape((TOKENS // TOK_DEV, SEQS_DEV)).astype(jnp.int32)
    routes_keys = jax.random.split(jax.random.fold_in(keys[4], 1), TOKENS // TOK_DEV)
    routes_turns = jax.random.permutation(jax.random.fold_in(keys[4], 3), TOKENS // TOK_DEV)
    routes = jax.vmap(lambda own, number: routed_block(jax.random.fold_in(keys[4], 2), own, number, TOK_DEV, EXPERTS, TOPK, CAP, 1))(routes_keys, routes_turns).reshape((TOKENS, TOPK))
    attention_gain = jnp.clip(1.0 + 0.15 * jax.random.normal(keys[5], (D,), jnp.float32), 0.25, 1.75)
    query_weight = normal_values(keys[6], (D, D), D ** -0.5, 0.125, ((0, 16), (1, 2)), jnp.float32)
    key_weight = normal_values(keys[7], (D, D), D ** -0.5, 0.125, ((0, 16), (1, 2)), jnp.float32)
    value_weight = normal_values(keys[8], (D, D), D ** -0.5, 0.125, ((0, 16), (1, 2)), jnp.float32)
    output_weight = normal_values(keys[9], (D, D), (D // 16) ** -0.5, 0.5, ((0, 2), (1, 16)), jnp.float32)
    query_gain = jnp.clip(1.0 + 0.15 * jax.random.normal(keys[10], (N_TENSOR, D // N_TENSOR), jnp.float32), 0.25, 1.75)
    key_gain = jnp.clip(1.0 + 0.15 * jax.random.normal(keys[11], (N_TENSOR, D // N_TENSOR), jnp.float32), 0.25, 1.75)
    ffn_gain = jnp.clip(1.0 + 0.15 * jax.random.normal(keys[12], (D,), jnp.float32), 0.25, 1.75)
    router_weight = normal_values(keys[13], (D, EXPERTS), (4 * D) ** -0.5, 0.0625, ((0, 16),), jnp.float32)
    gate_weight = normal_values(keys[14], (EXPERTS, D, FF), D ** -0.5, 0.125, ((1, 16), (2, 2)), jnp.float32)
    up_weight = normal_values(keys[15], (EXPERTS, D, FF), D ** -0.5, 0.125, ((1, 16), (2, 2)), jnp.float32)
    down_weight = normal_values(keys[16], (EXPERTS, FF, D), (max(FF // 64, 1)) ** -0.5, 1.5, ((1, 2), (2, 16)), jnp.float32)
    return {"tokens": tokens, "cotangent": cotangent, "dealing": dealing, "lengths": lengths, "routes": routes, "attention_gain": attention_gain, "query_weight": query_weight, "key_weight": key_weight, "value_weight": value_weight, "output_weight": output_weight, "query_gain": query_gain, "key_gain": key_gain, "ffn_gain": ffn_gain, "router_weight": router_weight, "gate_weight": gate_weight, "up_weight": up_weight, "down_weight": down_weight}


EPS = 1e-05
ROPE_BASE = 10000.0
MASKED = -1e+30
HIGHEST = lax.Precision.HIGHEST

@jax.custom_vjp
def low(v):
    return lax.optimization_barrier(v.astype(jnp.bfloat16)).astype(jnp.float32)

@jax.custom_vjp
def low_back(v):
    return v

def low_keep(v):
    return (low(v), None)

def low_pass(kept, grad):
    return (grad,)

def back_keep(v):
    return (v, None)

def back_low(kept, grad):
    return (low(grad),)
low.defvjp(low_keep, low_pass)
low_back.defvjp(back_keep, back_low)

def matmul_high(left, right):
    return jnp.dot(left, right, precision=HIGHEST)

def row_scale(values):
    return lax.rsqrt(lax.optimization_barrier(jnp.mean(values * values, -1, keepdims=True)) + EPS)

def softmax_rows(values):
    peak_value = lax.optimization_barrier(jnp.max(values, -1, keepdims=True))
    powered = jnp.exp(values - peak_value)
    return powered / lax.optimization_barrier(jnp.sum(powered, -1, keepdims=True))

def segment_layout(seq_lengths, row_count):
    finish_at = jnp.cumsum(seq_lengths).astype(jnp.int32)
    start_at = finish_at - seq_lengths
    places = jnp.arange(row_count, dtype=jnp.int32)
    segment_ids = lax.optimization_barrier(jnp.sum((places[:, None] >= finish_at[None, :]).astype(jnp.int32), -1))
    numbers = jnp.arange(seq_lengths.shape[0], dtype=jnp.int32)
    begins = lax.optimization_barrier(jnp.sum(jnp.where(segment_ids[:, None] == numbers[None, :], start_at[None, :], 0), -1))
    return (segment_ids, places - begins)

def rope_tables(positions, head_size):
    half_size = head_size // 2
    freq_table = ROPE_BASE ** (-2.0 * jnp.arange(half_size, dtype=jnp.float32) / head_size)
    angles = positions[:, None] * freq_table[None, :]
    angles = jnp.concatenate([angles, angles], -1)
    return (jnp.cos(angles), jnp.sin(angles))

def rotate_heads(values, cosine_table, sine_table):
    half_size = values.shape[-1] // 2
    turned = jnp.concatenate([-values[..., half_size:], values[..., :half_size]], -1)
    return values * cosine_table[:, None, :] + turned * sine_table[:, None, :]

def slot_table(expert_rows, expert_count, capacity):
    row_count, route_count = expert_rows.shape
    flat_ids = expert_rows.reshape(-1).astype(jnp.int32)
    matches = (flat_ids[:, None] == jnp.arange(expert_count, dtype=jnp.int32)[None, :]).astype(jnp.int32)
    earlier = jnp.cumsum(matches, 0) - matches
    slots = lax.optimization_barrier(jnp.sum(earlier * matches, -1)).astype(jnp.int32)
    cell_ids = flat_ids * capacity + slots
    owners = jnp.arange(row_count * route_count, dtype=jnp.int32) // route_count
    slot_owner = jnp.full((expert_count * capacity,), row_count, jnp.int32).at[cell_ids].set(owners)
    return (slot_owner, cell_ids)

def layer_rows(rows_in, seq_lengths, expert_rows, rounded):
    first_gain, query_full, key_full, value_full, output_full, query_scale_gain, key_scale_gain, second_gain, router_full, gate_full, up_full, down_full = rounded
    row_count = rows_in.shape[0]
    segment_ids, positions = segment_layout(seq_lengths, row_count)
    cosine_table, sine_table = rope_tables(positions.astype(jnp.float32), HEAD_DIM)
    places = jnp.arange(row_count, dtype=jnp.int32)
    allowed = (segment_ids[:, None] == segment_ids[None, :]) & (places[None, :] <= places[:, None])
    normed_one = low(rows_in * row_scale(rows_in) * first_gain)
    query_raw = low_back(matmul_high(normed_one, query_full))
    key_raw = low_back(matmul_high(normed_one, key_full))
    value_rows = low(low_back(matmul_high(normed_one, value_full)))
    query_normed = query_raw * row_scale(query_raw) * query_scale_gain
    key_normed = key_raw * row_scale(key_raw) * key_scale_gain
    query_heads = low(rotate_heads(query_normed.reshape(row_count, HEADS, HEAD_DIM), cosine_table, sine_table))
    key_heads = low(rotate_heads(key_normed.reshape(row_count, HEADS, HEAD_DIM), cosine_table, sine_table))
    value_heads = value_rows.reshape(row_count, HEADS, HEAD_DIM)
    raw_scores = low_back(jnp.einsum('qhd,khd->hqk', query_heads, key_heads, precision=HIGHEST) * HEAD_DIM ** (-0.5))
    probs = low(softmax_rows(jnp.where(allowed[None], raw_scores, MASKED)))
    context = jnp.einsum('hqk,khd->qhd', probs, value_heads, precision=HIGHEST).reshape(row_count, D)
    context = low(low_back(context))
    attention = low_back(matmul_high(context, output_full))
    hidden = rows_in + attention
    normed_two = low(hidden * row_scale(hidden) * second_gain)
    logits = low_back(matmul_high(normed_two, router_full))
    gate_values = jnp.take_along_axis(softmax_rows(logits), expert_rows, 1)
    slot_owner, cell_ids = slot_table(expert_rows, EXPERTS, CAP)
    padded_rows = jnp.concatenate([normed_two, jnp.zeros((1, D), jnp.float32)], 0)
    dispatched = padded_rows[slot_owner].reshape(EXPERTS, CAP, D)
    gate_pre = low_back(jnp.einsum('ecd,edf->ecf', dispatched, gate_full, precision=HIGHEST))
    up_pre = low_back(jnp.einsum('ecd,edf->ecf', dispatched, up_full, precision=HIGHEST))
    active = low(gate_pre / (1.0 + jnp.exp(-gate_pre)) * up_pre)
    produced = low_back(jnp.einsum('ecf,efd->ecd', active, down_full, precision=HIGHEST)).reshape(EXPERTS * CAP, D)
    gate_cells = jnp.zeros((EXPERTS * CAP,), jnp.float32).at[cell_ids].set(gate_values.reshape(-1))
    mixture = jnp.zeros((row_count + 1, D), jnp.float32).at[slot_owner].add(produced * gate_cells[:, None])
    return hidden + mixture[:row_count]

def reference(tokens, cotangent, dealing, lengths, routes, attention_gain, query_weight, key_weight, value_weight, output_weight, query_gain, key_gain, ffn_gain, router_weight, gate_weight, up_weight, down_weight):
    block_count = TOKENS // TOK_DEV
    masters = (attention_gain, query_weight, key_weight, value_weight, output_weight, query_gain, key_gain, ffn_gain, router_weight, gate_weight, up_weight, down_weight)

    def forward(rows_given, master_set):
        rounded = tuple((low(master) for master in master_set))
        rounded = rounded[:5] + (rounded[5].reshape(-1), rounded[6].reshape(-1)) + rounded[7:]
        processed = rows_given[dealing].reshape(block_count, TOK_DEV, D)
        route_blocks = routes.reshape(block_count, TOK_DEV, TOPK)

        def one_block(pieces):
            return layer_rows(pieces[0], pieces[1], pieces[2], rounded)
        outputs = lax.map(jax.checkpoint(one_block), (processed, lengths, route_blocks))
        return jnp.zeros_like(rows_given).at[dealing].set(outputs.reshape(TOKENS, D))
    result, pullback = jax.vjp(forward, tokens.astype(jnp.float32), masters)
    rows_grad, master_grads = pullback(cotangent.astype(jnp.float32))
    return (result.astype(jnp.bfloat16), rows_grad.astype(jnp.bfloat16), master_grads[0], master_grads[1], master_grads[2], master_grads[3], master_grads[4], master_grads[5], master_grads[6], master_grads[7], master_grads[8], master_grads[9], master_grads[10], master_grads[11])
```

```python
import jax
import jax.numpy as jnp
from jax import lax
from jax.sharding import PartitionSpec as P

HEAD_DIM = 128
EXPERTS = 16
EPS = 1e-05
ROPE_BASE = 10000.0
MASKED = -1e30
F32 = jnp.float32
BF16 = jnp.bfloat16


def row_scale(values):
    return lax.rsqrt(jnp.mean(values * values, -1, keepdims=True) + EPS)


def mm(left, right):
    return lax.dot_general(left, right, (((1,), (0,)), ((), ())), preferred_element_type=F32)


def inner_rows(left, right):
    return lax.dot_general(left, right, (((0,), (0,)), ((), ())), preferred_element_type=F32)


def outer_cols(left, right):
    return lax.dot_general(left, right, (((1,), (1,)), ((), ())), preferred_element_type=F32)


def rope_tables(positions, head_size):
    half_size = head_size // 2
    freq_table = ROPE_BASE ** (-2.0 * jnp.arange(half_size, dtype=F32) / head_size)
    angles = positions[:, None] * freq_table[None, :]
    angles = jnp.concatenate([angles, angles], -1)
    return (jnp.cos(angles), jnp.sin(angles))


def rotate_heads(values, cosine_table, sine_table):
    half_size = values.shape[-1] // 2
    turned = jnp.concatenate([-values[..., half_size:], values[..., :half_size]], -1)
    return values * cosine_table[:, None, :] + turned * sine_table[:, None, :]


def unrotate_heads(grads, cosine_table, sine_table):
    half_size = grads.shape[-1] // 2
    scaled = grads * sine_table[:, None, :]
    turned = jnp.concatenate([scaled[..., half_size:], -scaled[..., :half_size]], -1)
    return grads * cosine_table[:, None, :] + turned


def ring_chip(place, chips):
    return 2 * place if place < chips // 2 else 2 * (chips - 1 - place) + 1


def ring_pairs(chips, step):
    pairs = []
    for first in range(0, lax.axis_size("dp"), 2 * chips):
        for place in range(chips):
            here = ring_chip(place, chips)
            there = ring_chip((place + step) % chips, chips)
            for core in range(2):
                pairs.append((first + 2 * here + core, first + 2 * there + core))
    return pairs


def ring_place(chips):
    chip = (lax.axis_index("dp") // 2) % chips
    return jnp.where(chip % 2 == 0, chip // 2, chips - 1 - chip // 2)


def to_sibling(values):
    pairs = [(index, index ^ 1) for index in range(lax.axis_size("dp"))]
    return lax.ppermute(values, "dp", pairs)


def to_peer(values):
    return lax.ppermute(values, "tensor", [(0, 1), (1, 0)])


def ring_gather(block, chips):
    upward, downward = ring_pairs(chips, 1), ring_pairs(chips, -1)
    lane = [block] + [None] * (chips - 1)
    rising = falling = block
    for step in range(1, chips // 2):
        rising = lax.ppermute(rising, "dp", upward)
        falling = lax.ppermute(falling, "dp", downward)
        lane[chips - step] = rising
        lane[step] = falling
    half = block.shape[0] // 2
    rising = lax.ppermute(rising[:half], "dp", upward)
    falling = lax.ppermute(falling[half:], "dp", downward)
    lane[chips // 2] = jnp.concatenate([rising, falling], 0)
    return [(mine, to_sibling(mine)) for mine in lane]


def ring_scatter(parts, chips, wire):
    upward, downward = ring_pairs(chips, 1), ring_pairs(chips, -1)
    total = [None] * chips
    half_way = chips // 2
    farthest_first = [half_way]
    for step in range(half_way - 1, 0, -1):
        farthest_first += [step, chips - step]
    for offset in farthest_first + [0]:
        mine, other = parts[offset]
        total[offset] = mine.astype(F32) + to_sibling(other.astype(wire)).astype(F32)
    half = total[0].shape[0] // 2
    rising = lax.ppermute(total[half_way][:half].astype(wire), "dp", upward)
    falling = lax.ppermute(total[half_way][half:].astype(wire), "dp", downward)
    for step in range(half_way - 1, -1, -1):
        above, below = total[step], total[(chips - step) % chips]
        rising, falling = rising.astype(F32), falling.astype(F32)
        if step == half_way - 1:
            pad = jnp.zeros_like(rising)
            rising = jnp.concatenate([rising, pad], 0)
            falling = jnp.concatenate([pad, falling], 0)
        if step == 0:
            return above + rising + falling
        rising = lax.ppermute((above + rising).astype(wire), "dp", upward)
        falling = lax.ppermute((below + falling).astype(wire), "dp", downward)


def roll_columns(values, start):
    width = values.shape[1]
    return lax.dynamic_slice_in_dim(jnp.concatenate([values, values], 1), start, width, 1)


def swap_cores(values, chips):
    rows, width = values.shape
    piece = width // (2 * chips)
    pieces = [values[:, at * piece : (at + 1) * piece] for at in range(2 * chips)]
    swapped = jnp.concatenate([pieces[at ^ 1] for at in range(2 * chips)], 1)
    return jnp.where(lax.axis_index("dp") % 2 == 0, values, swapped)


def to_ring_order(values, chips):
    piece = values.shape[1] // chips
    order = [ring_chip(place, chips) for place in range(chips)]
    placed = jnp.concatenate([values[:, at * piece : (at + 1) * piece] for at in order], 1)
    return swap_cores(roll_columns(placed, ring_place(chips) * piece), chips)


def from_ring_order(values, chips):
    piece = values.shape[1] // chips
    order = [ring_chip(place, chips) for place in range(chips)]
    back = [order.index(chip) for chip in range(chips)]
    place = ring_place(chips)
    placed = roll_columns(swap_cores(values, chips), lax.rem(chips - place, chips) * piece)
    return jnp.concatenate([placed[:, at * piece : (at + 1) * piece] for at in back], 1)


def stacked(pairs):
    return jnp.concatenate([block for pair in pairs for block in pair], 0)


def unstacked(values, chips):
    size = values.shape[0] // (2 * chips)
    pieces = [values[at * size : (at + 1) * size] for at in range(2 * chips)]
    return [(pieces[2 * at], pieces[2 * at + 1]) for at in range(chips)]


def expert_exchange(chunks):
    count = lax.axis_size("dp")
    groups = [list(range(at, at + EXPERTS)) for at in range(0, count, EXPERTS)]
    kwargs = {} if len(groups) == 1 else {"axis_index_groups": groups}
    return lax.all_to_all(chunks, "dp", split_axis=0, concat_axis=0, tiled=True, **kwargs)


def body(
    tokens,
    cotangent,
    dealing,
    lengths,
    routes,
    attention_gain,
    query_weight,
    key_weight,
    value_weight,
    output_weight,
    query_gain,
    key_gain,
    ffn_gain,
    router_weight,
    gate_weight,
    up_weight,
    down_weight,
):
    groups = lax.axis_size("dp")
    me = lax.axis_index("dp")
    side = lax.axis_index("tensor")
    rows_here, model_width = tokens.shape
    per_peer = rows_here // groups
    half_peer = per_peer // 2
    half_rows = rows_here // 2
    chips = groups // 2
    moe_chips = EXPERTS // 2
    replicas = groups // EXPERTS
    expert = lax.rem(me, EXPERTS)

    dealt = dealing.reshape(groups, rows_here)
    places = jnp.arange(rows_here, dtype=jnp.int32)
    source_block = dealt // rows_here
    packed = (source_block * rows_here + places[None, :]) * rows_here + lax.rem(dealt, rows_here)
    packed = jnp.sort(packed, axis=1)
    leaving = lax.rem(
        lax.dynamic_slice_in_dim(packed, me * per_peer, per_peer, 1), rows_here
    ).reshape(groups, 2, half_peer)
    own_order = lax.rem(
        lax.dynamic_index_in_dim(packed, me, 0, keepdims=False) // rows_here, rows_here
    ).reshape(groups, 2, half_peer)

    def by_side(table):
        first, second = table[:, 0].reshape(-1), table[:, 1].reshape(-1)
        return jnp.concatenate(
            [jnp.where(side == 0, first, second), jnp.where(side == 0, second, first)]
        )

    leaving = by_side(leaving)
    own_order = by_side(own_order)
    pick = (leaving[:half_rows, None] == places[None, :]).astype(BF16)
    sent = jnp.concatenate(
        [
            mm(pick, tokens).astype(BF16).reshape(groups, half_peer, model_width),
            mm(pick, cotangent).astype(BF16).reshape(groups, half_peer, model_width),
        ],
        1,
    )
    got = lax.all_to_all(sent, "dp", split_axis=0, concat_axis=0, tiled=True)
    rows = got[:, :half_peer].reshape(half_rows, model_width).astype(F32)
    cot_rows = got[:, half_peer:].reshape(half_rows, model_width)

    small = jnp.concatenate(
        [
            attention_gain,
            ffn_gain,
            query_gain.reshape(-1),
            key_gain.reshape(-1),
            router_weight.reshape(-1),
        ]
    ).astype(BF16)
    small = lax.all_gather(small[None], "dp", axis=0, tiled=True)
    shard = attention_gain.shape[0]
    gain_shard = query_gain.shape[1]
    first_gain = small[:, :shard].reshape(-1).astype(F32)
    second_gain = small[:, shard : 2 * shard].reshape(-1).astype(F32)
    at = 2 * shard
    query_scale_gain = small[:, at : at + gain_shard].reshape(-1).astype(F32)
    key_scale_gain = small[:, at + gain_shard : at + 2 * gain_shard].reshape(-1).astype(F32)
    router_full = small[:, at + 2 * gain_shard :].reshape(model_width, EXPERTS)

    qkv_block = jnp.concatenate([query_weight, key_weight, value_weight], 1).astype(BF16)
    qkv_full = stacked(ring_gather(qkv_block, chips))
    output_full = stacked(ring_gather(output_weight.T.astype(BF16), chips))
    heads_width = query_weight.shape[1]

    expert_block = jnp.concatenate(
        [gate_weight.astype(BF16), up_weight.astype(BF16), down_weight.astype(BF16).swapaxes(1, 2)],
        2,
    )
    hidden_half = gate_weight.shape[2]
    expert_own = expert_exchange(expert_block).reshape(-1, 3 * hidden_half)
    across = [list(range(at, groups, EXPERTS)) for at in range(EXPERTS)]
    if replicas > 1:
        expert_own = lax.all_gather(
            expert_own, "dp", axis=0, tiled=True, axis_index_groups=across
        )
    expert_peer = to_peer(expert_own)

    cot_all = stacked(ring_gather(cot_rows, moe_chips))

    finish_at = jnp.cumsum(lengths[0])
    start_at = finish_at - lengths[0]
    segment_ids = jnp.sum((own_order[:, None] >= finish_at[None, :]).astype(jnp.int32), -1)
    numbers = jnp.arange(lengths.shape[1], dtype=jnp.int32)
    begins = jnp.sum(jnp.where(segment_ids[:, None] == numbers[None, :], start_at[None, :], 0), -1)
    cosine_table, sine_table = rope_tables((own_order - begins).astype(F32), HEAD_DIM)
    allowed = (segment_ids[:, None] == segment_ids[None, :]) & (
        own_order[None, :] <= own_order[:, None]
    )
    head_scale = HEAD_DIM ** (-0.5)

    expert_ids = jnp.arange(EXPERTS, dtype=jnp.int32)
    uses = jnp.sum((routes[:, :, None] == expert_ids[None, None, :]).astype(F32), 1)
    reorder = (own_order[:half_rows, None] == places[None, :]).astype(BF16)
    used = mm(reorder, uses.astype(BF16))

    norm_one = row_scale(rows)
    normed_own = (rows * norm_one * first_gain).astype(BF16)
    normed_one = to_ring_order(jnp.concatenate([normed_own, to_peer(normed_own)], 0), chips)
    qkv = mm(normed_one, qkv_full)
    query_raw, key_raw = qkv[:, :heads_width], qkv[:, heads_width : 2 * heads_width]
    value_rows = qkv[:, 2 * heads_width :].astype(BF16)

    def over_sides(values):
        theirs = to_peer(values)
        return values + jnp.concatenate([theirs[:, half_rows:], theirs[:, :half_rows]], 1)

    squares = over_sides(
        jnp.stack([jnp.sum(query_raw * query_raw, -1), jnp.sum(key_raw * key_raw, -1)])
    )
    query_scale = lax.rsqrt(squares[0] / model_width + EPS)[:, None]
    key_scale = lax.rsqrt(squares[1] / model_width + EPS)[:, None]
    heads_here = heads_width // HEAD_DIM
    query_normed = query_raw * query_scale * query_scale_gain
    key_normed = key_raw * key_scale * key_scale_gain
    query_heads = rotate_heads(
        query_normed.reshape(rows_here, heads_here, HEAD_DIM), cosine_table, sine_table
    ).astype(BF16)
    key_heads = rotate_heads(
        key_normed.reshape(rows_here, heads_here, HEAD_DIM), cosine_table, sine_table
    ).astype(BF16)
    value_heads = value_rows.reshape(rows_here, heads_here, HEAD_DIM)

    def attention_scores(query_part, key_part):
        raw_scores = (
            jnp.einsum("qhd,khd->hqk", query_part, key_part, preferred_element_type=F32)
            * head_scale
        )
        return jnp.where(allowed[None], raw_scores, MASKED)

    masked_scores = attention_scores(query_heads, key_heads)
    peak_value = jnp.max(masked_scores, -1, keepdims=True)
    powered = jnp.exp(masked_scores - peak_value)
    total_weight = jnp.sum(powered, -1, keepdims=True)
    probs = powered / total_weight
    log_total = peak_value + jnp.log(total_weight)
    context = jnp.einsum(
        "hqk,khd->qhd", probs.astype(BF16), value_heads, preferred_element_type=F32
    )
    context = context.reshape(rows_here, -1).astype(BF16)
    attention = outer_cols(context, output_full)
    attention = attention[:half_rows] + to_peer(attention[half_rows:].astype(BF16)).astype(F32)
    hidden = rows + from_ring_order(attention, chips)

    norm_two = row_scale(hidden)
    normed_two = (hidden * norm_two * second_gain).astype(BF16)
    logits = mm(normed_two, router_full)
    powered_two = jnp.exp(logits - jnp.max(logits, -1, keepdims=True))
    router_probs = powered_two / jnp.sum(powered_two, -1, keepdims=True)
    gate_table = (router_probs * used).T

    inputs_all = stacked(ring_gather(normed_two, moe_chips))
    gate_blocks = jnp.stack([b for pair in ring_gather(gate_table, moe_chips) for b in pair])
    gates = lax.dynamic_index_in_dim(gate_blocks, expert, 1, keepdims=False).reshape(-1, 1)
    out_cells = (cot_all.astype(F32) * gates).astype(BF16)
    halves = []
    for weights in (expert_own, expert_peer):
        front = mm(inputs_all, weights[:, : 2 * hidden_half])
        gate_pre, up_pre = front[:, :hidden_half], front[:, hidden_half:]
        sigmoid_gate = 1.0 / (1.0 + jnp.exp(-gate_pre))
        active = (gate_pre * sigmoid_gate * up_pre).astype(BF16)
        active_grad = mm(out_cells, weights[:, 2 * hidden_half :])
        gate_grad = (
            active_grad * up_pre * sigmoid_gate * (1.0 + gate_pre * (1.0 - sigmoid_gate))
        ).astype(BF16)
        up_grad = (active_grad * gate_pre * sigmoid_gate).astype(BF16)
        halves.append((active, jnp.concatenate([gate_grad, up_grad], 1), weights))
    input_grad = sum(outer_cols(grad, w[:, : 2 * hidden_half]) for _, grad, w in halves)
    produced = sum(outer_cols(active, w[:, 2 * hidden_half :]) for active, _, w in halves)
    mixing = jnp.sum(produced * cot_all.astype(F32), -1)
    expert_wgrads = [
        jnp.concatenate([inner_rows(inputs_all, grad), inner_rows(out_cells, active)], 1)
        for active, grad, _ in halves
    ]

    normed_two_grad = ring_scatter(unstacked(input_grad, moe_chips), moe_chips, BF16)
    mine = (expert_ids == expert).astype(F32)[None, :, None]
    mixing_table = (mixing.reshape(EXPERTS, 1, half_rows) * mine).reshape(-1, half_rows)
    mixing_table = ring_scatter(unstacked(mixing_table, moe_chips), moe_chips, F32)
    mixture = ring_scatter(unstacked(produced * gates, moe_chips), moe_chips, BF16)
    out_rows = (hidden + mixture).astype(BF16)

    expert_wgrad = expert_wgrads[0] + to_peer(expert_wgrads[1].astype(BF16)).astype(F32)
    expert_wgrad = expert_wgrad.astype(BF16)
    if replicas > 1:
        expert_wgrad = lax.psum_scatter(
            expert_wgrad, "dp", scatter_dimension=0, tiled=True, axis_index_groups=across
        )
    wgrads = expert_exchange(expert_wgrad.reshape(EXPERTS, -1, 3 * hidden_half))
    gate_weight_grad = wgrads[:, :, :hidden_half].astype(F32)
    up_weight_grad = wgrads[:, :, hidden_half : 2 * hidden_half].astype(F32)
    down_weight_grad = wgrads[:, :, 2 * hidden_half :].swapaxes(1, 2).astype(F32)

    prob_grad = mixing_table.T * used
    logit_grad = (
        router_probs * (prob_grad - jnp.sum(router_probs * prob_grad, -1, keepdims=True))
    ).astype(BF16)
    router_wgrad = inner_rows(normed_two, logit_grad)
    normed_two_grad = normed_two_grad + outer_cols(logit_grad, router_full)
    ffn_gain_grad = jnp.sum(normed_two_grad * hidden * norm_two, 0)
    scaled_two = normed_two_grad * second_gain
    hidden_grad = cot_rows.astype(F32) + norm_two * (
        scaled_two - hidden * norm_two * norm_two * jnp.mean(scaled_two * hidden, -1, keepdims=True)
    )

    attn_own = hidden_grad.astype(BF16)
    attn_grad = to_ring_order(jnp.concatenate([attn_own, to_peer(attn_own)], 0), chips)
    output_wgrad = inner_rows(attn_grad, context)
    output_wgrad = ring_scatter(unstacked(output_wgrad, chips), chips, BF16)
    context_grad = mm(attn_grad, output_full).astype(BF16)
    context_grad = context_grad.reshape(rows_here, heads_here, HEAD_DIM)
    recomputed = jnp.exp(attention_scores(query_heads, key_heads) - log_total)
    prob_pair_grad = jnp.einsum(
        "qhd,khd->hqk", context_grad, value_heads, preferred_element_type=F32
    )
    value_grad = jnp.einsum(
        "hqk,qhd->khd", recomputed.astype(BF16), context_grad, preferred_element_type=F32
    )
    value_grad = value_grad.reshape(rows_here, -1).astype(BF16)
    score_grad = (
        recomputed * (prob_pair_grad - jnp.sum(recomputed * prob_pair_grad, -1, keepdims=True))
    ).astype(BF16)
    query_rot_grad = (
        jnp.einsum("hqk,khd->qhd", score_grad, key_heads, preferred_element_type=F32) * head_scale
    )
    key_rot_grad = (
        jnp.einsum("hqk,qhd->khd", score_grad, query_heads, preferred_element_type=F32)
        * head_scale
    )
    query_norm_grad = unrotate_heads(query_rot_grad, cosine_table, sine_table).reshape(
        rows_here, -1
    )
    key_norm_grad = unrotate_heads(key_rot_grad, cosine_table, sine_table).reshape(rows_here, -1)
    inners = over_sides(
        jnp.stack(
            [
                jnp.sum(query_norm_grad * query_scale_gain * query_raw, -1),
                jnp.sum(key_norm_grad * key_scale_gain * key_raw, -1),
            ]
        )
    )
    query_gain_grad = jnp.sum(query_norm_grad * query_raw * query_scale, 0)
    key_gain_grad = jnp.sum(key_norm_grad * key_raw * key_scale, 0)
    query_raw_grad = (
        query_scale * query_scale_gain * query_norm_grad
        - query_raw * query_scale**3 * inners[0][:, None] / model_width
    ).astype(BF16)
    key_raw_grad = (
        key_scale * key_scale_gain * key_norm_grad
        - key_raw * key_scale**3 * inners[1][:, None] / model_width
    ).astype(BF16)
    qkv_grad = jnp.concatenate([query_raw_grad, key_raw_grad, value_grad], 1)
    qkv_wgrad = ring_scatter(
        unstacked(inner_rows(normed_one, qkv_grad), chips), chips, BF16
    )
    normed_one_grad = outer_cols(qkv_grad, qkv_full)
    normed_one_grad = normed_one_grad[:half_rows] + to_peer(
        normed_one_grad[half_rows:].astype(BF16)
    ).astype(F32)
    normed_one_grad = from_ring_order(normed_one_grad, chips)
    attention_gain_grad = jnp.sum(normed_one_grad * rows * norm_one, 0)
    scaled_one = normed_one_grad * first_gain
    rows_grad = hidden_grad + norm_one * (
        scaled_one - rows * norm_one * norm_one * jnp.mean(scaled_one * rows, -1, keepdims=True)
    )

    small_grad = jnp.concatenate(
        [
            query_gain_grad.reshape(groups, -1),
            key_gain_grad.reshape(groups, -1),
            attention_gain_grad.reshape(groups, -1),
            ffn_gain_grad.reshape(groups, -1),
            router_wgrad.reshape(groups, -1),
        ],
        1,
    )
    small_grad = jnp.sum(
        lax.all_to_all(small_grad, "dp", split_axis=0, concat_axis=0, tiled=True), 0
    )
    at = 2 * gain_shard
    by_rows = small_grad[at:]
    by_rows = by_rows + to_peer(by_rows)

    place_back = (places[:, None] == leaving[None, :]).astype(BF16)

    def send_back(values):
        back = values.reshape(groups, half_peer, model_width)
        back = lax.all_to_all(back, "dp", split_axis=0, concat_axis=0, tiled=True)
        back = back.reshape(half_rows, model_width)
        return mm(place_back, jnp.concatenate([back, to_peer(back)], 0)).astype(BF16)

    return (
        send_back(out_rows),
        send_back(rows_grad.astype(BF16)),
        by_rows[:shard],
        qkv_wgrad[:, :heads_width],
        qkv_wgrad[:, heads_width : 2 * heads_width],
        qkv_wgrad[:, 2 * heads_width :],
        output_wgrad.T,
        small_grad[:gain_shard][None],
        small_grad[gain_shard:at][None],
        by_rows[shard : 2 * shard],
        by_rows[2 * shard :].reshape(router_weight.shape),
        gate_weight_grad,
        up_weight_grad,
        down_weight_grad,
    )


def solution(mesh):
    rows = P("dp", None)
    columns = P("tensor", "dp")
    inputs = (rows, rows, P(), rows, rows, P("dp"))
    inputs += (P("dp", "tensor"),) * 3 + (columns,) * 3 + (P("dp"), rows)
    inputs += (P(None, "dp", "tensor"),) * 2 + (P(None, "tensor", "dp"),)
    outputs = (rows, rows, P("dp")) + (P("dp", "tensor"),) * 3 + (columns,) * 3
    outputs += (P("dp"), rows) + (P(None, "dp", "tensor"),) * 2 + (P(None, "tensor", "dp"),)
    return jax.shard_map(body, mesh=mesh, in_specs=inputs, out_specs=outputs, check_vma=False)
```

```python
import jax
import jax.numpy as jnp
from jax import lax
from jax.experimental import pallas as pl
from jax.experimental.pallas import tpu as pltpu
from jax.sharding import PartitionSpec as P

HEAD_DIM = 128
EXPERTS = 16
EPS = 1e-05
ROPE_BASE = 10000.0
MASKED = -1e30
F32 = jnp.float32
BF16 = jnp.bfloat16


def row_scale(values):
    return lax.rsqrt(jnp.mean(values * values, -1, keepdims=True) + EPS)


def mm(left, right):
    return lax.dot_general(left, right, (((1,), (0,)), ((), ())), preferred_element_type=F32)


def inner_rows(left, right):
    return lax.dot_general(left, right, (((0,), (0,)), ((), ())), preferred_element_type=F32)


def outer_cols(left, right):
    return lax.dot_general(left, right, (((1,), (1,)), ((), ())), preferred_element_type=F32)


def rope_tables(positions, head_size):
    half_size = head_size // 2
    freq_table = ROPE_BASE ** (-2.0 * jnp.arange(half_size, dtype=F32) / head_size)
    angles = positions[:, None] * freq_table[None, :]
    angles = jnp.concatenate([angles, angles], -1)
    return (jnp.cos(angles), jnp.sin(angles))


def rotate_heads(values, cosine_table, sine_table):
    half_size = values.shape[-1] // 2
    turned = jnp.concatenate([-values[..., half_size:], values[..., :half_size]], -1)
    return values * cosine_table[:, None, :] + turned * sine_table[:, None, :]


def unrotate_heads(grads, cosine_table, sine_table):
    half_size = grads.shape[-1] // 2
    scaled = grads * sine_table[:, None, :]
    turned = jnp.concatenate([scaled[..., half_size:], -scaled[..., :half_size]], -1)
    return grads * cosine_table[:, None, :] + turned


class Wire:
    def __init__(self, depth):
        self.depth = depth
        self.sent = []

    def __call__(self, values, axis, pairs):
        if len(self.sent) >= self.depth:
            values, _ = lax.optimization_barrier((values, self.sent[-self.depth]))
        self.sent.append(lax.ppermute(values, axis, pairs))
        return self.sent[-1]


def weave(*transfers):
    results = [None] * len(transfers)
    going = list(enumerate(transfers))
    while going:
        still = []
        for number, transfer in going:
            try:
                next(transfer)
                still.append((number, transfer))
            except StopIteration as ended:
                results[number] = ended.value
        going = still
    return results


def ring_chip(place, chips):
    return 2 * place if place < chips // 2 else 2 * (chips - 1 - place) + 1


def core_index():
    return lax.axis_index("dp") % 2


def flow_pairs(chips):
    pairs = []
    for first in range(0, lax.axis_size("dp"), 2 * chips):
        for place in range(chips):
            here = ring_chip(place, chips)
            for core, step in ((0, 1), (1, -1)):
                there = ring_chip((place + step) % chips, chips)
                pairs.append((first + 2 * here + core, first + 2 * there + core))
    return pairs


def ring_order(chips):
    chip = (lax.axis_index("dp") // 2) % chips
    place = jnp.where(chip % 2 == 0, chip // 2, chips - 1 - chip // 2)
    toward = jnp.where(core_index() == 0, -1, 1)
    offsets = [0]
    for step in range(1, chips // 2):
        offsets += [toward * step, -toward * step]
    offsets.append(chips // 2)
    places = [lax.rem(place + offset + chips, chips) for offset in offsets]
    return jnp.stack(
        [jnp.where(at < chips // 2, 2 * at, 2 * (chips - 1 - at) + 1) for at in places]
    )


def ring_order_back(chips):
    order = ring_order(chips)
    numbers = jnp.arange(chips, dtype=order.dtype)
    return jnp.sum(jnp.where(order[None, :] == numbers[:, None], numbers[None, :], 0), 1)


def to_sibling(values):
    pairs = [(index, index ^ 1) for index in range(lax.axis_size("dp"))]
    return lax.ppermute(values, "dp", pairs)


def to_peer(wire, values):
    return wire(values, "tensor", [(0, 1), (1, 0)])


def by_core(mine, sibling, axis=0):
    return jnp.where(
        core_index() == 0,
        jnp.concatenate([mine, sibling], axis),
        jnp.concatenate([sibling, mine], axis),
    )


def core_part(values, core):
    size = values.shape[0] // 2
    return lax.dynamic_slice_in_dim(values, core * size, size, 0)


def ring_gather(wire, block, chips):
    core, pairs = core_index(), flow_pairs(chips)
    flow = by_core(block, to_sibling(block))
    gathered = [flow]
    for _ in range(1, chips // 2):
        flow = wire(flow, "dp", pairs)
        gathered += [flow, to_sibling(flow)]
        yield
    flow = wire(core_part(flow, core), "dp", pairs)
    yield
    gathered.append(by_core(flow, to_sibling(flow)))
    return gathered


def ring_scatter(wire, parts, chips, kind):
    core, pairs = core_index(), flow_pairs(chips)
    theirs = to_sibling(core_part(parts[-1], 1 - core).astype(kind)).astype(F32)
    flow = wire((core_part(parts[-1], core) + theirs).astype(kind), "dp", pairs)
    yield
    none = jnp.zeros_like(flow)
    flow = by_core(flow, none).astype(F32)
    for step in range(chips // 2 - 1, 0, -1):
        theirs = to_sibling(parts[2 * step - 1].astype(kind)).astype(F32)
        flow = wire((parts[2 * step] + theirs + flow).astype(kind), "dp", pairs).astype(F32)
        yield
    total = parts[0] + flow
    theirs = to_sibling(core_part(total, 1 - core).astype(kind)).astype(F32)
    return core_part(total, core) + theirs


def pieces_of(values, count, axis=0):
    size = values.shape[axis] // count
    return [lax.slice_in_dim(values, at * size, (at + 1) * size, axis=axis) for at in range(count)]


def columns_in(values, order, count):
    size = values.shape[1] // count
    blocks = [lax.dynamic_slice_in_dim(values, order[at] * size, size, 1) for at in range(count)]
    return jnp.concatenate(blocks, 1)


def pack_kernel(place_ref, gate_ref, up_ref, down_ref, own_ref, sibling_ref):
    width = gate_ref.shape[2]
    for out_ref, core in ((own_ref, place_ref[1]), (sibling_ref, 1 - place_ref[1])):
        out_ref[0, :, :width] = gate_ref[core].astype(BF16)
        out_ref[0, :, width : 2 * width] = up_ref[core].astype(BF16)
        out_ref[0, :, 2 * width :] = down_ref[core].T.astype(BF16)


def pack_experts(place, gate_weight, up_weight, down_weight):
    count, shard, width = gate_weight.shape
    side_in = pl.BlockSpec((2, shard, width), lambda k, p: (p[0] ^ k, 0, 0))
    down_in = pl.BlockSpec((2, width, shard), lambda k, p: (p[0] ^ k, 0, 0))
    out = pl.BlockSpec((1, shard, 3 * width), lambda k, p: (k, 0, 0))
    return pl.pallas_call(
        pack_kernel,
        grid_spec=pltpu.PrefetchScalarGridSpec(
            num_scalar_prefetch=1,
            grid=(count // 2,),
            in_specs=[side_in, side_in, down_in],
            out_specs=[out, out],
        ),
        out_shape=[jax.ShapeDtypeStruct((count // 2, shard, 3 * width), BF16)] * 2,
    )(place, gate_weight, up_weight, down_weight)


def unpack_kernel(place_ref, own_ref, sibling_ref, gate_ref, up_ref, down_ref):
    width = gate_ref.shape[2]
    for chunk, core in ((own_ref[0, 0], place_ref[1]), (sibling_ref[0], 1 - place_ref[1])):
        chunk = chunk.astype(F32)
        gate_ref[core] = chunk[:, :width]
        up_ref[core] = chunk[:, width : 2 * width]
        down_ref[core] = chunk[:, 2 * width :].T


def unpack_experts(place, own, sibling):
    chips, _, shard, width = own.shape
    width = width // 3
    side_out = pl.BlockSpec((2, shard, width), lambda k, p: (p[0] ^ k, 0, 0))
    down_out = pl.BlockSpec((2, width, shard), lambda k, p: (p[0] ^ k, 0, 0))
    sides = jax.ShapeDtypeStruct((2 * chips, shard, width), F32)
    return pl.pallas_call(
        unpack_kernel,
        grid_spec=pltpu.PrefetchScalarGridSpec(
            num_scalar_prefetch=1,
            grid=(chips,),
            in_specs=[
                pl.BlockSpec((1, 1, shard, 3 * width), lambda k, p: (k, p[1], 0, 0)),
                pl.BlockSpec((1, shard, 3 * width), lambda k, p: (k, 0, 0)),
            ],
            out_specs=[side_out, side_out, down_out],
        ),
        out_shape=[sides, sides, jax.ShapeDtypeStruct((2 * chips, width, shard), F32)],
    )(place, own, sibling)


def body(
    tokens,
    cotangent,
    dealing,
    lengths,
    routes,
    attention_gain,
    query_weight,
    key_weight,
    value_weight,
    output_weight,
    query_gain,
    key_gain,
    ffn_gain,
    router_weight,
    gate_weight,
    up_weight,
    down_weight,
):
    groups = lax.axis_size("dp")
    me = lax.axis_index("dp")
    side = lax.axis_index("tensor")
    rows_here, model_width = tokens.shape
    per_peer = rows_here // groups
    half_peer = per_peer // 2
    half_rows = rows_here // 2
    chips = groups // 2
    moe_chips = EXPERTS // 2
    replicas = groups // EXPERTS
    expert = lax.rem(me, EXPERTS)
    expert_chip, core = expert // 2, core_index()
    expert_place = jnp.stack([expert_chip, core]).astype(jnp.int32)
    long_wire, side_wire = Wire(3), Wire(2)

    dealt = dealing.reshape(groups, rows_here)
    places = jnp.arange(rows_here, dtype=jnp.int32)
    source_block = dealt // rows_here
    packed = (source_block * rows_here + places[None, :]) * rows_here + lax.rem(dealt, rows_here)
    packed = jnp.sort(packed, axis=1)
    leaving = lax.rem(
        lax.dynamic_slice_in_dim(packed, me * per_peer, per_peer, 1), rows_here
    ).reshape(groups, 2, half_peer)
    own_order = lax.rem(
        lax.dynamic_index_in_dim(packed, me, 0, keepdims=False) // rows_here, rows_here
    ).reshape(groups, 2, half_peer)

    def by_side(table):
        first, second = table[:, 0].reshape(-1), table[:, 1].reshape(-1)
        return jnp.concatenate(
            [jnp.where(side == 0, first, second), jnp.where(side == 0, second, first)]
        )

    leaving = by_side(leaving)
    own_order = by_side(own_order)
    pick = (leaving[:half_rows, None] == places[None, :]).astype(BF16)
    sent = jnp.concatenate(
        [
            mm(pick, tokens).astype(BF16).reshape(groups, half_peer, model_width),
            mm(pick, cotangent).astype(BF16).reshape(groups, half_peer, model_width),
        ],
        1,
    )
    got = lax.all_to_all(sent, "dp", split_axis=0, concat_axis=0, tiled=True)
    rows = got[:, :half_peer].reshape(half_rows, model_width).astype(F32)
    cot_rows = got[:, half_peer:].reshape(half_rows, model_width)

    small = jnp.concatenate(
        [
            attention_gain,
            ffn_gain,
            query_gain.reshape(-1),
            key_gain.reshape(-1),
            router_weight.reshape(-1),
        ]
    ).astype(BF16)
    small = jnp.broadcast_to(small[None], (groups, small.shape[0]))
    small = lax.all_to_all(small, "dp", split_axis=0, concat_axis=0, tiled=True)
    shard = attention_gain.shape[0]
    gain_shard = query_gain.shape[1]
    first_gain = small[:, :shard].reshape(-1).astype(F32)
    second_gain = small[:, shard : 2 * shard].reshape(-1).astype(F32)
    at = 2 * shard
    query_scale_gain = small[:, at : at + gain_shard].reshape(-1).astype(F32)
    key_scale_gain = small[:, at + gain_shard : at + 2 * gain_shard].reshape(-1).astype(F32)
    router_full = small[:, at + 2 * gain_shard :].reshape(model_width, EXPERTS)

    norm_one = row_scale(rows)
    normed_own = (rows * norm_one * first_gain).astype(BF16)
    normed_peer = to_peer(side_wire, normed_own)

    hidden_half = gate_weight.shape[2]
    packed_own, packed_sibling = pack_experts(expert_place, gate_weight, up_weight, down_weight)
    packed_experts = by_core(packed_own, to_sibling(packed_sibling), 1)
    across = [list(range(at, groups, EXPERTS)) for at in range(EXPERTS)]
    own_chunks = [packed_experts[0]] + [None] * (moe_chips - 1)
    peer_chunks = [None] * moe_chips

    def chip_pairs(step):
        return [(index, index ^ (2 * step)) for index in range(groups)]

    def fetch_experts(steps):
        for step in steps:
            if step > 0:
                own_chunks[step] = long_wire(packed_experts[step], "dp", chip_pairs(step))
            peer_chunks[step] = to_peer(side_wire, own_chunks[step])
            yield

    qkv_block = jnp.concatenate([query_weight, key_weight, value_weight], 1).astype(BF16)
    qkv_full, _ = weave(ring_gather(long_wire, qkv_block, chips), fetch_experts([0, 4, 1, 6, 2]))
    qkv_full = jnp.concatenate(qkv_full, 0)
    heads_width = query_weight.shape[1]
    order, order_back = ring_order(chips), ring_order_back(chips)

    finish_at = jnp.cumsum(lengths[0])
    start_at = finish_at - lengths[0]
    segment_ids = jnp.sum((own_order[:, None] >= finish_at[None, :]).astype(jnp.int32), -1)
    numbers = jnp.arange(lengths.shape[1], dtype=jnp.int32)
    begins = jnp.sum(jnp.where(segment_ids[:, None] == numbers[None, :], start_at[None, :], 0), -1)
    cosine_table, sine_table = rope_tables((own_order - begins).astype(F32), HEAD_DIM)
    allowed = (segment_ids[:, None] == segment_ids[None, :]) & (
        own_order[None, :] <= own_order[:, None]
    )
    head_scale = HEAD_DIM ** (-0.5)

    expert_ids = jnp.arange(EXPERTS, dtype=jnp.int32)
    uses = jnp.sum((routes[:, :, None] == expert_ids[None, None, :]).astype(F32), 1)
    reorder = (own_order[:half_rows, None] == places[None, :]).astype(BF16)
    used = mm(reorder, uses.astype(BF16))

    normed_one = columns_in(jnp.concatenate([normed_own, normed_peer], 0), order, chips)
    qkv = mm(normed_one, qkv_full)
    query_raw, key_raw = qkv[:, :heads_width], qkv[:, heads_width : 2 * heads_width]
    value_rows = qkv[:, 2 * heads_width :].astype(BF16)

    def over_sides(values):
        theirs = to_peer(side_wire, values)
        return values + jnp.concatenate([theirs[:, half_rows:], theirs[:, :half_rows]], 1)

    squares = over_sides(
        jnp.stack([jnp.sum(query_raw * query_raw, -1), jnp.sum(key_raw * key_raw, -1)])
    )
    output_block = output_weight.T.astype(BF16)
    output_full, _ = weave(ring_gather(long_wire, output_block, chips), fetch_experts([5]))
    output_full = jnp.concatenate(output_full, 0)
    query_scale = lax.rsqrt(squares[0] / model_width + EPS)[:, None]
    key_scale = lax.rsqrt(squares[1] / model_width + EPS)[:, None]
    heads_here = heads_width // HEAD_DIM
    query_normed = query_raw * query_scale * query_scale_gain
    key_normed = key_raw * key_scale * key_scale_gain
    query_heads = rotate_heads(
        query_normed.reshape(rows_here, heads_here, HEAD_DIM), cosine_table, sine_table
    ).astype(BF16)
    key_heads = rotate_heads(
        key_normed.reshape(rows_here, heads_here, HEAD_DIM), cosine_table, sine_table
    ).astype(BF16)
    value_heads = value_rows.reshape(rows_here, heads_here, HEAD_DIM)

    def attention_scores(query_part, key_part):
        raw_scores = (
            jnp.einsum("qhd,khd->hqk", query_part, key_part, preferred_element_type=F32)
            * head_scale
        )
        return jnp.where(allowed[None], raw_scores, MASKED)

    masked_scores = attention_scores(query_heads, key_heads)
    peak_value = jnp.max(masked_scores, -1, keepdims=True)
    powered = jnp.exp(masked_scores - peak_value)
    total_weight = jnp.sum(powered, -1, keepdims=True)
    probs = powered / total_weight
    log_total = peak_value + jnp.log(total_weight)
    context = jnp.einsum(
        "hqk,khd->qhd", probs.astype(BF16), value_heads, preferred_element_type=F32
    )
    context = context.reshape(rows_here, -1).astype(BF16)
    attention = outer_cols(context, output_full)
    attention = attention[:half_rows] + to_peer(
        side_wire, attention[half_rows:].astype(BF16)
    ).astype(F32)
    weave(fetch_experts([3, 7]))
    hidden = rows + columns_in(attention, order_back, chips)

    norm_two = row_scale(hidden)
    normed_two = (hidden * norm_two * second_gain).astype(BF16)
    logits = mm(normed_two, router_full)
    powered_two = jnp.exp(logits - jnp.max(logits, -1, keepdims=True))
    router_probs = powered_two / jnp.sum(powered_two, -1, keepdims=True)
    gate_table = (router_probs * used).T

    inputs_all, cot_all = (
        jnp.concatenate(weave(ring_gather(long_wire, block, moe_chips))[0], 0)
        for block in (normed_two, cot_rows)
    )
    moe_order, moe_order_back = ring_order(moe_chips), ring_order_back(moe_chips)

    def to_experts(table):
        kwargs = {}
        if replicas > 1:
            kwargs["axis_index_groups"] = [
                list(range(at, at + EXPERTS)) for at in range(0, groups, EXPERTS)
            ]
        return lax.all_to_all(table, "dp", split_axis=0, concat_axis=0, tiled=True, **kwargs)

    gates = to_experts(gate_table).reshape(moe_chips, -1)
    gates = jnp.take(gates, moe_order, axis=0).reshape(-1, 1)

    def placed(chunks):
        size, width = chunks[0].shape
        whole = jnp.zeros((moe_chips * size, width), chunks[0].dtype)
        for step, chunk in enumerate(chunks):
            at = (expert_chip ^ step) * size
            whole = lax.dynamic_update_slice_in_dim(whole, chunk, at, 0)
        return whole

    expert_own, expert_peer = placed(own_chunks), placed(peer_chunks)
    if replicas > 1:
        expert_own, expert_peer = (
            lax.all_gather(part, "dp", axis=0, tiled=True, axis_index_groups=across)
            for part in (expert_own, expert_peer)
        )
    out_cells = (cot_all.astype(F32) * gates).astype(BF16)
    halves = []
    for weights in (expert_own, expert_peer):
        front = mm(inputs_all, weights[:, : 2 * hidden_half])
        gate_pre, up_pre = front[:, :hidden_half], front[:, hidden_half:]
        sigmoid_gate = 1.0 / (1.0 + jnp.exp(-gate_pre))
        active = (gate_pre * sigmoid_gate * up_pre).astype(BF16)
        active_grad = mm(out_cells, weights[:, 2 * hidden_half :])
        gate_grad = (
            active_grad * up_pre * sigmoid_gate * (1.0 + gate_pre * (1.0 - sigmoid_gate))
        ).astype(BF16)
        up_grad = (active_grad * gate_pre * sigmoid_gate).astype(BF16)
        halves.append((active, jnp.concatenate([gate_grad, up_grad], 1), weights))
    input_grad = sum(outer_cols(grad, w[:, : 2 * hidden_half]) for _, grad, w in halves)
    produced = sum(outer_cols(active, w[:, 2 * hidden_half :]) for active, _, w in halves)
    mixing = jnp.sum(produced * cot_all.astype(F32), -1)
    expert_wgrads = [
        jnp.concatenate([inner_rows(inputs_all, grad), inner_rows(out_cells, active)], 1)
        for active, grad, _ in halves
    ]

    normed_two_grad = weave(
        ring_scatter(long_wire, pieces_of(input_grad, moe_chips), moe_chips, BF16)
    )[0]
    mixing_table = jnp.take(mixing.reshape(moe_chips, -1), moe_order_back, axis=0)
    mixing_table = to_experts(mixing_table.reshape(EXPERTS, -1))
    mixture = weave(
        ring_scatter(long_wire, pieces_of(produced * gates, moe_chips), moe_chips, BF16)
    )[0]
    out_rows = (hidden + mixture).astype(BF16)

    wgrad_own, wgrad_peer = expert_wgrads[0], expert_wgrads[1].astype(BF16)
    if replicas > 1:
        wgrad_own, wgrad_peer = (
            lax.psum_scatter(
                part.astype(BF16), "dp", scatter_dimension=0, tiled=True, axis_index_groups=across
            )
            for part in (wgrad_own, wgrad_peer)
        )
    chip_rows = wgrad_own.shape[0] // moe_chips

    def wgrad_chunk(values, step):
        return lax.dynamic_slice_in_dim(values, (expert_chip ^ step) * chip_rows, chip_rows, 0)

    summed_chunks, wgrad_chunks = [None] * moe_chips, [None] * moe_chips

    def sum_wgrads(steps):
        for step in steps:
            theirs = to_peer(side_wire, wgrad_chunk(wgrad_peer, step)).astype(F32)
            chunk = wgrad_chunk(wgrad_own, step).astype(F32) + theirs
            summed_chunks[step] = chunk.astype(BF16)

    def return_wgrads(steps):
        for step in steps:
            wgrad_chunks[step] = long_wire(summed_chunks[step], "dp", chip_pairs(step))
            yield

    sum_wgrads([4, 1, 6, 2, 5])

    prob_grad = mixing_table.T * used
    logit_grad = (
        router_probs * (prob_grad - jnp.sum(router_probs * prob_grad, -1, keepdims=True))
    ).astype(BF16)
    router_wgrad = inner_rows(normed_two, logit_grad)
    normed_two_grad = normed_two_grad + outer_cols(logit_grad, router_full)
    ffn_gain_grad = jnp.sum(normed_two_grad * hidden * norm_two, 0)
    scaled_two = normed_two_grad * second_gain
    hidden_grad = cot_rows.astype(F32) + norm_two * (
        scaled_two - hidden * norm_two * norm_two * jnp.mean(scaled_two * hidden, -1, keepdims=True)
    )

    attn_own = hidden_grad.astype(BF16)
    attn_peer = to_peer(side_wire, attn_own)
    sum_wgrads([3, 7, 0])
    attn_grad = columns_in(jnp.concatenate([attn_own, attn_peer], 0), order, chips)
    output_wgrad = pieces_of(inner_rows(attn_grad, context), chips)
    output_wgrad, _ = weave(
        ring_scatter(long_wire, output_wgrad, chips, BF16), return_wgrads([4, 1, 6, 2])
    )
    context_grad = mm(attn_grad, output_full).astype(BF16)
    context_grad = context_grad.reshape(rows_here, heads_here, HEAD_DIM)
    recomputed = jnp.exp(attention_scores(query_heads, key_heads) - log_total)
    prob_pair_grad = jnp.einsum(
        "qhd,khd->hqk", context_grad, value_heads, preferred_element_type=F32
    )
    value_grad = jnp.einsum(
        "hqk,qhd->khd", recomputed.astype(BF16), context_grad, preferred_element_type=F32
    )
    value_grad = value_grad.reshape(rows_here, -1).astype(BF16)
    score_grad = (
        recomputed * (prob_pair_grad - jnp.sum(recomputed * prob_pair_grad, -1, keepdims=True))
    ).astype(BF16)
    query_rot_grad = (
        jnp.einsum("hqk,khd->qhd", score_grad, key_heads, preferred_element_type=F32) * head_scale
    )
    key_rot_grad = (
        jnp.einsum("hqk,qhd->khd", score_grad, query_heads, preferred_element_type=F32)
        * head_scale
    )
    query_norm_grad = unrotate_heads(query_rot_grad, cosine_table, sine_table).reshape(
        rows_here, -1
    )
    key_norm_grad = unrotate_heads(key_rot_grad, cosine_table, sine_table).reshape(rows_here, -1)
    inners = over_sides(
        jnp.stack(
            [
                jnp.sum(query_norm_grad * query_scale_gain * query_raw, -1),
                jnp.sum(key_norm_grad * key_scale_gain * key_raw, -1),
            ]
        )
    )
    query_gain_grad = jnp.sum(query_norm_grad * query_raw * query_scale, 0)
    key_gain_grad = jnp.sum(key_norm_grad * key_raw * key_scale, 0)
    query_raw_grad = (
        query_scale * query_scale_gain * query_norm_grad
        - query_raw * query_scale**3 * inners[0][:, None] / model_width
    ).astype(BF16)
    key_raw_grad = (
        key_scale * key_scale_gain * key_norm_grad
        - key_raw * key_scale**3 * inners[1][:, None] / model_width
    ).astype(BF16)
    qkv_grad = jnp.concatenate([query_raw_grad, key_raw_grad, value_grad], 1)
    qkv_wgrad = pieces_of(inner_rows(normed_one, qkv_grad), chips)
    qkv_wgrad, _ = weave(
        ring_scatter(long_wire, qkv_wgrad, chips, BF16), return_wgrads([5, 3, 7])
    )
    wgrad_chunks[0] = summed_chunks[0]
    returned = jnp.stack(wgrad_chunks).reshape(moe_chips, 2, -1, 3 * hidden_half)
    of_sibling = to_sibling(lax.dynamic_index_in_dim(returned, 1 - core, 1, keepdims=False))
    gate_weight_grad, up_weight_grad, down_weight_grad = unpack_experts(
        expert_place, returned, of_sibling
    )
    normed_one_grad = outer_cols(qkv_grad, qkv_full)
    normed_one_grad = normed_one_grad[:half_rows] + to_peer(
        side_wire, normed_one_grad[half_rows:].astype(BF16)
    ).astype(F32)
    normed_one_grad = columns_in(normed_one_grad, order_back, chips)
    attention_gain_grad = jnp.sum(normed_one_grad * rows * norm_one, 0)
    scaled_one = normed_one_grad * first_gain
    rows_grad = hidden_grad + norm_one * (
        scaled_one - rows * norm_one * norm_one * jnp.mean(scaled_one * rows, -1, keepdims=True)
    )

    small_grad = jnp.concatenate(
        [
            query_gain_grad.reshape(groups, -1),
            key_gain_grad.reshape(groups, -1),
            attention_gain_grad.reshape(groups, -1),
            ffn_gain_grad.reshape(groups, -1),
            router_wgrad.reshape(groups, -1),
        ],
        1,
    )
    small_grad = jnp.sum(
        lax.all_to_all(small_grad, "dp", split_axis=0, concat_axis=0, tiled=True), 0
    )
    at = 2 * gain_shard
    by_rows = small_grad[at:]
    by_rows = by_rows + to_peer(side_wire, by_rows)

    place_back = (places[:, None] == leaving[None, :]).astype(BF16)

    def send_back(values):
        back = values.reshape(groups, half_peer, model_width)
        back = lax.all_to_all(back, "dp", split_axis=0, concat_axis=0, tiled=True)
        back = back.reshape(half_rows, model_width)
        return mm(place_back, jnp.concatenate([back, to_peer(side_wire, back)], 0)).astype(BF16)

    return (
        send_back(out_rows),
        send_back(rows_grad.astype(BF16)),
        by_rows[:shard],
        qkv_wgrad[:, :heads_width],
        qkv_wgrad[:, heads_width : 2 * heads_width],
        qkv_wgrad[:, 2 * heads_width :],
        output_wgrad.T,
        small_grad[:gain_shard][None],
        small_grad[gain_shard:at][None],
        by_rows[shard : 2 * shard],
        by_rows[2 * shard :].reshape(router_weight.shape),
        gate_weight_grad,
        up_weight_grad,
        down_weight_grad,
    )


def solution(mesh):
    rows = P("dp", None)
    columns = P("tensor", "dp")
    inputs = (rows, rows, P(), rows, rows, P("dp"))
    inputs += (P("dp", "tensor"),) * 3 + (columns,) * 3 + (P("dp"), rows)
    inputs += (P(None, "dp", "tensor"),) * 2 + (P(None, "tensor", "dp"),)
    outputs = (rows, rows, P("dp")) + (P("dp", "tensor"),) * 3 + (columns,) * 3
    outputs += (P("dp"), rows) + (P(None, "dp", "tensor"),) * 2 + (P(None, "tensor", "dp"),)
    return jax.shard_map(body, mesh=mesh, in_specs=inputs, out_specs=outputs, check_vma=False)
```

```python
import jax
import jax.numpy as jnp
from jax import lax
from jax.experimental import pallas as pl
from jax.experimental.pallas import tpu as pltpu
from jax.sharding import PartitionSpec as P

HEAD_DIM = 128
EXPERTS = 16
EPS = 1e-05
ROPE_BASE = 10000.0
MASKED = -1e30
F32 = jnp.float32
BF16 = jnp.bfloat16


def row_scale(values):
    return lax.rsqrt(jnp.mean(values * values, -1, keepdims=True) + EPS)


def mm(left, right):
    return lax.dot_general(left, right, (((1,), (0,)), ((), ())), preferred_element_type=F32)


def inner_rows(left, right):
    return lax.dot_general(left, right, (((0,), (0,)), ((), ())), preferred_element_type=F32)


def outer_cols(left, right):
    return lax.dot_general(left, right, (((1,), (1,)), ((), ())), preferred_element_type=F32)


def rope_tables(positions, head_size):
    half_size = head_size // 2
    freq_table = ROPE_BASE ** (-2.0 * jnp.arange(half_size, dtype=F32) / head_size)
    angles = positions[:, None] * freq_table[None, :]
    cosines, sines = jnp.cos(angles), jnp.sin(angles)
    return jnp.stack(
        [jnp.concatenate([cosines, cosines], -1), jnp.concatenate([-sines, sines], -1)]
    )


def after(value, *others):
    return lax.optimization_barrier((value, others))[0]


def ring_chip(place, chips):
    return 2 * place if place < chips // 2 else 2 * (chips - 1 - place) + 1


def core_index():
    return lax.axis_index("dp") % 2


def flow_pairs(chips):
    pairs = []
    for first in range(0, lax.axis_size("dp"), 2 * chips):
        for place in range(chips):
            here = ring_chip(place, chips)
            for core, step in ((0, 1), (1, -1)):
                there = ring_chip((place + step) % chips, chips)
                pairs.append((first + 2 * here + core, first + 2 * there + core))
    return pairs


def ring_order(chips):
    chip = (lax.axis_index("dp") // 2) % chips
    place = jnp.where(chip % 2 == 0, chip // 2, chips - 1 - chip // 2)
    toward = jnp.where(core_index() == 0, -1, 1)
    offsets = [0]
    for step in range(1, chips // 2):
        offsets += [toward * step, -toward * step]
    offsets.append(chips // 2)
    places = [lax.rem(place + offset + chips, chips) for offset in offsets]
    return jnp.stack(
        [jnp.where(at < chips // 2, 2 * at, 2 * (chips - 1 - at) + 1) for at in places]
    )


def to_sibling(values):
    pairs = [(index, index ^ 1) for index in range(lax.axis_size("dp"))]
    return lax.ppermute(values, "dp", pairs)


def to_peer(values):
    return lax.ppermute(values, "tensor", [(0, 1), (1, 0)])


def by_core(mine, sibling, axis=0):
    return jnp.where(
        core_index() == 0,
        jnp.concatenate([mine, sibling], axis),
        jnp.concatenate([sibling, mine], axis),
    )


def core_part(values, core):
    size = values.shape[0] // 2
    return lax.dynamic_slice_in_dim(values, core * size, size, 0)


def ring_scatter(parts, chips, kind, waits=()):
    core, pairs = core_index(), flow_pairs(chips)
    parts = [part.astype(F32) for part in parts]
    theirs = to_sibling(core_part(parts[-1], 1 - core).astype(kind)).astype(F32)
    flow = lax.ppermute((core_part(parts[-1], core) + theirs).astype(kind), "dp", pairs)
    none = jnp.zeros_like(flow)
    flow = by_core(flow, none).astype(F32)
    for step in range(chips // 2 - 1, 0, -1):
        theirs = to_sibling(parts[2 * step - 1].astype(kind)).astype(F32)
        flow = after((parts[2 * step] + theirs + flow).astype(kind), *waits[-step:][:1])
        flow = lax.ppermute(flow, "dp", pairs).astype(F32)
    total = parts[0] + flow
    theirs = to_sibling(core_part(total, 1 - core).astype(kind)).astype(F32)
    return core_part(total, core) + theirs


def pieces_of(values, count, axis=0):
    size = values.shape[axis] // count
    return [lax.slice_in_dim(values, at * size, (at + 1) * size, axis=axis) for at in range(count)]


def columns_in(values, order, count):
    size = values.shape[1] // count
    blocks = [lax.dynamic_slice_in_dim(values, order[at] * size, size, 1) for at in range(count)]
    return jnp.concatenate(blocks, 1)


def pack_kernel(place_ref, gate_ref, up_ref, down_ref, own_ref, sibling_ref):
    width = gate_ref.shape[2]
    for out_ref, core in ((own_ref, place_ref[1]), (sibling_ref, 1 - place_ref[1])):
        out_ref[0, :, :width] = gate_ref[core].astype(BF16)
        out_ref[0, :, width : 2 * width] = up_ref[core].astype(BF16)
        out_ref[0, :, 2 * width :] = down_ref[core].T.astype(BF16)


def pack_experts(place, gate_weight, up_weight, down_weight):
    count, shard, width = gate_weight.shape
    side_in = pl.BlockSpec((2, shard, width), lambda k, p: (p[0] ^ k, 0, 0))
    down_in = pl.BlockSpec((2, width, shard), lambda k, p: (p[0] ^ k, 0, 0))
    out = pl.BlockSpec((1, shard, 3 * width), lambda k, p: (k, 0, 0))
    return pl.pallas_call(
        pack_kernel,
        grid_spec=pltpu.PrefetchScalarGridSpec(
            num_scalar_prefetch=1,
            grid=(count // 2,),
            in_specs=[side_in, side_in, down_in],
            out_specs=[out, out],
        ),
        out_shape=[jax.ShapeDtypeStruct((count // 2, shard, 3 * width), BF16)] * 2,
    )(place, gate_weight, up_weight, down_weight)


def merge_kernel(place_ref, own_ref, sibling_ref, out_ref):
    size = own_ref.shape[1]
    for part_ref, core in ((own_ref, place_ref[1]), (sibling_ref, 1 - place_ref[1])):
        out_ref[0, pl.ds(pl.multiple_of(core * size, size), size)] = part_ref[0]


def merge_cores(place, own, sibling):
    chips, size, width = own.shape
    part = pl.BlockSpec((1, size, width), lambda k, p: (k, 0, 0))
    return pl.pallas_call(
        merge_kernel,
        grid_spec=pltpu.PrefetchScalarGridSpec(
            num_scalar_prefetch=1,
            grid=(chips,),
            in_specs=[part, part],
            out_specs=pl.BlockSpec((1, 2 * size, width), lambda k, p: (k, 0, 0)),
        ),
        out_shape=jax.ShapeDtypeStruct((chips, 2 * size, width), own.dtype),
    )(place, own, sibling)


def unpack_kernel(place_ref, own_ref, sibling_ref, gate_ref, up_ref, down_ref):
    width = gate_ref.shape[2]
    own_core = place_ref[pl.num_programs(0)]
    for chunk, core in ((own_ref[0, 0], own_core), (sibling_ref[0], 1 - own_core)):
        chunk = chunk.astype(F32)
        gate_ref[core] = chunk[:, :width]
        up_ref[core] = chunk[:, width : 2 * width]
        down_ref[core] = chunk[:, 2 * width :].T


def unpack_experts(place, own, sibling):
    chips, _, shard, width = own.shape
    width = width // 3
    side_out = pl.BlockSpec((2, shard, width), lambda k, p: (p[k], 0, 0))
    down_out = pl.BlockSpec((2, width, shard), lambda k, p: (p[k], 0, 0))
    sides = jax.ShapeDtypeStruct((2 * chips, shard, width), F32)
    return pl.pallas_call(
        unpack_kernel,
        grid_spec=pltpu.PrefetchScalarGridSpec(
            num_scalar_prefetch=1,
            grid=(chips,),
            in_specs=[
                pl.BlockSpec((1, 1, shard, 3 * width), lambda k, p: (k, p[chips], 0, 0)),
                pl.BlockSpec((1, shard, 3 * width), lambda k, p: (k, 0, 0)),
            ],
            out_specs=[side_out, side_out, down_out],
        ),
        out_shape=[sides, sides, jax.ShapeDtypeStruct((2 * chips, width, shard), F32)],
    )(place, own, sibling)


ROW_VMEM = 48 * 1024 * 1024
LIGHT = pl.CostEstimate(flops=1024, bytes_accessed=1024, transcendentals=0)


def mix_grads(front, active_grad, width):
    gate_pre, up_pre = front[:, :width], front[:, width:]
    sigmoid_gate = 1.0 / (1.0 + jnp.exp(-gate_pre))
    active = (gate_pre * sigmoid_gate * up_pre).astype(BF16)
    gate_grad = active_grad * up_pre * sigmoid_gate * (1.0 + gate_pre * (1.0 - sigmoid_gate))
    up_grad = active_grad * gate_pre * sigmoid_gate
    return active, jnp.concatenate([gate_grad.astype(BF16), up_grad.astype(BF16)], 1)


def rows_kernel(
    expert_ref, rows_ref, cot_ref, use_ref, router_ref, own_ref, peer_ref, *out_refs
):
    grad_ref, active_ref, front_grad_ref, cells_ref, gate_ref = out_refs
    width = own_ref.shape[1] // 3
    logits = mm(rows_ref[...], router_ref[...])
    powered = jnp.exp(logits - jnp.max(logits, -1, keepdims=True))
    router_probs = powered / jnp.sum(powered, -1, keepdims=True)
    numbers = lax.broadcasted_iota(jnp.int32, router_probs.shape, 1)
    gate = jnp.sum(jnp.where(numbers == expert_ref[0], router_probs, 0.0), -1, keepdims=True)
    gate = gate * use_ref[...]
    gate_ref[...] = gate
    cells = (cot_ref[...].astype(F32) * gate).astype(BF16)
    cells_ref[...] = cells
    total = None
    for half, weights_ref in enumerate((own_ref, peer_ref)):
        front = mm(rows_ref[...], weights_ref[:, : 2 * width])
        active_grad = mm(cells, weights_ref[:, 2 * width :])
        active, front_grad = mix_grads(front, active_grad, width)
        active_ref[:, half * width : (half + 1) * width] = active
        front_grad_ref[:, 2 * half * width : 2 * (half + 1) * width] = front_grad
        part = outer_cols(front_grad, weights_ref[:, : 2 * width])
        total = part if total is None else total + part
    grad_ref[...] = total.astype(BF16)


def expert_rows(expert, rows, cot_rows, uses, router, own, peer, tile):
    count, model_width = rows.shape
    width = own.shape[1] // 3
    part = lambda columns: pl.BlockSpec((tile, columns), lambda i, e: (i, 0))
    whole = lambda values: pl.BlockSpec(
        values.shape, lambda i, e: (0, 0), pipeline_mode=pl.Buffered(1)
    )
    outs = (model_width, 2 * width, 4 * width, model_width)
    return pl.pallas_call(
        rows_kernel,
        grid_spec=pltpu.PrefetchScalarGridSpec(
            num_scalar_prefetch=1,
            grid=(count // tile,),
            in_specs=[part(model_width), part(model_width), part(1)]
            + [whole(values) for values in (router, own, peer)],
            out_specs=[part(columns) for columns in outs + (1,)],
        ),
        out_shape=[jax.ShapeDtypeStruct((count, columns), BF16) for columns in outs]
        + [jax.ShapeDtypeStruct((count, 1), F32)],
        compiler_params=pltpu.CompilerParams(vmem_limit_bytes=ROW_VMEM),
        cost_estimate=LIGHT,
    )(expert, rows, cot_rows, uses, router, own, peer)


def mixture_kernel(active_ref, cot_ref, gate_ref, own_ref, peer_ref, mixed_ref, mixing_ref):
    width = own_ref.shape[1]
    produced = outer_cols(active_ref[:, :width], own_ref[...])
    produced = produced + outer_cols(active_ref[:, width:], peer_ref[...])
    mixing_ref[...] = jnp.sum(produced * cot_ref[...].astype(F32), -1, keepdims=True)
    mixed_ref[...] = (produced * gate_ref[...]).astype(BF16)


def expert_mixture(active, cot_rows, gates, own, peer, tile):
    count, model_width = cot_rows.shape
    width = own.shape[1] // 3
    wide = pl.BlockSpec((tile, model_width), lambda i: (i, 0))
    single = pl.BlockSpec((tile, 1), lambda i: (i, 0))
    down = pl.BlockSpec((model_width, width), lambda i: (0, 2), pipeline_mode=pl.Buffered(1))
    return pl.pallas_call(
        mixture_kernel,
        grid=(count // tile,),
        in_specs=[pl.BlockSpec((tile, 2 * width), lambda i: (i, 0)), wide, single, down, down],
        out_specs=[wide, single],
        out_shape=[
            jax.ShapeDtypeStruct((count, model_width), BF16),
            jax.ShapeDtypeStruct((count, 1), F32),
        ],
        compiler_params=pltpu.CompilerParams(vmem_limit_bytes=ROW_VMEM),
        cost_estimate=LIGHT,
    )(active, cot_rows, gates, own, peer)


def wgrad_kernel(
    order_ref, rows_ref, cells_ref, front_grad_ref, active_ref, first_ref, last_ref, own_ref
):
    number, early = pl.program_id(0), 3 * pl.num_programs(0) // 4
    width = active_ref.shape[1] // 2
    front = mm(rows_ref[...].T, front_grad_ref[...]).astype(BF16)
    down = mm(cells_ref[...].T, active_ref[...]).astype(BF16)
    own_ref[0, :, : 2 * width] = front[:, : 2 * width]
    own_ref[0, :, 2 * width :] = down[:, :width]
    for wanted, out_ref in ((number < early, first_ref), (number >= early, last_ref)):

        @pl.when(wanted)
        def _():
            out_ref[0, :, : 2 * width] = front[:, 2 * width :]
            out_ref[0, :, 2 * width :] = down[:, width:]


def expert_wgrads(order, rows, cells, front_grad, active):
    count, model_width = rows.shape
    blocks = order.shape[0]
    early = 3 * blocks // 4
    size, width = model_width // blocks, active.shape[1] // 2
    columns = pl.BlockSpec((count, size), lambda i, o: (0, o[i]))
    whole = lambda values: pl.BlockSpec(
        values.shape, lambda i, o: (0, 0), pipeline_mode=pl.Buffered(1)
    )
    part = (1, size, 3 * width)
    return pl.pallas_call(
        wgrad_kernel,
        grid_spec=pltpu.PrefetchScalarGridSpec(
            num_scalar_prefetch=1,
            grid=(blocks,),
            in_specs=[columns, columns, whole(front_grad), whole(active)],
            out_specs=[
                pl.BlockSpec(part, lambda i, o: (jnp.minimum(i, early - 1), 0, 0)),
                pl.BlockSpec(part, lambda i, o: (jnp.maximum(i - early, 0), 0, 0)),
                pl.BlockSpec(part, lambda i, o: (i, 0, 0)),
            ],
        ),
        out_shape=[
            jax.ShapeDtypeStruct((many, size, 3 * width), BF16) for many in (early, blocks - early, blocks)
        ],
        compiler_params=pltpu.CompilerParams(vmem_limit_bytes=ROW_VMEM),
        cost_estimate=LIGHT,
    )(order, rows, cells, front_grad, active)


def attention_kernel(
    query_ref, key_ref, value_ref, scale_ref, gain_ref, turn_ref, mask_ref, *out_refs
):
    rotated_query_ref, rotated_key_ref, context_ref, log_ref = out_refs
    cosine, sine = turn_ref[0], turn_ref[1]
    rotated = []
    for number, (raw_ref, out_ref) in enumerate(
        ((query_ref, rotated_query_ref), (key_ref, rotated_key_ref))
    ):
        normed = raw_ref[...] * scale_ref[number] * gain_ref[number : number + 1]
        turned = normed * cosine + pltpu.roll(normed, HEAD_DIM // 2, 1) * sine
        rotated.append(turned.astype(BF16))
        out_ref[...] = rotated[number]
    scores = outer_cols(rotated[0], rotated[1]) * HEAD_DIM ** (-0.5)
    scores = jnp.where(mask_ref[...] > 0, scores, MASKED)
    peak_value = jnp.max(scores, -1, keepdims=True)
    powered = jnp.exp(scores - peak_value)
    total_weight = jnp.sum(powered, -1, keepdims=True)
    probs = (powered / total_weight).astype(BF16)
    log_ref[0] = peak_value + jnp.log(total_weight)
    context_ref[...] = mm(probs, value_ref[...].astype(BF16)).astype(BF16)


def attention_grad_kernel(
    query_ref,
    key_ref,
    value_ref,
    scale_ref,
    gain_ref,
    turn_ref,
    mask_ref,
    rotated_query_ref,
    rotated_key_ref,
    log_ref,
    context_grad_ref,
    query_grad_ref,
    key_grad_ref,
    value_grad_ref,
    gain_grad_ref,
    inner_ref,
):
    head_scale = HEAD_DIM ** (-0.5)
    cosine, sine = turn_ref[0], turn_ref[1]
    query, key = rotated_query_ref[...], rotated_key_ref[...]
    scores = outer_cols(query, key) * head_scale
    scores = jnp.where(mask_ref[...] > 0, scores, MASKED)
    probs = jnp.exp(scores - log_ref[0])
    context_grad = context_grad_ref[...]
    probs_grad = outer_cols(context_grad, value_ref[...].astype(BF16))
    value_grad_ref[...] = mm(probs.astype(BF16).T, context_grad).astype(BF16)
    scores_grad = probs * (probs_grad - jnp.sum(probs * probs_grad, -1, keepdims=True))
    scores_grad = scores_grad.astype(BF16)

    @pl.when(pl.program_id(0) == 0)
    def _():
        inner_ref[...] = jnp.zeros_like(inner_ref)

    for number, (raw_ref, grad, out_ref) in enumerate(
        (
            (query_ref, mm(scores_grad, key), query_grad_ref),
            (key_ref, mm(scores_grad.T, query), key_grad_ref),
        )
    ):
        grad = grad * head_scale
        grad = grad * cosine - pltpu.roll(grad, HEAD_DIM // 2, 1) * sine
        out_ref[...] = grad
        raw = raw_ref[...]
        gain_grad_ref[number : number + 1] = jnp.sum(
            grad * raw * scale_ref[number], 0, keepdims=True
        )
        inner_ref[number] += jnp.sum(
            grad * gain_ref[number : number + 1] * raw, -1, keepdims=True
        )


def by_heads(kernel, rows, heads, inputs, extra, outs, log_out):
    column = pl.BlockSpec((rows, HEAD_DIM), lambda h: (0, h))
    at = lambda part: pl.BlockSpec((rows, HEAD_DIM), lambda h: (0, part * heads + h))
    logs = pl.BlockSpec((1, rows, 1), lambda h: (h, 0, 0))
    pair = pl.BlockSpec((2, HEAD_DIM), lambda h: (0, h))
    whole = lambda *shape: pl.BlockSpec(shape, lambda h: (0,) * len(shape))
    in_specs = [at(0), at(1), at(2), whole(2, rows, 1), pair]
    in_specs += [whole(2, rows, HEAD_DIM), whole(rows, rows)]
    in_specs += [logs if values.ndim == 3 else column for values in extra]
    out_shape = [jax.ShapeDtypeStruct((rows, heads * HEAD_DIM), kind) for kind in outs]
    out_specs = [column] * len(outs)
    if log_out:
        out_shape += [jax.ShapeDtypeStruct((heads, rows, 1), F32)]
        out_specs += [logs]
    else:
        out_shape += [
            jax.ShapeDtypeStruct((2, heads * HEAD_DIM), F32),
            jax.ShapeDtypeStruct((2, rows, 1), F32),
        ]
        out_specs += [pair, whole(2, rows, 1)]
    return pl.pallas_call(
        kernel,
        grid=(heads,),
        in_specs=in_specs,
        out_specs=out_specs,
        out_shape=out_shape,
        cost_estimate=LIGHT,
    )(*inputs, *extra)


def body(
    tokens,
    cotangent,
    dealing,
    lengths,
    routes,
    attention_gain,
    query_weight,
    key_weight,
    value_weight,
    output_weight,
    query_gain,
    key_gain,
    ffn_gain,
    router_weight,
    gate_weight,
    up_weight,
    down_weight,
):
    groups = lax.axis_size("dp")
    me = lax.axis_index("dp")
    side = lax.axis_index("tensor")
    rows_here, model_width = tokens.shape
    per_peer = rows_here // groups
    half_peer = per_peer // 2
    half_rows = rows_here // 2
    chips = groups // 2
    moe_chips = EXPERTS // 2
    replicas = groups // EXPERTS
    expert = lax.rem(me, EXPERTS)
    expert_chip, core = expert // 2, core_index()
    expert_place = jnp.stack([expert_chip, core]).astype(jnp.int32)

    dealt = dealing.reshape(groups, rows_here)
    places = jnp.arange(rows_here, dtype=jnp.int32)
    source_block = dealt // rows_here
    own_sources = lax.dynamic_slice_in_dim(source_block, me, 1, 0)
    numbers = jnp.arange(groups, dtype=jnp.int32)[:, None]
    chosen = jnp.concatenate([source_block == me, own_sources == numbers], 0).astype(BF16)
    earlier = (places[:, None] < places[None, :]).astype(BF16)
    rank = mm(chosen, earlier).astype(jnp.int32)
    turns = jnp.arange(per_peer, dtype=jnp.int32)[None, :, None]
    listed = (rank[:, None, :] == turns) & (chosen[:, None, :] > 0)
    leaving = jnp.sum(jnp.where(listed[:groups], lax.rem(dealt, rows_here)[:, None, :], 0), -1)
    own_order = jnp.sum(jnp.where(listed[groups:], places[None, None, :], 0), -1)
    leaving = leaving.reshape(groups, 2, half_peer)
    own_order = own_order.reshape(groups, 2, half_peer)

    def by_side(table):
        first, second = table[:, 0].reshape(-1), table[:, 1].reshape(-1)
        return jnp.concatenate(
            [jnp.where(side == 0, first, second), jnp.where(side == 0, second, first)]
        )

    leaving = by_side(leaving)
    own_order = by_side(own_order)
    expert_ids = jnp.arange(EXPERTS, dtype=jnp.int32)
    uses = jnp.sum((routes[:, :, None] == expert_ids[None, None, :]).astype(F32), 1)
    reorder = (own_order[:half_rows, None] == places[None, :]).astype(BF16)
    used = mm(reorder, uses.astype(BF16))

    told = jnp.tile(used.T.astype(BF16), (groups // EXPERTS, 1)).reshape(groups, per_peer, -1)

    small = jnp.concatenate(
        [
            attention_gain,
            ffn_gain,
            query_gain.reshape(-1),
            key_gain.reshape(-1),
            router_weight.reshape(-1),
        ]
    ).astype(BF16)
    small = jnp.broadcast_to(small.reshape(1, per_peer, -1), (groups, per_peer, small.size // per_peer))
    pick = (leaving[:half_rows, None] == places[None, :]).astype(BF16)
    sent = jnp.concatenate(
        [
            mm(pick, tokens).astype(BF16).reshape(groups, half_peer, model_width),
            mm(pick, cotangent).astype(BF16).reshape(groups, half_peer, model_width),
        ],
        1,
    )
    sent = jnp.concatenate([sent, small, told], 2)
    got = lax.all_to_all(sent, "dp", split_axis=0, concat_axis=0, tiled=True)

    packed_own, packed_sibling = pack_experts(expert_place, gate_weight, up_weight, down_weight)
    packed_experts = merge_cores(expert_place, packed_own, to_sibling(packed_sibling))
    got = after(got, packed_experts)
    rows = got[:, :half_peer, :model_width].reshape(half_rows, model_width).astype(F32)
    cot_rows = got[:, half_peer:, :model_width].reshape(half_rows, model_width)
    small = got[:, :, model_width : model_width + small.shape[2]].reshape(groups, -1)
    told = got[:, :, got.shape[2] - told.shape[2] :].reshape(groups, -1)
    told = lax.dynamic_slice_in_dim(told, me // EXPERTS * EXPERTS, EXPERTS, 0)
    uses_all = told.reshape(-1, 1).astype(F32)

    shard = attention_gain.shape[0]
    gain_shard = query_gain.shape[1]
    first_gain = small[:, :shard].reshape(-1).astype(F32)
    second_gain = small[:, shard : 2 * shard].reshape(-1).astype(F32)
    at = 2 * shard
    query_scale_gain = small[:, at : at + gain_shard].reshape(-1).astype(F32)
    key_scale_gain = small[:, at + gain_shard : at + 2 * gain_shard].reshape(-1).astype(F32)
    router_full = small[:, at + 2 * gain_shard :].reshape(model_width, EXPERTS)

    norm_one = row_scale(rows)
    normed_own = (rows * norm_one * first_gain).astype(BF16)
    normed_peer = to_peer(normed_own)

    hidden_half = gate_weight.shape[2]
    across = [list(range(at, groups, EXPERTS)) for at in range(EXPERTS)]
    own_chunks = [packed_experts[0]] + [None] * (moe_chips - 1)
    peer_chunks = [None] * moe_chips

    def chip_pairs(step):
        return [(index, index ^ (2 * step)) for index in range(groups)]

    def fetch_experts(steps):
        for step in steps:
            if step > 0:
                own_chunks[step] = lax.ppermute(packed_experts[step], "dp", chip_pairs(step))

    def share_experts(steps):
        for step in steps:
            peer_chunks[step] = to_peer(own_chunks[step])

    qkv_block = jnp.concatenate([query_weight, key_weight, value_weight], 1).astype(BF16)
    qkv_full = lax.all_gather(qkv_block, "dp", axis=0, tiled=True)
    output_full = lax.all_gather(output_weight.T.astype(BF16), "dp", axis=0, tiled=True)
    within = [list(range(at, at + EXPERTS)) for at in range(0, groups, EXPERTS)]
    in_group = {} if replicas == 1 else {"axis_index_groups": within}
    fetch_experts([4, 6, 1, 2, 3, 5, 7])
    own_chunks[0] = after(own_chunks[0], normed_peer)
    share_experts([0, 1, 2, 3])
    heads_width = query_weight.shape[1]
    order = ring_order(chips)

    finish_at = jnp.cumsum(lengths[0])
    start_at = finish_at - lengths[0]
    segment_ids = jnp.sum((own_order[:, None] >= finish_at[None, :]).astype(jnp.int32), -1)
    numbers = jnp.arange(lengths.shape[1], dtype=jnp.int32)
    begins = jnp.sum(jnp.where(segment_ids[:, None] == numbers[None, :], start_at[None, :], 0), -1)
    turn_tables = rope_tables((own_order - begins).astype(F32), HEAD_DIM)
    allowed = (segment_ids[:, None] == segment_ids[None, :]) & (
        own_order[None, :] <= own_order[:, None]
    )

    normed_one = jnp.concatenate([normed_own, normed_peer], 0)
    normed_one = after(normed_one, *[own_chunks[step] for step in (1, 2, 3, 4, 6)])
    qkv = mm(normed_one, qkv_full)
    query_raw, key_raw = qkv[:, :heads_width], qkv[:, heads_width : 2 * heads_width]

    def over_sides(values):
        theirs = to_peer(values)
        return values + jnp.concatenate([theirs[:, half_rows:], theirs[:, :half_rows]], 1)

    squares = over_sides(
        jnp.stack([jnp.sum(query_raw * query_raw, -1), jnp.sum(key_raw * key_raw, -1)])
    )
    scales = lax.rsqrt(squares / model_width + EPS)[:, :, None]
    heads_here = heads_width // HEAD_DIM
    head_inputs = (
        qkv,
        qkv,
        qkv,
        scales,
        jnp.stack([query_scale_gain, key_scale_gain]),
        turn_tables,
        allowed.astype(F32),
    )
    query_heads, key_heads, context, log_total = by_heads(
        attention_kernel, rows_here, heads_here, head_inputs, (), (BF16,) * 3, True
    )
    attention = outer_cols(context, output_full)
    attention = after(attention, own_chunks[5])
    attention = attention[:half_rows] + to_peer(
        attention[half_rows:].astype(BF16)
    ).astype(F32)
    for step in (4, 6, 5, 7):
        own_chunks[step] = after(own_chunks[step], attention)
    share_experts([4, 6, 5, 7])
    hidden = rows + attention

    norm_two = row_scale(hidden)
    normed_two = (hidden * norm_two * second_gain).astype(BF16)
    logits = mm(normed_two, router_full)
    powered_two = jnp.exp(logits - jnp.max(logits, -1, keepdims=True))
    router_probs = powered_two / jnp.sum(powered_two, -1, keepdims=True)

    def to_experts(table):
        return lax.all_to_all(table, "dp", split_axis=0, concat_axis=0, tiled=True, **in_group)


    def placed(chunks):
        size, width = chunks[0].shape
        whole = jnp.zeros((moe_chips * size, width), chunks[0].dtype)
        for step, chunk in enumerate(chunks):
            at = (expert_chip ^ step) * size
            whole = lax.dynamic_update_slice_in_dim(whole, chunk, at, 0)
        return whole

    expert_own, expert_peer = placed(own_chunks), placed(peer_chunks)
    if replicas > 1:
        expert_own, expert_peer = (
            lax.all_gather(part, "dp", axis=0, tiled=True, axis_index_groups=across)
            for part in (expert_own, expert_peer)
        )
    inputs_all = lax.all_gather(after(normed_two, own_chunks[7]), "dp", axis=0, tiled=True, **in_group)
    cot_all = lax.all_gather(cot_rows, "dp", axis=0, tiled=True, **in_group)
    input_grad, active, front_grad, cells, gates = expert_rows(
        expert[None].astype(jnp.int32),
        inputs_all,
        cot_all,
        uses_all,
        router_full,
        expert_own,
        expert_peer,
        rows_here,
    )

    def sum_experts(values):
        return lax.psum_scatter(values, "dp", scatter_dimension=0, tiled=True, **in_group)

    steps_back = [4, 1, 6, 2, 5, 3, 7, 0]
    early = 3 * moe_chips // 4
    chips_back = jnp.stack([expert_chip ^ step for step in steps_back]).astype(jnp.int32)
    block_order = chips_back if replicas == 1 else jnp.arange(moe_chips, dtype=jnp.int32)
    wgrad_first, wgrad_last, wgrad_own = expert_wgrads(
        block_order, inputs_all, cells, front_grad, active
    )
    normed_two_grad = after(sum_experts(input_grad), wgrad_own)
    if replicas == 1:
        peer_first = to_peer(wgrad_first)
    mixed, mixing = expert_mixture(active, cot_all, gates, expert_own, expert_peer, rows_here)
    normed_two_grad = normed_two_grad.astype(F32)
    mixing_table = to_experts(mixing.reshape(EXPERTS, -1))
    mixture = sum_experts(after(mixed, normed_two_grad)).astype(F32)
    out_rows = (hidden + mixture).astype(BF16)

    if replicas > 1:

        def over_replicas(values):
            values = lax.psum_scatter(
                values.reshape(model_width, -1),
                "dp",
                scatter_dimension=0,
                tiled=True,
                axis_index_groups=across,
            )
            return jnp.take(values.reshape(moe_chips, -1, values.shape[1]), chips_back, axis=0)

        wgrad_own = over_replicas(wgrad_own)
        wgrad_peer = over_replicas(jnp.concatenate([wgrad_first, wgrad_last], 0))
        wgrad_first, wgrad_last = wgrad_peer[:early], wgrad_peer[early:]
        peer_first = to_peer(wgrad_first)

    def add_wgrads(own, theirs):
        return list((own.astype(F32) + theirs.astype(F32)).astype(BF16))

    summed = add_wgrads(wgrad_own[:early], peer_first)

    def return_wgrad(at):
        step = steps_back[at]
        return lax.ppermute(summed[at], "dp", chip_pairs(step)) if step > 0 else summed[at]

    wgrad_chunks = [return_wgrad(at) for at in range(early)]

    prob_grad = mixing_table.T * used
    logit_grad = (
        router_probs * (prob_grad - jnp.sum(router_probs * prob_grad, -1, keepdims=True))
    ).astype(BF16)
    router_wgrad = inner_rows(normed_two, logit_grad)
    normed_two_grad = normed_two_grad + outer_cols(logit_grad, router_full)
    ffn_gain_grad = jnp.sum(normed_two_grad * hidden * norm_two, 0)
    scaled_two = normed_two_grad * second_gain
    hidden_grad = cot_rows.astype(F32) + norm_two * (
        scaled_two - hidden * norm_two * norm_two * jnp.mean(scaled_two * hidden, -1, keepdims=True)
    )

    attn_own = hidden_grad.astype(BF16)
    attn_peer = to_peer(attn_own)
    attn_grad = jnp.concatenate([attn_own, attn_peer], 0)
    attn_grad = after(attn_grad, summed[0])
    context_grad = mm(attn_grad, output_full).astype(BF16)
    query_norm_grad, key_norm_grad, value_grad, gain_grads, inner_parts = by_heads(
        attention_grad_kernel,
        rows_here,
        heads_here,
        head_inputs,
        (query_heads, key_heads, log_total, context_grad),
        (F32, F32, BF16),
        False,
    )
    output_wgrad = inner_rows(attn_grad, context).astype(BF16)
    query_gain_grad, key_gain_grad = gain_grads
    inners = over_sides(inner_parts[:, :, 0])
    query_scale, key_scale = scales
    output_wgrad = lax.psum_scatter(output_wgrad, "dp", scatter_dimension=0, tiled=True)
    peer_last = to_peer(after(wgrad_last, attn_peer))
    summed += add_wgrads(wgrad_own[early:], peer_last)
    wgrad_chunks += [return_wgrad(at) for at in range(early, moe_chips)]
    query_raw_grad = (
        query_scale * query_scale_gain * query_norm_grad
        - query_raw * query_scale**3 * inners[0][:, None] / model_width
    ).astype(BF16)
    key_raw_grad = (
        key_scale * key_scale_gain * key_norm_grad
        - key_raw * key_scale**3 * inners[1][:, None] / model_width
    ).astype(BF16)
    qkv_grad = jnp.concatenate([query_raw_grad, key_raw_grad, value_grad], 1)
    qkv_grad = after(qkv_grad, wgrad_chunks[0])
    ring_rows = columns_in(normed_one, order, chips)
    qkv_wgrad = inner_rows(ring_rows, qkv_grad).astype(BF16)
    normed_one_grad = outer_cols(qkv_grad, qkv_full)
    normed_one_grad = normed_one_grad[:half_rows] + to_peer(
        normed_one_grad[half_rows:].astype(BF16)
    ).astype(F32)
    attention_gain_grad = jnp.sum(normed_one_grad * rows * norm_one, 0)
    scaled_one = normed_one_grad * first_gain
    rows_grad = hidden_grad + norm_one * (
        scaled_one - rows * norm_one * norm_one * jnp.mean(scaled_one * rows, -1, keepdims=True)
    )

    small_grad = jnp.concatenate(
        [
            query_gain_grad.reshape(groups, -1),
            key_gain_grad.reshape(groups, -1),
            attention_gain_grad.reshape(groups, -1),
            ffn_gain_grad.reshape(groups, -1),
            router_wgrad.reshape(groups, -1),
        ],
        1,
    )
    small_grad = jnp.sum(
        lax.all_to_all(small_grad, "dp", split_axis=0, concat_axis=0, tiled=True), 0
    )
    at = 2 * gain_shard
    by_rows = small_grad[at:]
    by_rows = by_rows + to_peer(by_rows)

    place_back = (places[:, None] == leaving[None, :]).astype(BF16)

    def send_back(values):
        back = values.reshape(groups, half_peer, model_width)
        back = lax.all_to_all(back, "dp", split_axis=0, concat_axis=0, tiled=True)
        back = back.reshape(half_rows, model_width)
        return mm(place_back, jnp.concatenate([back, to_peer(back)], 0)).astype(BF16)

    block_out = send_back(after(out_rows, qkv_grad))
    token_grad = send_back(rows_grad.astype(BF16))
    qkv_wgrad = after(qkv_wgrad, wgrad_chunks[2], summed[early])
    qkv_wgrad = ring_scatter(pieces_of(qkv_wgrad, chips), chips, BF16, ((by_rows, wgrad_chunks[4]), token_grad, block_out))
    returned = jnp.stack(wgrad_chunks).reshape(moe_chips, 2, -1, 3 * hidden_half)
    of_sibling = to_sibling(lax.dynamic_index_in_dim(returned, 1 - core, 1, keepdims=False))
    gate_weight_grad, up_weight_grad, down_weight_grad = unpack_experts(
        jnp.append(chips_back, core).astype(jnp.int32), returned, of_sibling
    )
    return (
        block_out,
        token_grad,
        by_rows[:shard],
        qkv_wgrad[:, :heads_width],
        qkv_wgrad[:, heads_width : 2 * heads_width],
        qkv_wgrad[:, 2 * heads_width :],
        output_wgrad.T.astype(F32),
        small_grad[:gain_shard][None],
        small_grad[gain_shard:at][None],
        by_rows[shard : 2 * shard],
        by_rows[2 * shard :].reshape(router_weight.shape),
        gate_weight_grad,
        up_weight_grad,
        down_weight_grad,
    )


def solution(mesh):
    rows = P("dp", None)
    columns = P("tensor", "dp")
    inputs = (rows, rows, P(), rows, rows, P("dp"))
    inputs += (P("dp", "tensor"),) * 3 + (columns,) * 3 + (P("dp"), rows)
    inputs += (P(None, "dp", "tensor"),) * 2 + (P(None, "tensor", "dp"),)
    outputs = (rows, rows, P("dp")) + (P("dp", "tensor"),) * 3 + (columns,) * 3
    outputs += (P("dp"), rows) + (P(None, "dp", "tensor"),) * 2 + (P(None, "tensor", "dp"),)
    return jax.shard_map(body, mesh=mesh, in_specs=inputs, out_specs=outputs, check_vma=False)
```

```python
import jax
import jax.numpy as jnp
from jax import lax
from jax.experimental import pallas as pl
from jax.experimental.pallas import tpu as pltpu
from jax.sharding import PartitionSpec as P

HEAD_DIM = 128
EXPERTS = 16
EPS = 1e-05
ROPE_BASE = 10000.0
MASKED = -1e30
F32 = jnp.float32
BF16 = jnp.bfloat16


def row_scale(values):
    return lax.rsqrt(jnp.mean(values * values, -1, keepdims=True) + EPS)


def mm(left, right):
    return lax.dot_general(left, right, (((1,), (0,)), ((), ())), preferred_element_type=F32)


def inner_rows(left, right):
    return lax.dot_general(left, right, (((0,), (0,)), ((), ())), preferred_element_type=F32)


def outer_cols(left, right):
    return lax.dot_general(left, right, (((1,), (1,)), ((), ())), preferred_element_type=F32)


def rope_tables(positions, head_size):
    half_size = head_size // 2
    freq_table = ROPE_BASE ** (-2.0 * jnp.arange(half_size, dtype=F32) / head_size)
    angles = positions[:, None] * freq_table[None, :]
    cosines, sines = jnp.cos(angles), jnp.sin(angles)
    return jnp.stack(
        [jnp.concatenate([cosines, cosines], -1), jnp.concatenate([-sines, sines], -1)]
    )


def after(value, *others):
    return lax.optimization_barrier((value, others))[0]


def ring_chip(place, chips):
    return 2 * place if place < chips // 2 else 2 * (chips - 1 - place) + 1


def core_index():
    return lax.axis_index("dp") % 2


def flow_pairs(chips):
    pairs = []
    for first in range(0, lax.axis_size("dp"), 2 * chips):
        for place in range(chips):
            here = ring_chip(place, chips)
            for core, step in ((0, 1), (1, -1)):
                there = ring_chip((place + step) % chips, chips)
                pairs.append((first + 2 * here + core, first + 2 * there + core))
    return pairs


def ring_order(chips):
    chip = (lax.axis_index("dp") // 2) % chips
    place = jnp.where(chip % 2 == 0, chip // 2, chips - 1 - chip // 2)
    toward = jnp.where(core_index() == 0, -1, 1)
    offsets = [0]
    for step in range(1, chips // 2):
        offsets += [toward * step, -toward * step]
    offsets.append(chips // 2)
    places = [lax.rem(place + offset + chips, chips) for offset in offsets]
    return jnp.stack(
        [jnp.where(at < chips // 2, 2 * at, 2 * (chips - 1 - at) + 1) for at in places]
    )


def to_sibling(values):
    pairs = [(index, index ^ 1) for index in range(lax.axis_size("dp"))]
    return lax.ppermute(values, "dp", pairs)


def to_peer(values):
    return lax.ppermute(values, "tensor", [(0, 1), (1, 0)])


def by_core(mine, sibling, axis=0):
    return jnp.where(
        core_index() == 0,
        jnp.concatenate([mine, sibling], axis),
        jnp.concatenate([sibling, mine], axis),
    )


def core_part(values, core):
    size = values.shape[0] // 2
    return lax.dynamic_slice_in_dim(values, core * size, size, 0)


def ring_scatter(parts, chips, kind, waits=()):
    core, pairs = core_index(), flow_pairs(chips)
    parts = [part.astype(F32) for part in parts]
    theirs = to_sibling(core_part(parts[-1], 1 - core).astype(kind)).astype(F32)
    flow = lax.ppermute((core_part(parts[-1], core) + theirs).astype(kind), "dp", pairs)
    none = jnp.zeros_like(flow)
    flow = by_core(flow, none).astype(F32)
    for step in range(chips // 2 - 1, 0, -1):
        theirs = to_sibling(parts[2 * step - 1].astype(kind)).astype(F32)
        flow = after((parts[2 * step] + theirs + flow).astype(kind), *waits[-step:][:1])
        flow = lax.ppermute(flow, "dp", pairs).astype(F32)
    total = parts[0] + flow
    theirs = to_sibling(core_part(total, 1 - core).astype(kind)).astype(F32)
    return core_part(total, core) + theirs


def pieces_of(values, count, axis=0):
    size = values.shape[axis] // count
    return [lax.slice_in_dim(values, at * size, (at + 1) * size, axis=axis) for at in range(count)]


def columns_in(values, order, count):
    size = values.shape[1] // count
    blocks = [lax.dynamic_slice_in_dim(values, order[at] * size, size, 1) for at in range(count)]
    return jnp.concatenate(blocks, 1)


def pack_kernel(place_ref, gate_ref, up_ref, down_ref, own_ref, sibling_ref):
    width = gate_ref.shape[2]
    for out_ref, core in ((own_ref, place_ref[1]), (sibling_ref, 1 - place_ref[1])):
        out_ref[0, :, :width] = gate_ref[core].astype(BF16)
        out_ref[0, :, width : 2 * width] = up_ref[core].astype(BF16)
        out_ref[0, :, 2 * width :] = down_ref[core].T.astype(BF16)


def pack_experts(place, gate_weight, up_weight, down_weight):
    count, shard, width = gate_weight.shape
    side_in = pl.BlockSpec((2, shard, width), lambda k, p: (p[0] ^ k, 0, 0))
    down_in = pl.BlockSpec((2, width, shard), lambda k, p: (p[0] ^ k, 0, 0))
    out = pl.BlockSpec((1, shard, 3 * width), lambda k, p: (k, 0, 0))
    return pl.pallas_call(
        pack_kernel,
        grid_spec=pltpu.PrefetchScalarGridSpec(
            num_scalar_prefetch=1,
            grid=(count // 2,),
            in_specs=[side_in, side_in, down_in],
            out_specs=[out, out],
        ),
        out_shape=[jax.ShapeDtypeStruct((count // 2, shard, 3 * width), BF16)] * 2,
    )(place, gate_weight, up_weight, down_weight)


def merge_kernel(place_ref, own_ref, sibling_ref, out_ref):
    size = own_ref.shape[1]
    for part_ref, core in ((own_ref, place_ref[1]), (sibling_ref, 1 - place_ref[1])):
        out_ref[0, pl.ds(pl.multiple_of(core * size, size), size)] = part_ref[0]


def merge_cores(place, own, sibling):
    chips, size, width = own.shape
    part = pl.BlockSpec((1, size, width), lambda k, p: (k, 0, 0))
    return pl.pallas_call(
        merge_kernel,
        grid_spec=pltpu.PrefetchScalarGridSpec(
            num_scalar_prefetch=1,
            grid=(chips,),
            in_specs=[part, part],
            out_specs=pl.BlockSpec((1, 2 * size, width), lambda k, p: (k, 0, 0)),
        ),
        out_shape=jax.ShapeDtypeStruct((chips, 2 * size, width), own.dtype),
    )(place, own, sibling)


def unpack_kernel(place_ref, own_ref, sibling_ref, gate_ref, up_ref, down_ref):
    width = gate_ref.shape[2]
    own_core = place_ref[pl.num_programs(0)]
    for chunk, core in ((own_ref[0, 0], own_core), (sibling_ref[0], 1 - own_core)):
        chunk = chunk.astype(F32)
        gate_ref[core] = chunk[:, :width]
        up_ref[core] = chunk[:, width : 2 * width]
        down_ref[core] = chunk[:, 2 * width :].T


def unpack_experts(place, own, sibling):
    chips, _, shard, width = own.shape
    width = width // 3
    side_out = pl.BlockSpec((2, shard, width), lambda k, p: (p[k], 0, 0))
    down_out = pl.BlockSpec((2, width, shard), lambda k, p: (p[k], 0, 0))
    sides = jax.ShapeDtypeStruct((2 * chips, shard, width), F32)
    return pl.pallas_call(
        unpack_kernel,
        grid_spec=pltpu.PrefetchScalarGridSpec(
            num_scalar_prefetch=1,
            grid=(chips,),
            in_specs=[
                pl.BlockSpec((1, 1, shard, 3 * width), lambda k, p: (k, p[chips], 0, 0)),
                pl.BlockSpec((1, shard, 3 * width), lambda k, p: (k, 0, 0)),
            ],
            out_specs=[side_out, side_out, down_out],
        ),
        out_shape=[sides, sides, jax.ShapeDtypeStruct((2 * chips, width, shard), F32)],
    )(place, own, sibling)


ROW_VMEM = 48 * 1024 * 1024
LIGHT = pl.CostEstimate(flops=1024, bytes_accessed=1024, transcendentals=0)


def mix_grads(front, active_grad, width):
    gate_pre, up_pre = front[:, :width], front[:, width:]
    sigmoid_gate = 1.0 / (1.0 + jnp.exp(-gate_pre))
    active = (gate_pre * sigmoid_gate * up_pre).astype(BF16)
    gate_grad = active_grad * up_pre * sigmoid_gate * (1.0 + gate_pre * (1.0 - sigmoid_gate))
    up_grad = active_grad * gate_pre * sigmoid_gate
    return active, jnp.concatenate([gate_grad.astype(BF16), up_grad.astype(BF16)], 1)


def rows_kernel(
    expert_ref, rows_ref, cot_ref, use_ref, router_ref, own_ref, peer_ref, *out_refs
):
    grad_ref, active_ref, front_grad_ref, cells_ref, gate_ref = out_refs
    width = own_ref.shape[1] // 3
    logits = mm(rows_ref[...], router_ref[...])
    powered = jnp.exp(logits - jnp.max(logits, -1, keepdims=True))
    router_probs = powered / jnp.sum(powered, -1, keepdims=True)
    numbers = lax.broadcasted_iota(jnp.int32, router_probs.shape, 1)
    gate = jnp.sum(jnp.where(numbers == expert_ref[0], router_probs, 0.0), -1, keepdims=True)
    gate = gate * use_ref[...]
    gate_ref[...] = gate
    cells = (cot_ref[...].astype(F32) * gate).astype(BF16)
    cells_ref[...] = cells
    total = None
    for half, weights_ref in enumerate((own_ref, peer_ref)):
        front = mm(rows_ref[...], weights_ref[:, : 2 * width])
        active_grad = mm(cells, weights_ref[:, 2 * width :])
        active, front_grad = mix_grads(front, active_grad, width)
        active_ref[:, half * width : (half + 1) * width] = active
        front_grad_ref[:, 2 * half * width : 2 * (half + 1) * width] = front_grad
        part = outer_cols(front_grad, weights_ref[:, : 2 * width])
        total = part if total is None else total + part
    grad_ref[...] = total.astype(BF16)


def expert_rows(expert, rows, cot_rows, uses, router, own, peer, tile):
    count, model_width = rows.shape
    width = own.shape[1] // 3
    part = lambda columns: pl.BlockSpec((tile, columns), lambda i, e: (i, 0))
    whole = lambda values: pl.BlockSpec(
        values.shape, lambda i, e: (0, 0), pipeline_mode=pl.Buffered(1)
    )
    outs = (model_width, 2 * width, 4 * width, model_width)
    return pl.pallas_call(
        rows_kernel,
        grid_spec=pltpu.PrefetchScalarGridSpec(
            num_scalar_prefetch=1,
            grid=(count // tile,),
            in_specs=[part(model_width), part(model_width), part(1)]
            + [whole(values) for values in (router, own, peer)],
            out_specs=[part(columns) for columns in outs + (1,)],
        ),
        out_shape=[jax.ShapeDtypeStruct((count, columns), BF16) for columns in outs]
        + [jax.ShapeDtypeStruct((count, 1), F32)],
        compiler_params=pltpu.CompilerParams(vmem_limit_bytes=ROW_VMEM),
        cost_estimate=LIGHT,
    )(expert, rows, cot_rows, uses, router, own, peer)


def mixture_kernel(active_ref, cot_ref, gate_ref, own_ref, peer_ref, mixed_ref, mixing_ref):
    width = own_ref.shape[1]
    produced = outer_cols(active_ref[:, :width], own_ref[...])
    produced = produced + outer_cols(active_ref[:, width:], peer_ref[...])
    mixing_ref[...] = jnp.sum(produced * cot_ref[...].astype(F32), -1, keepdims=True)
    mixed_ref[...] = (produced * gate_ref[...]).astype(BF16)


def expert_mixture(active, cot_rows, gates, own, peer, tile):
    count, model_width = cot_rows.shape
    width = own.shape[1] // 3
    wide = pl.BlockSpec((tile, model_width), lambda i: (i, 0))
    single = pl.BlockSpec((tile, 1), lambda i: (i, 0))
    down = pl.BlockSpec((model_width, width), lambda i: (0, 2), pipeline_mode=pl.Buffered(1))
    return pl.pallas_call(
        mixture_kernel,
        grid=(count // tile,),
        in_specs=[pl.BlockSpec((tile, 2 * width), lambda i: (i, 0)), wide, single, down, down],
        out_specs=[wide, single],
        out_shape=[
            jax.ShapeDtypeStruct((count, model_width), BF16),
            jax.ShapeDtypeStruct((count, 1), F32),
        ],
        compiler_params=pltpu.CompilerParams(vmem_limit_bytes=ROW_VMEM),
        cost_estimate=LIGHT,
    )(active, cot_rows, gates, own, peer)


def wgrad_kernel(
    order_ref, rows_ref, cells_ref, front_grad_ref, active_ref, first_ref, last_ref, own_ref
):
    number, early = pl.program_id(0), 3 * pl.num_programs(0) // 4
    width = active_ref.shape[1] // 2
    front = mm(rows_ref[...].T, front_grad_ref[...]).astype(BF16)
    down = mm(cells_ref[...].T, active_ref[...]).astype(BF16)
    own_ref[0, :, : 2 * width] = front[:, : 2 * width]
    own_ref[0, :, 2 * width :] = down[:, :width]
    for wanted, out_ref in ((number < early, first_ref), (number >= early, last_ref)):

        @pl.when(wanted)
        def _():
            out_ref[0, :, : 2 * width] = front[:, 2 * width :]
            out_ref[0, :, 2 * width :] = down[:, width:]


def expert_wgrads(order, rows, cells, front_grad, active):
    count, model_width = rows.shape
    blocks = order.shape[0]
    early = 3 * blocks // 4
    size, width = model_width // blocks, active.shape[1] // 2
    columns = pl.BlockSpec((count, size), lambda i, o: (0, o[i]))
    whole = lambda values: pl.BlockSpec(
        values.shape, lambda i, o: (0, 0), pipeline_mode=pl.Buffered(1)
    )
    part = (1, size, 3 * width)
    return pl.pallas_call(
        wgrad_kernel,
        grid_spec=pltpu.PrefetchScalarGridSpec(
            num_scalar_prefetch=1,
            grid=(blocks,),
            in_specs=[columns, columns, whole(front_grad), whole(active)],
            out_specs=[
                pl.BlockSpec(part, lambda i, o: (jnp.minimum(i, early - 1), 0, 0)),
                pl.BlockSpec(part, lambda i, o: (jnp.maximum(i - early, 0), 0, 0)),
                pl.BlockSpec(part, lambda i, o: (i, 0, 0)),
            ],
        ),
        out_shape=[
            jax.ShapeDtypeStruct((many, size, 3 * width), BF16) for many in (early, blocks - early, blocks)
        ],
        compiler_params=pltpu.CompilerParams(vmem_limit_bytes=ROW_VMEM),
        cost_estimate=LIGHT,
    )(order, rows, cells, front_grad, active)


def attention_kernel(
    query_ref, key_ref, value_ref, scale_ref, gain_ref, turn_ref, mask_ref, *out_refs
):
    rotated_query_ref, rotated_key_ref, context_ref, log_ref = out_refs
    cosine, sine = turn_ref[0], turn_ref[1]
    rotated = []
    for number, (raw_ref, out_ref) in enumerate(
        ((query_ref, rotated_query_ref), (key_ref, rotated_key_ref))
    ):
        normed = raw_ref[...] * scale_ref[number] * gain_ref[number : number + 1]
        turned = normed * cosine + pltpu.roll(normed, HEAD_DIM // 2, 1) * sine
        rotated.append(turned.astype(BF16))
        out_ref[...] = rotated[number]
    scores = outer_cols(rotated[0], rotated[1]) * HEAD_DIM ** (-0.5)
    scores = jnp.where(mask_ref[...] > 0, scores, MASKED)
    peak_value = jnp.max(scores, -1, keepdims=True)
    powered = jnp.exp(scores - peak_value)
    total_weight = jnp.sum(powered, -1, keepdims=True)
    probs = (powered / total_weight).astype(BF16)
    log_ref[0] = peak_value + jnp.log(total_weight)
    context_ref[...] = mm(probs, value_ref[...].astype(BF16)).astype(BF16)


def attention_grad_kernel(
    query_ref,
    key_ref,
    value_ref,
    scale_ref,
    gain_ref,
    turn_ref,
    mask_ref,
    rotated_query_ref,
    rotated_key_ref,
    log_ref,
    context_grad_ref,
    query_grad_ref,
    key_grad_ref,
    value_grad_ref,
    gain_grad_ref,
    inner_ref,
):
    head_scale = HEAD_DIM ** (-0.5)
    cosine, sine = turn_ref[0], turn_ref[1]
    query, key = rotated_query_ref[...], rotated_key_ref[...]
    scores = outer_cols(query, key) * head_scale
    scores = jnp.where(mask_ref[...] > 0, scores, MASKED)
    probs = jnp.exp(scores - log_ref[0])
    context_grad = context_grad_ref[...]
    probs_grad = outer_cols(context_grad, value_ref[...].astype(BF16))
    value_grad_ref[...] = mm(probs.astype(BF16).T, context_grad).astype(BF16)
    scores_grad = probs * (probs_grad - jnp.sum(probs * probs_grad, -1, keepdims=True))
    scores_grad = scores_grad.astype(BF16)

    @pl.when(pl.program_id(0) == 0)
    def _():
        inner_ref[...] = jnp.zeros_like(inner_ref)

    for number, (raw_ref, grad, out_ref) in enumerate(
        (
            (query_ref, mm(scores_grad, key), query_grad_ref),
            (key_ref, mm(scores_grad.T, query), key_grad_ref),
        )
    ):
        grad = grad * head_scale
        grad = grad * cosine - pltpu.roll(grad, HEAD_DIM // 2, 1) * sine
        out_ref[...] = grad
        raw = raw_ref[...]
        gain_grad_ref[number : number + 1] = jnp.sum(
            grad * raw * scale_ref[number], 0, keepdims=True
        )
        inner_ref[number] += jnp.sum(
            grad * gain_ref[number : number + 1] * raw, -1, keepdims=True
        )


def by_heads(kernel, rows, heads, inputs, extra, outs, log_out):
    column = pl.BlockSpec((rows, HEAD_DIM), lambda h: (0, h))
    at = lambda part: pl.BlockSpec((rows, HEAD_DIM), lambda h: (0, part * heads + h))
    logs = pl.BlockSpec((1, rows, 1), lambda h: (h, 0, 0))
    pair = pl.BlockSpec((2, HEAD_DIM), lambda h: (0, h))
    whole = lambda *shape: pl.BlockSpec(shape, lambda h: (0,) * len(shape))
    in_specs = [at(0), at(1), at(2), whole(2, rows, 1), pair]
    in_specs += [whole(2, rows, HEAD_DIM), whole(rows, rows)]
    in_specs += [logs if values.ndim == 3 else column for values in extra]
    out_shape = [jax.ShapeDtypeStruct((rows, heads * HEAD_DIM), kind) for kind in outs]
    out_specs = [column] * len(outs)
    if log_out:
        out_shape += [jax.ShapeDtypeStruct((heads, rows, 1), F32)]
        out_specs += [logs]
    else:
        out_shape += [
            jax.ShapeDtypeStruct((2, heads * HEAD_DIM), F32),
            jax.ShapeDtypeStruct((2, rows, 1), F32),
        ]
        out_specs += [pair, whole(2, rows, 1)]
    return pl.pallas_call(
        kernel,
        grid=(heads,),
        in_specs=in_specs,
        out_specs=out_specs,
        out_shape=out_shape,
        cost_estimate=LIGHT,
    )(*inputs, *extra)


def body(
    tokens,
    cotangent,
    dealing,
    lengths,
    routes,
    attention_gain,
    query_weight,
    key_weight,
    value_weight,
    output_weight,
    query_gain,
    key_gain,
    ffn_gain,
    router_weight,
    gate_weight,
    up_weight,
    down_weight,
):
    groups = lax.axis_size("dp")
    me = lax.axis_index("dp")
    side = lax.axis_index("tensor")
    rows_here, model_width = tokens.shape
    per_peer = rows_here // groups
    half_peer = per_peer // 2
    half_rows = rows_here // 2
    chips = groups // 2
    moe_chips = EXPERTS // 2
    replicas = groups // EXPERTS
    expert = lax.rem(me, EXPERTS)
    expert_chip, core = expert // 2, core_index()
    expert_place = jnp.stack([expert_chip, core]).astype(jnp.int32)

    dealt = dealing.reshape(groups, rows_here)
    places = jnp.arange(rows_here, dtype=jnp.int32)
    source_block = dealt // rows_here
    own_sources = lax.dynamic_slice_in_dim(source_block, me, 1, 0)
    numbers = jnp.arange(groups, dtype=jnp.int32)[:, None]
    chosen = jnp.concatenate([source_block == me, own_sources == numbers], 0).astype(BF16)
    earlier = (places[:, None] < places[None, :]).astype(BF16)
    rank = mm(chosen, earlier).astype(jnp.int32)
    turns = jnp.arange(per_peer, dtype=jnp.int32)[None, :, None]
    listed = (rank[:, None, :] == turns) & (chosen[:, None, :] > 0)
    leaving = jnp.sum(jnp.where(listed[:groups], lax.rem(dealt, rows_here)[:, None, :], 0), -1)
    own_order = jnp.sum(jnp.where(listed[groups:], places[None, None, :], 0), -1)
    leaving = leaving.reshape(groups, 2, half_peer)
    own_order = own_order.reshape(groups, 2, half_peer)

    def by_side(table):
        first, second = table[:, 0].reshape(-1), table[:, 1].reshape(-1)
        return jnp.concatenate(
            [jnp.where(side == 0, first, second), jnp.where(side == 0, second, first)]
        )

    leaving = by_side(leaving)
    own_order = by_side(own_order)
    expert_ids = jnp.arange(EXPERTS, dtype=jnp.int32)
    uses = jnp.sum((routes[:, :, None] == expert_ids[None, None, :]).astype(F32), 1)
    reorder = (own_order[:half_rows, None] == places[None, :]).astype(BF16)
    used = mm(reorder, uses.astype(BF16))

    told = jnp.tile(used.T.astype(BF16), (groups // EXPERTS, 1)).reshape(groups, per_peer, -1)

    small = jnp.concatenate(
        [
            attention_gain,
            ffn_gain,
            query_gain.reshape(-1),
            key_gain.reshape(-1),
            router_weight.reshape(-1),
        ]
    ).astype(BF16)
    small = jnp.broadcast_to(small.reshape(1, per_peer, -1), (groups, per_peer, small.size // per_peer))
    pick = (leaving[:half_rows, None] == places[None, :]).astype(BF16)
    sent = jnp.concatenate(
        [
            mm(pick, tokens).astype(BF16).reshape(groups, half_peer, model_width),
            mm(pick, cotangent).astype(BF16).reshape(groups, half_peer, model_width),
        ],
        1,
    )
    sent = jnp.concatenate([sent, small, told], 2)
    got = lax.all_to_all(sent, "dp", split_axis=0, concat_axis=0, tiled=True)

    packed_own, packed_sibling = pack_experts(expert_place, gate_weight, up_weight, down_weight)
    packed_experts = merge_cores(expert_place, packed_own, to_sibling(packed_sibling))
    got = after(got, packed_experts)
    rows = got[:, :half_peer, :model_width].reshape(half_rows, model_width).astype(F32)
    cot_rows = got[:, half_peer:, :model_width].reshape(half_rows, model_width)
    small = got[:, :, model_width : model_width + small.shape[2]].reshape(groups, -1)
    told = got[:, :, got.shape[2] - told.shape[2] :].reshape(groups, -1)
    told = lax.dynamic_slice_in_dim(told, me // EXPERTS * EXPERTS, EXPERTS, 0)
    uses_all = told.reshape(-1, 1).astype(F32)

    shard = attention_gain.shape[0]
    gain_shard = query_gain.shape[1]
    first_gain = small[:, :shard].reshape(-1).astype(F32)
    second_gain = small[:, shard : 2 * shard].reshape(-1).astype(F32)
    at = 2 * shard
    query_scale_gain = small[:, at : at + gain_shard].reshape(-1).astype(F32)
    key_scale_gain = small[:, at + gain_shard : at + 2 * gain_shard].reshape(-1).astype(F32)
    router_full = small[:, at + 2 * gain_shard :].reshape(model_width, EXPERTS)

    norm_one = row_scale(rows)
    normed_own = (rows * norm_one * first_gain).astype(BF16)
    normed_peer = to_peer(normed_own)

    hidden_half = gate_weight.shape[2]
    across = [list(range(at, groups, EXPERTS)) for at in range(EXPERTS)]
    own_chunks = [packed_experts[0]] + [None] * (moe_chips - 1)
    peer_chunks = [None] * moe_chips

    def chip_pairs(step):
        return [(index, index ^ (2 * step)) for index in range(groups)]

    def fetch_experts(steps):
        for step in steps:
            if step > 0:
                own_chunks[step] = lax.ppermute(packed_experts[step], "dp", chip_pairs(step))

    def share_experts(steps):
        for step in steps:
            peer_chunks[step] = to_peer(own_chunks[step])

    qkv_block = jnp.concatenate([query_weight, key_weight, value_weight], 1).astype(BF16)
    qkv_full = lax.all_gather(qkv_block, "dp", axis=0, tiled=True)
    output_full = lax.all_gather(output_weight.T.astype(BF16), "dp", axis=0, tiled=True)
    within = [list(range(at, at + EXPERTS)) for at in range(0, groups, EXPERTS)]
    in_group = {} if replicas == 1 else {"axis_index_groups": within}
    fetch_experts([4, 6, 1, 2, 3])
    packed_experts = list(packed_experts)
    for step in (5, 7):
        packed_experts[step] = after(packed_experts[step], output_full)
    fetch_experts([5, 7])
    own_chunks[0] = after(own_chunks[0], normed_peer)
    share_experts([0, 1, 2, 3])
    heads_width = query_weight.shape[1]
    order = ring_order(chips)

    finish_at = jnp.cumsum(lengths[0])
    start_at = finish_at - lengths[0]
    segment_ids = jnp.sum((own_order[:, None] >= finish_at[None, :]).astype(jnp.int32), -1)
    numbers = jnp.arange(lengths.shape[1], dtype=jnp.int32)
    begins = jnp.sum(jnp.where(segment_ids[:, None] == numbers[None, :], start_at[None, :], 0), -1)
    turn_tables = rope_tables((own_order - begins).astype(F32), HEAD_DIM)
    allowed = (segment_ids[:, None] == segment_ids[None, :]) & (
        own_order[None, :] <= own_order[:, None]
    )

    normed_one = jnp.concatenate([normed_own, normed_peer], 0)
    normed_one = after(normed_one, *[own_chunks[step] for step in (1, 2, 3, 4, 6)])
    qkv = mm(normed_one, qkv_full)
    query_raw, key_raw = qkv[:, :heads_width], qkv[:, heads_width : 2 * heads_width]

    def over_sides(values):
        theirs = to_peer(values)
        return values + jnp.concatenate([theirs[:, half_rows:], theirs[:, :half_rows]], 1)

    squares = over_sides(
        jnp.stack([jnp.sum(query_raw * query_raw, -1), jnp.sum(key_raw * key_raw, -1)])
    )
    scales = lax.rsqrt(squares / model_width + EPS)[:, :, None]
    for step in (4, 6):
        own_chunks[step] = after(own_chunks[step], squares)
    share_experts([4, 6])
    heads_here = heads_width // HEAD_DIM
    head_inputs = (
        qkv,
        qkv,
        qkv,
        scales,
        jnp.stack([query_scale_gain, key_scale_gain]),
        turn_tables,
        allowed.astype(F32),
    )
    query_heads, key_heads, context, log_total = by_heads(
        attention_kernel, rows_here, heads_here, head_inputs, (), (BF16,) * 3, True
    )
    attention = outer_cols(context, output_full)
    attention = after(attention, peer_chunks[4], peer_chunks[6])
    attention = attention[:half_rows] + to_peer(
        attention[half_rows:].astype(BF16)
    ).astype(F32)
    for step in (5, 7):
        own_chunks[step] = after(own_chunks[step], attention)
    share_experts([5, 7])
    hidden = rows + attention

    norm_two = row_scale(hidden)
    normed_two = (hidden * norm_two * second_gain).astype(BF16)
    logits = mm(normed_two, router_full)
    powered_two = jnp.exp(logits - jnp.max(logits, -1, keepdims=True))
    router_probs = powered_two / jnp.sum(powered_two, -1, keepdims=True)

    def to_experts(table):
        return lax.all_to_all(table, "dp", split_axis=0, concat_axis=0, tiled=True, **in_group)


    def placed(chunks):
        size, width = chunks[0].shape
        whole = jnp.zeros((moe_chips * size, width), chunks[0].dtype)
        for step, chunk in enumerate(chunks):
            at = (expert_chip ^ step) * size
            whole = lax.dynamic_update_slice_in_dim(whole, chunk, at, 0)
        return whole

    expert_own, expert_peer = placed(own_chunks), placed(peer_chunks)
    if replicas > 1:
        expert_own, expert_peer = (
            lax.all_gather(part, "dp", axis=0, tiled=True, axis_index_groups=across)
            for part in (expert_own, expert_peer)
        )
    inputs_all = lax.all_gather(after(normed_two, own_chunks[7]), "dp", axis=0, tiled=True, **in_group)
    cot_all = lax.all_gather(cot_rows, "dp", axis=0, tiled=True, **in_group)
    input_grad, active, front_grad, cells, gates = expert_rows(
        expert[None].astype(jnp.int32),
        inputs_all,
        cot_all,
        uses_all,
        router_full,
        expert_own,
        expert_peer,
        rows_here,
    )

    def sum_experts(values):
        return lax.psum_scatter(values, "dp", scatter_dimension=0, tiled=True, **in_group)

    steps_back = [4, 1, 6, 2, 5, 3, 7, 0]
    early = 3 * moe_chips // 4
    chips_back = jnp.stack([expert_chip ^ step for step in steps_back]).astype(jnp.int32)
    block_order = chips_back if replicas == 1 else jnp.arange(moe_chips, dtype=jnp.int32)
    wgrad_first, wgrad_last, wgrad_own = expert_wgrads(
        block_order, inputs_all, cells, front_grad, active
    )
    normed_two_grad = after(sum_experts(input_grad), wgrad_own)
    if replicas == 1:
        peer_first = to_peer(wgrad_first)
    mixed, mixing = expert_mixture(active, cot_all, gates, expert_own, expert_peer, rows_here)
    normed_two_grad = normed_two_grad.astype(F32)
    mixing_table = to_experts(mixing.reshape(EXPERTS, -1))
    mixture = sum_experts(after(mixed, normed_two_grad)).astype(F32)
    out_rows = (hidden + mixture).astype(BF16)

    if replicas > 1:

        def over_replicas(values):
            values = lax.psum_scatter(
                values.reshape(model_width, -1),
                "dp",
                scatter_dimension=0,
                tiled=True,
                axis_index_groups=across,
            )
            return jnp.take(values.reshape(moe_chips, -1, values.shape[1]), chips_back, axis=0)

        wgrad_own = over_replicas(wgrad_own)
        wgrad_peer = over_replicas(jnp.concatenate([wgrad_first, wgrad_last], 0))
        wgrad_first, wgrad_last = wgrad_peer[:early], wgrad_peer[early:]
        peer_first = to_peer(wgrad_first)

    def add_wgrads(own, theirs):
        return list((own.astype(F32) + theirs.astype(F32)).astype(BF16))

    summed = add_wgrads(wgrad_own[:early], peer_first)

    def return_wgrad(at):
        step = steps_back[at]
        return lax.ppermute(summed[at], "dp", chip_pairs(step)) if step > 0 else summed[at]

    wgrad_chunks = [return_wgrad(at) for at in range(early)]

    prob_grad = mixing_table.T * used
    logit_grad = (
        router_probs * (prob_grad - jnp.sum(router_probs * prob_grad, -1, keepdims=True))
    ).astype(BF16)
    router_wgrad = inner_rows(normed_two, logit_grad)
    normed_two_grad = normed_two_grad + outer_cols(logit_grad, router_full)
    ffn_gain_grad = jnp.sum(normed_two_grad * hidden * norm_two, 0)
    scaled_two = normed_two_grad * second_gain
    hidden_grad = cot_rows.astype(F32) + norm_two * (
        scaled_two - hidden * norm_two * norm_two * jnp.mean(scaled_two * hidden, -1, keepdims=True)
    )

    attn_own = hidden_grad.astype(BF16)
    attn_peer = to_peer(attn_own)
    attn_grad = jnp.concatenate([attn_own, attn_peer], 0)
    attn_grad = after(attn_grad, summed[0])
    context_grad = mm(attn_grad, output_full).astype(BF16)
    query_norm_grad, key_norm_grad, value_grad, gain_grads, inner_parts = by_heads(
        attention_grad_kernel,
        rows_here,
        heads_here,
        head_inputs,
        (query_heads, key_heads, log_total, context_grad),
        (F32, F32, BF16),
        False,
    )
    output_wgrad = inner_rows(attn_grad, context).astype(BF16)
    query_gain_grad, key_gain_grad = gain_grads
    inners = over_sides(inner_parts[:, :, 0])
    query_scale, key_scale = scales
    output_wgrad = lax.psum_scatter(output_wgrad, "dp", scatter_dimension=0, tiled=True)
    peer_last = to_peer(after(wgrad_last, attn_peer))
    summed += add_wgrads(wgrad_own[early:], peer_last)
    wgrad_chunks += [return_wgrad(at) for at in range(early, moe_chips)]
    query_raw_grad = (
        query_scale * query_scale_gain * query_norm_grad
        - query_raw * query_scale**3 * inners[0][:, None] / model_width
    ).astype(BF16)
    key_raw_grad = (
        key_scale * key_scale_gain * key_norm_grad
        - key_raw * key_scale**3 * inners[1][:, None] / model_width
    ).astype(BF16)
    qkv_grad = jnp.concatenate([query_raw_grad, key_raw_grad, value_grad], 1)
    ring_rows = columns_in(normed_one, order, chips)
    qkv_wgrad = inner_rows(ring_rows, qkv_grad).astype(BF16)
    normed_one_grad = outer_cols(qkv_grad, qkv_full)
    normed_one_grad = normed_one_grad[:half_rows] + to_peer(
        normed_one_grad[half_rows:].astype(BF16)
    ).astype(F32)
    attention_gain_grad = jnp.sum(normed_one_grad * rows * norm_one, 0)
    scaled_one = normed_one_grad * first_gain
    rows_grad = hidden_grad + norm_one * (
        scaled_one - rows * norm_one * norm_one * jnp.mean(scaled_one * rows, -1, keepdims=True)
    )

    small_grad = jnp.concatenate(
        [
            query_gain_grad.reshape(groups, -1),
            key_gain_grad.reshape(groups, -1),
            attention_gain_grad.reshape(groups, -1),
            ffn_gain_grad.reshape(groups, -1),
            router_wgrad.reshape(groups, -1),
        ],
        1,
    )
    small_grad = jnp.sum(
        lax.all_to_all(small_grad, "dp", split_axis=0, concat_axis=0, tiled=True), 0
    )
    at = 2 * gain_shard
    by_rows = small_grad[at:]
    by_rows = by_rows + to_peer(by_rows)

    place_back = (places[:, None] == leaving[None, :]).astype(BF16)

    def send_back(values):
        back = values.reshape(groups, half_peer, model_width)
        back = lax.all_to_all(back, "dp", split_axis=0, concat_axis=0, tiled=True)
        back = back.reshape(half_rows, model_width)
        return mm(place_back, jnp.concatenate([back, to_peer(back)], 0)).astype(BF16)

    block_out = send_back(after(out_rows, qkv_grad))
    token_grad = send_back(rows_grad.astype(BF16))
    qkv_wgrad = after(qkv_wgrad, wgrad_chunks[0], wgrad_chunks[2], summed[early])
    qkv_wgrad = ring_scatter(pieces_of(qkv_wgrad, chips), chips, BF16, ((by_rows, wgrad_chunks[4]), token_grad, block_out))
    returned = jnp.stack(wgrad_chunks).reshape(moe_chips, 2, -1, 3 * hidden_half)
    of_sibling = to_sibling(lax.dynamic_index_in_dim(returned, 1 - core, 1, keepdims=False))
    gate_weight_grad, up_weight_grad, down_weight_grad = unpack_experts(
        jnp.append(chips_back, core).astype(jnp.int32), returned, of_sibling
    )
    return (
        block_out,
        token_grad,
        by_rows[:shard],
        qkv_wgrad[:, :heads_width],
        qkv_wgrad[:, heads_width : 2 * heads_width],
        qkv_wgrad[:, 2 * heads_width :],
        output_wgrad.T.astype(F32),
        small_grad[:gain_shard][None],
        small_grad[gain_shard:at][None],
        by_rows[shard : 2 * shard],
        by_rows[2 * shard :].reshape(router_weight.shape),
        gate_weight_grad,
        up_weight_grad,
        down_weight_grad,
    )


def solution(mesh):
    rows = P("dp", None)
    columns = P("tensor", "dp")
    inputs = (rows, rows, P(), rows, rows, P("dp"))
    inputs += (P("dp", "tensor"),) * 3 + (columns,) * 3 + (P("dp"), rows)
    inputs += (P(None, "dp", "tensor"),) * 2 + (P(None, "tensor", "dp"),)
    outputs = (rows, rows, P("dp")) + (P("dp", "tensor"),) * 3 + (columns,) * 3
    outputs += (P("dp"), rows) + (P(None, "dp", "tensor"),) * 2 + (P(None, "tensor", "dp"),)
    return jax.shard_map(body, mesh=mesh, in_specs=inputs, out_specs=outputs, check_vma=False)
```

```python
import jax
import jax.numpy as jnp
from jax import lax
from jax.experimental import pallas as pl
from jax.experimental.pallas import tpu as pltpu
from jax.sharding import PartitionSpec as P

HEAD_DIM = 128
EXPERTS = 16
EPS = 1e-05
ROPE_BASE = 10000.0
MASKED = -1e30
F32 = jnp.float32
BF16 = jnp.bfloat16


def row_scale(values):
    return lax.rsqrt(jnp.mean(values * values, -1, keepdims=True) + EPS)


def mm(left, right):
    return lax.dot_general(left, right, (((1,), (0,)), ((), ())), preferred_element_type=F32)


def inner_rows(left, right):
    return lax.dot_general(left, right, (((0,), (0,)), ((), ())), preferred_element_type=F32)


def outer_cols(left, right):
    return lax.dot_general(left, right, (((1,), (1,)), ((), ())), preferred_element_type=F32)


def rope_tables(positions, head_size):
    half_size = head_size // 2
    freq_table = ROPE_BASE ** (-2.0 * jnp.arange(half_size, dtype=F32) / head_size)
    angles = positions[:, None] * freq_table[None, :]
    cosines, sines = jnp.cos(angles), jnp.sin(angles)
    return jnp.stack(
        [jnp.concatenate([cosines, cosines], -1), jnp.concatenate([-sines, sines], -1)]
    )


def after(value, *others):
    return lax.optimization_barrier((value, others))[0]


def ring_chip(place, chips):
    return 2 * place if place < chips // 2 else 2 * (chips - 1 - place) + 1


def core_index():
    return lax.axis_index("dp") % 2


def flow_pairs(chips):
    pairs = []
    for first in range(0, lax.axis_size("dp"), 2 * chips):
        for place in range(chips):
            here = ring_chip(place, chips)
            for core, step in ((0, 1), (1, -1)):
                there = ring_chip((place + step) % chips, chips)
                pairs.append((first + 2 * here + core, first + 2 * there + core))
    return pairs


def ring_order(chips):
    chip = (lax.axis_index("dp") // 2) % chips
    place = jnp.where(chip % 2 == 0, chip // 2, chips - 1 - chip // 2)
    toward = jnp.where(core_index() == 0, -1, 1)
    offsets = [0]
    for step in range(1, chips // 2):
        offsets += [toward * step, -toward * step]
    offsets.append(chips // 2)
    places = [lax.rem(place + offset + chips, chips) for offset in offsets]
    return jnp.stack(
        [jnp.where(at < chips // 2, 2 * at, 2 * (chips - 1 - at) + 1) for at in places]
    )


def to_sibling(values):
    pairs = [(index, index ^ 1) for index in range(lax.axis_size("dp"))]
    return lax.ppermute(values, "dp", pairs)


def to_peer(values):
    return lax.ppermute(values, "tensor", [(0, 1), (1, 0)])


def by_core(mine, sibling, axis=0):
    return jnp.where(
        core_index() == 0,
        jnp.concatenate([mine, sibling], axis),
        jnp.concatenate([sibling, mine], axis),
    )


def core_part(values, core):
    size = values.shape[0] // 2
    return lax.dynamic_slice_in_dim(values, core * size, size, 0)


def ring_scatter(parts, chips, kind, waits=()):
    core, pairs = core_index(), flow_pairs(chips)
    parts = [part.astype(F32) for part in parts]
    theirs = to_sibling(core_part(parts[-1], 1 - core).astype(kind)).astype(F32)
    flow = lax.ppermute((core_part(parts[-1], core) + theirs).astype(kind), "dp", pairs)
    none = jnp.zeros_like(flow)
    flow = by_core(flow, none).astype(F32)
    for step in range(chips // 2 - 1, 0, -1):
        theirs = to_sibling(parts[2 * step - 1].astype(kind)).astype(F32)
        flow = after((parts[2 * step] + theirs + flow).astype(kind), *waits[-step:][:1])
        flow = lax.ppermute(flow, "dp", pairs).astype(F32)
    total = parts[0] + flow
    theirs = to_sibling(core_part(total, 1 - core).astype(kind)).astype(F32)
    return core_part(total, core) + theirs


def pieces_of(values, count, axis=0):
    size = values.shape[axis] // count
    return [lax.slice_in_dim(values, at * size, (at + 1) * size, axis=axis) for at in range(count)]


def columns_in(values, order, count):
    size = values.shape[1] // count
    blocks = [lax.dynamic_slice_in_dim(values, order[at] * size, size, 1) for at in range(count)]
    return jnp.concatenate(blocks, 1)


def pack_kernel(place_ref, gate_ref, up_ref, down_ref, own_ref, sibling_ref):
    width = gate_ref.shape[2]
    for out_ref, core in ((own_ref, place_ref[1]), (sibling_ref, 1 - place_ref[1])):
        out_ref[0, :, :width] = gate_ref[core].astype(BF16)
        out_ref[0, :, width : 2 * width] = up_ref[core].astype(BF16)
        out_ref[0, :, 2 * width :] = down_ref[core].T.astype(BF16)


def pack_experts(place, gate_weight, up_weight, down_weight):
    count, shard, width = gate_weight.shape
    side_in = pl.BlockSpec((2, shard, width), lambda k, p: (p[0] ^ k, 0, 0))
    down_in = pl.BlockSpec((2, width, shard), lambda k, p: (p[0] ^ k, 0, 0))
    out = pl.BlockSpec((1, shard, 3 * width), lambda k, p: (k, 0, 0))
    return pl.pallas_call(
        pack_kernel,
        grid_spec=pltpu.PrefetchScalarGridSpec(
            num_scalar_prefetch=1,
            grid=(count // 2,),
            in_specs=[side_in, side_in, down_in],
            out_specs=[out, out],
        ),
        out_shape=[jax.ShapeDtypeStruct((count // 2, shard, 3 * width), BF16)] * 2,
    )(place, gate_weight, up_weight, down_weight)


def merge_kernel(place_ref, own_ref, sibling_ref, out_ref):
    size = own_ref.shape[1]
    for part_ref, core in ((own_ref, place_ref[1]), (sibling_ref, 1 - place_ref[1])):
        out_ref[0, pl.ds(pl.multiple_of(core * size, size), size)] = part_ref[0]


def merge_cores(place, own, sibling):
    chips, size, width = own.shape
    part = pl.BlockSpec((1, size, width), lambda k, p: (k, 0, 0))
    return pl.pallas_call(
        merge_kernel,
        grid_spec=pltpu.PrefetchScalarGridSpec(
            num_scalar_prefetch=1,
            grid=(chips,),
            in_specs=[part, part],
            out_specs=pl.BlockSpec((1, 2 * size, width), lambda k, p: (k, 0, 0)),
        ),
        out_shape=jax.ShapeDtypeStruct((chips, 2 * size, width), own.dtype),
    )(place, own, sibling)


def unpack_kernel(place_ref, own_ref, sibling_ref, gate_ref, up_ref, down_ref):
    width = gate_ref.shape[2]
    own_core = place_ref[pl.num_programs(0)]
    for chunk, core in ((own_ref[0, 0], own_core), (sibling_ref[0], 1 - own_core)):
        chunk = chunk.astype(F32)
        gate_ref[core] = chunk[:, :width]
        up_ref[core] = chunk[:, width : 2 * width]
        down_ref[core] = chunk[:, 2 * width :].T


def unpack_experts(place, own, sibling):
    chips, _, shard, width = own.shape
    width = width // 3
    side_out = pl.BlockSpec((2, shard, width), lambda k, p: (p[k], 0, 0))
    down_out = pl.BlockSpec((2, width, shard), lambda k, p: (p[k], 0, 0))
    sides = jax.ShapeDtypeStruct((2 * chips, shard, width), F32)
    return pl.pallas_call(
        unpack_kernel,
        grid_spec=pltpu.PrefetchScalarGridSpec(
            num_scalar_prefetch=1,
            grid=(chips,),
            in_specs=[
                pl.BlockSpec((1, 1, shard, 3 * width), lambda k, p: (k, p[chips], 0, 0)),
                pl.BlockSpec((1, shard, 3 * width), lambda k, p: (k, 0, 0)),
            ],
            out_specs=[side_out, side_out, down_out],
        ),
        out_shape=[sides, sides, jax.ShapeDtypeStruct((2 * chips, width, shard), F32)],
    )(place, own, sibling)


ROW_VMEM = 48 * 1024 * 1024
LIGHT = pl.CostEstimate(flops=1024, bytes_accessed=1024, transcendentals=0)


def mix_grads(front, active_grad, width):
    gate_pre, up_pre = front[:, :width], front[:, width:]
    sigmoid_gate = 1.0 / (1.0 + jnp.exp(-gate_pre))
    active = (gate_pre * sigmoid_gate * up_pre).astype(BF16)
    gate_grad = active_grad * up_pre * sigmoid_gate * (1.0 + gate_pre * (1.0 - sigmoid_gate))
    up_grad = active_grad * gate_pre * sigmoid_gate
    return active, jnp.concatenate([gate_grad.astype(BF16), up_grad.astype(BF16)], 1)


def rows_kernel(
    expert_ref, rows_ref, cot_ref, use_ref, router_ref, own_ref, peer_ref, *out_refs
):
    grad_ref, active_ref, front_grad_ref, cells_ref, gate_ref = out_refs
    width = own_ref.shape[1] // 3
    logits = mm(rows_ref[...], router_ref[...])
    powered = jnp.exp(logits - jnp.max(logits, -1, keepdims=True))
    router_probs = powered / jnp.sum(powered, -1, keepdims=True)
    numbers = lax.broadcasted_iota(jnp.int32, router_probs.shape, 1)
    gate = jnp.sum(jnp.where(numbers == expert_ref[0], router_probs, 0.0), -1, keepdims=True)
    gate = gate * use_ref[...]
    gate_ref[...] = gate
    cells = (cot_ref[...].astype(F32) * gate).astype(BF16)
    cells_ref[...] = cells
    total = None
    for half, weights_ref in enumerate((own_ref, peer_ref)):
        front = mm(rows_ref[...], weights_ref[:, : 2 * width])
        active_grad = mm(cells, weights_ref[:, 2 * width :])
        active, front_grad = mix_grads(front, active_grad, width)
        active_ref[:, half * width : (half + 1) * width] = active
        front_grad_ref[:, 2 * half * width : 2 * (half + 1) * width] = front_grad
        part = outer_cols(front_grad, weights_ref[:, : 2 * width])
        total = part if total is None else total + part
    grad_ref[...] = total.astype(BF16)


def expert_rows(expert, rows, cot_rows, uses, router, own, peer, tile):
    count, model_width = rows.shape
    width = own.shape[1] // 3
    part = lambda columns: pl.BlockSpec((tile, columns), lambda i, e: (i, 0))
    whole = lambda values: pl.BlockSpec(
        values.shape, lambda i, e: (0, 0), pipeline_mode=pl.Buffered(1)
    )
    outs = (model_width, 2 * width, 4 * width, model_width)
    return pl.pallas_call(
        rows_kernel,
        grid_spec=pltpu.PrefetchScalarGridSpec(
            num_scalar_prefetch=1,
            grid=(count // tile,),
            in_specs=[part(model_width), part(model_width), part(1)]
            + [whole(values) for values in (router, own, peer)],
            out_specs=[part(columns) for columns in outs + (1,)],
        ),
        out_shape=[jax.ShapeDtypeStruct((count, columns), BF16) for columns in outs]
        + [jax.ShapeDtypeStruct((count, 1), F32)],
        compiler_params=pltpu.CompilerParams(vmem_limit_bytes=ROW_VMEM),
        cost_estimate=LIGHT,
    )(expert, rows, cot_rows, uses, router, own, peer)


def mixture_kernel(active_ref, cot_ref, gate_ref, own_ref, peer_ref, mixed_ref, mixing_ref):
    width = own_ref.shape[1]
    produced = outer_cols(active_ref[:, :width], own_ref[...])
    produced = produced + outer_cols(active_ref[:, width:], peer_ref[...])
    mixing_ref[...] = jnp.sum(produced * cot_ref[...].astype(F32), -1, keepdims=True)
    mixed_ref[...] = (produced * gate_ref[...]).astype(BF16)


def expert_mixture(active, cot_rows, gates, own, peer, tile):
    count, model_width = cot_rows.shape
    width = own.shape[1] // 3
    wide = pl.BlockSpec((tile, model_width), lambda i: (i, 0))
    single = pl.BlockSpec((tile, 1), lambda i: (i, 0))
    down = pl.BlockSpec((model_width, width), lambda i: (0, 2), pipeline_mode=pl.Buffered(1))
    return pl.pallas_call(
        mixture_kernel,
        grid=(count // tile,),
        in_specs=[pl.BlockSpec((tile, 2 * width), lambda i: (i, 0)), wide, single, down, down],
        out_specs=[wide, single],
        out_shape=[
            jax.ShapeDtypeStruct((count, model_width), BF16),
            jax.ShapeDtypeStruct((count, 1), F32),
        ],
        compiler_params=pltpu.CompilerParams(vmem_limit_bytes=ROW_VMEM),
        cost_estimate=LIGHT,
    )(active, cot_rows, gates, own, peer)


PARTS = 4


def wgrad_kernel(order_ref, rows_ref, cells_ref, front_grad_ref, active_ref, *out_refs):
    number, many = pl.program_id(0), pl.num_programs(0) // PARTS
    width = active_ref.shape[1] // 2
    front = mm(rows_ref[...].T, front_grad_ref[...]).astype(BF16)
    down = mm(cells_ref[...].T, active_ref[...]).astype(BF16)
    for part in range(PARTS):

        @pl.when((number >= part * many) & (number < (part + 1) * many))
        def _():
            own_ref, peer_ref = out_refs[part], out_refs[PARTS + part]
            own_ref[0, :, : 2 * width] = front[:, : 2 * width]
            own_ref[0, :, 2 * width :] = down[:, :width]
            peer_ref[0, :, : 2 * width] = front[:, 2 * width :]
            peer_ref[0, :, 2 * width :] = down[:, width:]


def expert_wgrads(order, rows, cells, front_grad, active):
    count, model_width = rows.shape
    blocks = order.shape[0]
    many = blocks // PARTS
    size, width = model_width // blocks, active.shape[1] // 2
    columns = pl.BlockSpec((count, size), lambda i, o: (0, o[i]))
    whole = lambda values: pl.BlockSpec(
        values.shape, lambda i, o: (0, 0), pipeline_mode=pl.Buffered(1)
    )
    block = (1, size, 3 * width)

    def of_part(part):
        return pl.BlockSpec(block, lambda i, o: (jnp.clip(i - part * many, 0, many - 1), 0, 0))

    found = pl.pallas_call(
        wgrad_kernel,
        grid_spec=pltpu.PrefetchScalarGridSpec(
            num_scalar_prefetch=1,
            grid=(blocks,),
            in_specs=[columns, columns, whole(front_grad), whole(active)],
            out_specs=[of_part(part) for part in range(PARTS)] * 2,
        ),
        out_shape=[jax.ShapeDtypeStruct((many,) + block[1:], BF16)] * (2 * PARTS),
        compiler_params=pltpu.CompilerParams(vmem_limit_bytes=ROW_VMEM),
        cost_estimate=LIGHT,
    )(order, rows, cells, front_grad, active)
    return found[:PARTS], found[PARTS:]


def attention_kernel(
    query_ref, key_ref, value_ref, scale_ref, gain_ref, turn_ref, mask_ref, *out_refs
):
    rotated_query_ref, rotated_key_ref, context_ref, log_ref = out_refs
    cosine, sine = turn_ref[0], turn_ref[1]
    rotated = []
    for number, (raw_ref, out_ref) in enumerate(
        ((query_ref, rotated_query_ref), (key_ref, rotated_key_ref))
    ):
        normed = raw_ref[...] * scale_ref[number] * gain_ref[number : number + 1]
        turned = normed * cosine + pltpu.roll(normed, HEAD_DIM // 2, 1) * sine
        rotated.append(turned.astype(BF16))
        out_ref[...] = rotated[number]
    scores = outer_cols(rotated[0], rotated[1]) * HEAD_DIM ** (-0.5)
    scores = jnp.where(mask_ref[...] > 0, scores, MASKED)
    peak_value = jnp.max(scores, -1, keepdims=True)
    powered = jnp.exp(scores - peak_value)
    total_weight = jnp.sum(powered, -1, keepdims=True)
    probs = (powered / total_weight).astype(BF16)
    log_ref[0] = peak_value + jnp.log(total_weight)
    context_ref[...] = mm(probs, value_ref[...].astype(BF16)).astype(BF16)


def attention_grad_kernel(
    query_ref,
    key_ref,
    value_ref,
    scale_ref,
    gain_ref,
    turn_ref,
    mask_ref,
    rotated_query_ref,
    rotated_key_ref,
    log_ref,
    context_grad_ref,
    query_grad_ref,
    key_grad_ref,
    value_grad_ref,
    gain_grad_ref,
    inner_ref,
):
    head_scale = HEAD_DIM ** (-0.5)
    cosine, sine = turn_ref[0], turn_ref[1]
    query, key = rotated_query_ref[...], rotated_key_ref[...]
    scores = outer_cols(query, key) * head_scale
    scores = jnp.where(mask_ref[...] > 0, scores, MASKED)
    probs = jnp.exp(scores - log_ref[0])
    context_grad = context_grad_ref[...]
    probs_grad = outer_cols(context_grad, value_ref[...].astype(BF16))
    value_grad_ref[...] = mm(probs.astype(BF16).T, context_grad).astype(BF16)
    scores_grad = probs * (probs_grad - jnp.sum(probs * probs_grad, -1, keepdims=True))
    scores_grad = scores_grad.astype(BF16)

    @pl.when(pl.program_id(0) == 0)
    def _():
        inner_ref[...] = jnp.zeros_like(inner_ref)

    for number, (raw_ref, grad, out_ref) in enumerate(
        (
            (query_ref, mm(scores_grad, key), query_grad_ref),
            (key_ref, mm(scores_grad.T, query), key_grad_ref),
        )
    ):
        grad = grad * head_scale
        grad = grad * cosine - pltpu.roll(grad, HEAD_DIM // 2, 1) * sine
        out_ref[...] = grad
        raw = raw_ref[...]
        gain_grad_ref[number : number + 1] = jnp.sum(
            grad * raw * scale_ref[number], 0, keepdims=True
        )
        inner_ref[number] += jnp.sum(
            grad * gain_ref[number : number + 1] * raw, -1, keepdims=True
        )


def by_heads(kernel, rows, heads, inputs, extra, outs, log_out):
    column = pl.BlockSpec((rows, HEAD_DIM), lambda h: (0, h))
    at = lambda part: pl.BlockSpec((rows, HEAD_DIM), lambda h: (0, part * heads + h))
    logs = pl.BlockSpec((1, rows, 1), lambda h: (h, 0, 0))
    pair = pl.BlockSpec((2, HEAD_DIM), lambda h: (0, h))
    whole = lambda *shape: pl.BlockSpec(shape, lambda h: (0,) * len(shape))
    in_specs = [at(0), at(1), at(2), whole(2, rows, 1), pair]
    in_specs += [whole(2, rows, HEAD_DIM), whole(rows, rows)]
    in_specs += [logs if values.ndim == 3 else column for values in extra]
    out_shape = [jax.ShapeDtypeStruct((rows, heads * HEAD_DIM), kind) for kind in outs]
    out_specs = [column] * len(outs)
    if log_out:
        out_shape += [jax.ShapeDtypeStruct((heads, rows, 1), F32)]
        out_specs += [logs]
    else:
        out_shape += [
            jax.ShapeDtypeStruct((2, heads * HEAD_DIM), F32),
            jax.ShapeDtypeStruct((2, rows, 1), F32),
        ]
        out_specs += [pair, whole(2, rows, 1)]
    return pl.pallas_call(
        kernel,
        grid=(heads,),
        in_specs=in_specs,
        out_specs=out_specs,
        out_shape=out_shape,
        cost_estimate=LIGHT,
    )(*inputs, *extra)


def body(
    tokens,
    cotangent,
    dealing,
    lengths,
    routes,
    attention_gain,
    query_weight,
    key_weight,
    value_weight,
    output_weight,
    query_gain,
    key_gain,
    ffn_gain,
    router_weight,
    gate_weight,
    up_weight,
    down_weight,
):
    groups = lax.axis_size("dp")
    me = lax.axis_index("dp")
    side = lax.axis_index("tensor")
    rows_here, model_width = tokens.shape
    per_peer = rows_here // groups
    half_peer = per_peer // 2
    half_rows = rows_here // 2
    chips = groups // 2
    moe_chips = EXPERTS // 2
    replicas = groups // EXPERTS
    expert = lax.rem(me, EXPERTS)
    expert_chip, core = expert // 2, core_index()
    expert_place = jnp.stack([expert_chip, core]).astype(jnp.int32)

    dealt = dealing.reshape(groups, rows_here)
    places = jnp.arange(rows_here, dtype=jnp.int32)
    source_block = dealt // rows_here
    own_sources = lax.dynamic_slice_in_dim(source_block, me, 1, 0)
    numbers = jnp.arange(groups, dtype=jnp.int32)[:, None]
    chosen = jnp.concatenate([source_block == me, own_sources == numbers], 0).astype(BF16)
    earlier = (places[:, None] < places[None, :]).astype(BF16)
    rank = mm(chosen, earlier).astype(jnp.int32)
    turns = jnp.arange(per_peer, dtype=jnp.int32)[None, :, None]
    listed = (rank[:, None, :] == turns) & (chosen[:, None, :] > 0)
    leaving = jnp.sum(jnp.where(listed[:groups], lax.rem(dealt, rows_here)[:, None, :], 0), -1)
    own_order = jnp.sum(jnp.where(listed[groups:], places[None, None, :], 0), -1)
    leaving = leaving.reshape(groups, 2, half_peer)
    own_order = own_order.reshape(groups, 2, half_peer)

    def by_side(table):
        first, second = table[:, 0].reshape(-1), table[:, 1].reshape(-1)
        return jnp.concatenate(
            [jnp.where(side == 0, first, second), jnp.where(side == 0, second, first)]
        )

    leaving = by_side(leaving)
    own_order = by_side(own_order)
    expert_ids = jnp.arange(EXPERTS, dtype=jnp.int32)
    uses = jnp.sum((routes[:, :, None] == expert_ids[None, None, :]).astype(F32), 1)
    reorder = (own_order[:half_rows, None] == places[None, :]).astype(BF16)
    used = mm(reorder, uses.astype(BF16))

    told = jnp.tile(used.T.astype(BF16), (groups // EXPERTS, 1)).reshape(groups, per_peer, -1)

    small = jnp.concatenate(
        [
            attention_gain,
            ffn_gain,
            query_gain.reshape(-1),
            key_gain.reshape(-1),
            router_weight.reshape(-1),
        ]
    ).astype(BF16)
    small = jnp.broadcast_to(small.reshape(1, per_peer, -1), (groups, per_peer, small.size // per_peer))
    pick = (leaving[:half_rows, None] == places[None, :]).astype(BF16)
    sent = jnp.concatenate(
        [
            mm(pick, tokens).astype(BF16).reshape(groups, half_peer, model_width),
            mm(pick, cotangent).astype(BF16).reshape(groups, half_peer, model_width),
        ],
        1,
    )
    sent = jnp.concatenate([sent, small, told], 2)
    got = lax.all_to_all(sent, "dp", split_axis=0, concat_axis=0, tiled=True)

    packed_own, packed_sibling = pack_experts(expert_place, gate_weight, up_weight, down_weight)
    packed_experts = merge_cores(expert_place, packed_own, to_sibling(packed_sibling))
    got = after(got, packed_experts)
    rows = got[:, :half_peer, :model_width].reshape(half_rows, model_width).astype(F32)
    cot_rows = got[:, half_peer:, :model_width].reshape(half_rows, model_width)
    small = got[:, :, model_width : model_width + small.shape[2]].reshape(groups, -1)
    told = got[:, :, got.shape[2] - told.shape[2] :].reshape(groups, -1)
    told = lax.dynamic_slice_in_dim(told, me // EXPERTS * EXPERTS, EXPERTS, 0)
    uses_all = told.reshape(-1, 1).astype(F32)

    shard = attention_gain.shape[0]
    gain_shard = query_gain.shape[1]
    first_gain = small[:, :shard].reshape(-1).astype(F32)
    second_gain = small[:, shard : 2 * shard].reshape(-1).astype(F32)
    at = 2 * shard
    query_scale_gain = small[:, at : at + gain_shard].reshape(-1).astype(F32)
    key_scale_gain = small[:, at + gain_shard : at + 2 * gain_shard].reshape(-1).astype(F32)
    router_full = small[:, at + 2 * gain_shard :].reshape(model_width, EXPERTS)

    norm_one = row_scale(rows)
    normed_own = (rows * norm_one * first_gain).astype(BF16)
    normed_peer = to_peer(normed_own)

    hidden_half = gate_weight.shape[2]
    across = [list(range(at, groups, EXPERTS)) for at in range(EXPERTS)]
    own_chunks = [packed_experts[0]] + [None] * (moe_chips - 1)
    peer_chunks = [None] * moe_chips

    def chip_pairs(step):
        return [(index, index ^ (2 * step)) for index in range(groups)]

    def fetch_experts(steps):
        for step in steps:
            if step > 0:
                own_chunks[step] = lax.ppermute(packed_experts[step], "dp", chip_pairs(step))

    def share_experts(steps):
        for step in steps:
            peer_chunks[step] = to_peer(own_chunks[step])

    qkv_block = jnp.concatenate([query_weight, key_weight, value_weight], 1).astype(BF16)
    qkv_full = lax.all_gather(qkv_block, "dp", axis=0, tiled=True)
    output_full = lax.all_gather(output_weight.T.astype(BF16), "dp", axis=0, tiled=True)
    within = [list(range(at, at + EXPERTS)) for at in range(0, groups, EXPERTS)]
    in_group = {} if replicas == 1 else {"axis_index_groups": within}
    fetch_experts([4, 6, 1, 2, 3])
    packed_experts = list(packed_experts)
    for step in (5, 7):
        packed_experts[step] = after(packed_experts[step], output_full)
    fetch_experts([5, 7])
    own_chunks[0] = after(own_chunks[0], normed_peer)
    share_experts([0, 1, 2, 3])
    heads_width = query_weight.shape[1]
    order = ring_order(chips)

    finish_at = jnp.cumsum(lengths[0])
    start_at = finish_at - lengths[0]
    segment_ids = jnp.sum((own_order[:, None] >= finish_at[None, :]).astype(jnp.int32), -1)
    numbers = jnp.arange(lengths.shape[1], dtype=jnp.int32)
    begins = jnp.sum(jnp.where(segment_ids[:, None] == numbers[None, :], start_at[None, :], 0), -1)
    turn_tables = rope_tables((own_order - begins).astype(F32), HEAD_DIM)
    allowed = (segment_ids[:, None] == segment_ids[None, :]) & (
        own_order[None, :] <= own_order[:, None]
    )

    normed_one = jnp.concatenate([normed_own, normed_peer], 0)
    normed_one = after(normed_one, *[own_chunks[step] for step in (1, 2, 3, 4, 6)])
    qkv = mm(normed_one, qkv_full)
    query_raw, key_raw = qkv[:, :heads_width], qkv[:, heads_width : 2 * heads_width]

    def over_sides(values):
        theirs = to_peer(values)
        return values + jnp.concatenate([theirs[:, half_rows:], theirs[:, :half_rows]], 1)

    squares = over_sides(
        jnp.stack([jnp.sum(query_raw * query_raw, -1), jnp.sum(key_raw * key_raw, -1)])
    )
    scales = lax.rsqrt(squares / model_width + EPS)[:, :, None]
    for step in (4, 6):
        own_chunks[step] = after(own_chunks[step], squares)
    share_experts([4, 6])
    heads_here = heads_width // HEAD_DIM
    head_inputs = (
        qkv,
        qkv,
        qkv,
        scales,
        jnp.stack([query_scale_gain, key_scale_gain]),
        turn_tables,
        allowed.astype(F32),
    )
    query_heads, key_heads, context, log_total = by_heads(
        attention_kernel, rows_here, heads_here, head_inputs, (), (BF16,) * 3, True
    )
    attention = outer_cols(context, output_full)
    attention = after(attention, peer_chunks[4], peer_chunks[6])
    attention = attention[:half_rows] + to_peer(
        attention[half_rows:].astype(BF16)
    ).astype(F32)
    for step in (5, 7):
        own_chunks[step] = after(own_chunks[step], attention)
    share_experts([5, 7])
    hidden = rows + attention

    norm_two = row_scale(hidden)
    normed_two = (hidden * norm_two * second_gain).astype(BF16)
    logits = mm(normed_two, router_full)
    powered_two = jnp.exp(logits - jnp.max(logits, -1, keepdims=True))
    router_probs = powered_two / jnp.sum(powered_two, -1, keepdims=True)

    def to_experts(table):
        return lax.all_to_all(table, "dp", split_axis=0, concat_axis=0, tiled=True, **in_group)


    def placed(chunks):
        size, width = chunks[0].shape
        whole = jnp.zeros((moe_chips * size, width), chunks[0].dtype)
        for step, chunk in enumerate(chunks):
            at = (expert_chip ^ step) * size
            whole = lax.dynamic_update_slice_in_dim(whole, chunk, at, 0)
        return whole

    expert_own, expert_peer = placed(own_chunks), placed(peer_chunks)
    if replicas > 1:
        expert_own, expert_peer = (
            lax.all_gather(part, "dp", axis=0, tiled=True, axis_index_groups=across)
            for part in (expert_own, expert_peer)
        )
    inputs_all = lax.all_gather(after(normed_two, own_chunks[7]), "dp", axis=0, tiled=True, **in_group)
    cot_all = lax.all_gather(cot_rows, "dp", axis=0, tiled=True, **in_group)
    input_grad, active, front_grad, cells, gates = expert_rows(
        expert[None].astype(jnp.int32),
        inputs_all,
        cot_all,
        uses_all,
        router_full,
        expert_own,
        expert_peer,
        rows_here,
    )

    def sum_experts(values):
        return lax.psum_scatter(values, "dp", scatter_dimension=0, tiled=True, **in_group)

    steps_back = [4, 1, 6, 2, 5, 3, 7, 0]
    chips_back = jnp.stack([expert_chip ^ step for step in steps_back]).astype(jnp.int32)
    block_order = chips_back if replicas == 1 else jnp.arange(moe_chips, dtype=jnp.int32)
    wgrad_own, wgrad_peer = expert_wgrads(block_order, inputs_all, cells, front_grad, active)
    normed_two_grad = after(sum_experts(input_grad), wgrad_own[0])
    mixed, mixing = expert_mixture(active, cot_all, gates, expert_own, expert_peer, rows_here)
    normed_two_grad = normed_two_grad.astype(F32)
    mixing_table = to_experts(mixing.reshape(EXPERTS, -1))
    mixture = sum_experts(after(mixed, normed_two_grad)).astype(F32)
    out_rows = (hidden + mixture).astype(BF16)

    if replicas > 1:

        def over_replicas(values):
            values = lax.psum_scatter(
                values.reshape(model_width, -1),
                "dp",
                scatter_dimension=0,
                tiled=True,
                axis_index_groups=across,
            )
            return jnp.take(values.reshape(moe_chips, -1, values.shape[1]), chips_back, axis=0)

        wgrad_own, wgrad_peer = (
            pieces_of(over_replicas(jnp.concatenate(parts, 0)), PARTS)
            for parts in (wgrad_own, wgrad_peer)
        )
    summed, wgrad_chunks, exchanged = [], [], []

    def return_wgrads(part, *others):
        exchanged.append(to_peer(after(wgrad_peer[part], *others)))
        chunks = wgrad_own[part].astype(F32) + exchanged[part].astype(F32)
        for chunk in chunks.astype(BF16):
            step = steps_back[len(summed)]
            summed.append(chunk)
            wgrad_chunks.append(
                lax.ppermute(chunk, "dp", chip_pairs(step)) if step > 0 else chunk
            )

    for part in range(PARTS - 1):
        return_wgrads(part)

    prob_grad = mixing_table.T * used
    logit_grad = (
        router_probs * (prob_grad - jnp.sum(router_probs * prob_grad, -1, keepdims=True))
    ).astype(BF16)
    router_wgrad = inner_rows(normed_two, logit_grad)
    normed_two_grad = normed_two_grad + outer_cols(logit_grad, router_full)
    ffn_gain_grad = jnp.sum(normed_two_grad * hidden * norm_two, 0)
    scaled_two = normed_two_grad * second_gain
    hidden_grad = cot_rows.astype(F32) + norm_two * (
        scaled_two - hidden * norm_two * norm_two * jnp.mean(scaled_two * hidden, -1, keepdims=True)
    )

    attn_own = hidden_grad.astype(BF16)
    attn_peer = to_peer(attn_own)
    attn_grad = jnp.concatenate([attn_own, attn_peer], 0)
    attn_grad = after(attn_grad, wgrad_chunks[0], summed[2], summed[4])
    context_grad = mm(attn_grad, output_full).astype(BF16)
    query_norm_grad, key_norm_grad, value_grad, gain_grads, inner_parts = by_heads(
        attention_grad_kernel,
        rows_here,
        heads_here,
        head_inputs,
        (query_heads, key_heads, log_total, context_grad),
        (F32, F32, BF16),
        False,
    )
    output_wgrad = inner_rows(attn_grad, context).astype(BF16)
    query_gain_grad, key_gain_grad = gain_grads
    inners = over_sides(inner_parts[:, :, 0])
    query_scale, key_scale = scales
    output_wgrad = lax.psum_scatter(output_wgrad, "dp", scatter_dimension=0, tiled=True)
    return_wgrads(PARTS - 1, attn_peer)
    query_raw_grad = (
        query_scale * query_scale_gain * query_norm_grad
        - query_raw * query_scale**3 * inners[0][:, None] / model_width
    ).astype(BF16)
    key_raw_grad = (
        key_scale * key_scale_gain * key_norm_grad
        - key_raw * key_scale**3 * inners[1][:, None] / model_width
    ).astype(BF16)
    qkv_grad = jnp.concatenate([query_raw_grad, key_raw_grad, value_grad], 1)
    ring_rows = columns_in(normed_one, order, chips)
    qkv_wgrad = inner_rows(ring_rows, qkv_grad).astype(BF16)
    normed_one_grad = outer_cols(qkv_grad, qkv_full)
    normed_one_grad = normed_one_grad[:half_rows] + to_peer(
        normed_one_grad[half_rows:].astype(BF16)
    ).astype(F32)
    attention_gain_grad = jnp.sum(normed_one_grad * rows * norm_one, 0)
    scaled_one = normed_one_grad * first_gain
    rows_grad = hidden_grad + norm_one * (
        scaled_one - rows * norm_one * norm_one * jnp.mean(scaled_one * rows, -1, keepdims=True)
    )

    small_grad = jnp.concatenate(
        [
            query_gain_grad.reshape(groups, -1),
            key_gain_grad.reshape(groups, -1),
            attention_gain_grad.reshape(groups, -1),
            ffn_gain_grad.reshape(groups, -1),
            router_wgrad.reshape(groups, -1),
        ],
        1,
    )
    small_grad = jnp.sum(
        lax.all_to_all(small_grad, "dp", split_axis=0, concat_axis=0, tiled=True), 0
    )
    at = 2 * gain_shard
    by_rows = small_grad[at:]
    by_rows = by_rows + to_peer(by_rows)

    place_back = (places[:, None] == leaving[None, :]).astype(BF16)

    def send_back(values):
        back = values.reshape(groups, half_peer, model_width)
        back = lax.all_to_all(back, "dp", split_axis=0, concat_axis=0, tiled=True)
        back = back.reshape(half_rows, model_width)
        return mm(place_back, jnp.concatenate([back, to_peer(back)], 0)).astype(BF16)

    block_out = send_back(after(out_rows, qkv_grad))
    token_grad = send_back(rows_grad.astype(BF16))
    qkv_wgrad = after(qkv_wgrad, wgrad_chunks[0], wgrad_chunks[2], summed[6])
    qkv_wgrad = ring_scatter(pieces_of(qkv_wgrad, chips), chips, BF16, ((by_rows, wgrad_chunks[4]), token_grad, block_out))
    returned = jnp.stack(wgrad_chunks).reshape(moe_chips, 2, -1, 3 * hidden_half)
    of_sibling = to_sibling(lax.dynamic_index_in_dim(returned, 1 - core, 1, keepdims=False))
    gate_weight_grad, up_weight_grad, down_weight_grad = unpack_experts(
        jnp.append(chips_back, core).astype(jnp.int32), returned, of_sibling
    )
    return (
        block_out,
        token_grad,
        by_rows[:shard],
        qkv_wgrad[:, :heads_width],
        qkv_wgrad[:, heads_width : 2 * heads_width],
        qkv_wgrad[:, 2 * heads_width :],
        output_wgrad.T.astype(F32),
        small_grad[:gain_shard][None],
        small_grad[gain_shard:at][None],
        by_rows[shard : 2 * shard],
        by_rows[2 * shard :].reshape(router_weight.shape),
        gate_weight_grad,
        up_weight_grad,
        down_weight_grad,
    )


def solution(mesh):
    rows = P("dp", None)
    columns = P("tensor", "dp")
    inputs = (rows, rows, P(), rows, rows, P("dp"))
    inputs += (P("dp", "tensor"),) * 3 + (columns,) * 3 + (P("dp"), rows)
    inputs += (P(None, "dp", "tensor"),) * 2 + (P(None, "tensor", "dp"),)
    outputs = (rows, rows, P("dp")) + (P("dp", "tensor"),) * 3 + (columns,) * 3
    outputs += (P("dp"), rows) + (P(None, "dp", "tensor"),) * 2 + (P(None, "tensor", "dp"),)
    return jax.shard_map(body, mesh=mesh, in_specs=inputs, out_specs=outputs, check_vma=False)
```

```python
import jax
import jax.numpy as jnp
from jax import lax
from jax.experimental import pallas as pl
from jax.experimental.pallas import tpu as pltpu
from jax.sharding import PartitionSpec as P

HEAD_DIM = 128
EXPERTS = 16
EPS = 1e-05
ROPE_BASE = 10000.0
MASKED = -1e30
F32 = jnp.float32
BF16 = jnp.bfloat16


def row_scale(values):
    return lax.rsqrt(jnp.mean(values * values, -1, keepdims=True) + EPS)


def mm(left, right):
    return lax.dot_general(left, right, (((1,), (0,)), ((), ())), preferred_element_type=F32)


def inner_rows(left, right):
    return lax.dot_general(left, right, (((0,), (0,)), ((), ())), preferred_element_type=F32)


def outer_cols(left, right):
    return lax.dot_general(left, right, (((1,), (1,)), ((), ())), preferred_element_type=F32)


def rope_tables(positions, head_size):
    half_size = head_size // 2
    freq_table = ROPE_BASE ** (-2.0 * jnp.arange(half_size, dtype=F32) / head_size)
    angles = positions[:, None] * freq_table[None, :]
    cosines, sines = jnp.cos(angles), jnp.sin(angles)
    return jnp.stack(
        [jnp.concatenate([cosines, cosines], -1), jnp.concatenate([-sines, sines], -1)]
    )


def after(value, *others):
    return lax.optimization_barrier((value, others))[0]


def ring_chip(place, chips):
    return 2 * place if place < chips // 2 else 2 * (chips - 1 - place) + 1


def core_index():
    return lax.axis_index("dp") % 2


def flow_pairs(chips):
    pairs = []
    for first in range(0, lax.axis_size("dp"), 2 * chips):
        for place in range(chips):
            here = ring_chip(place, chips)
            for core, step in ((0, 1), (1, -1)):
                there = ring_chip((place + step) % chips, chips)
                pairs.append((first + 2 * here + core, first + 2 * there + core))
    return pairs


def ring_order(chips):
    chip = (lax.axis_index("dp") // 2) % chips
    place = jnp.where(chip % 2 == 0, chip // 2, chips - 1 - chip // 2)
    toward = jnp.where(core_index() == 0, -1, 1)
    offsets = [0]
    for step in range(1, chips // 2):
        offsets += [toward * step, -toward * step]
    offsets.append(chips // 2)
    places = [lax.rem(place + offset + chips, chips) for offset in offsets]
    return jnp.stack(
        [jnp.where(at < chips // 2, 2 * at, 2 * (chips - 1 - at) + 1) for at in places]
    )


def to_sibling(values):
    pairs = [(index, index ^ 1) for index in range(lax.axis_size("dp"))]
    return lax.ppermute(values, "dp", pairs)


def to_peer(values):
    return lax.ppermute(values, "tensor", [(0, 1), (1, 0)])


def by_core(mine, sibling, axis=0):
    return jnp.where(
        core_index() == 0,
        jnp.concatenate([mine, sibling], axis),
        jnp.concatenate([sibling, mine], axis),
    )


def core_part(values, core):
    size = values.shape[0] // 2
    return lax.dynamic_slice_in_dim(values, core * size, size, 0)


def ring_scatter(parts, chips, kind, waits=()):
    core, pairs = core_index(), flow_pairs(chips)
    parts = [part.astype(F32) for part in parts]
    theirs = to_sibling(core_part(parts[-1], 1 - core).astype(kind)).astype(F32)
    flow = lax.ppermute((core_part(parts[-1], core) + theirs).astype(kind), "dp", pairs)
    none = jnp.zeros_like(flow)
    flow = by_core(flow, none).astype(F32)
    for step in range(chips // 2 - 1, 0, -1):
        theirs = to_sibling(parts[2 * step - 1].astype(kind)).astype(F32)
        flow = after((parts[2 * step] + theirs + flow).astype(kind), *waits[-step:][:1])
        flow = lax.ppermute(flow, "dp", pairs).astype(F32)
    total = parts[0] + flow
    theirs = to_sibling(core_part(total, 1 - core).astype(kind)).astype(F32)
    return core_part(total, core) + theirs


def pieces_of(values, count, axis=0):
    size = values.shape[axis] // count
    return [lax.slice_in_dim(values, at * size, (at + 1) * size, axis=axis) for at in range(count)]


def columns_in(values, order, count):
    size = values.shape[1] // count
    blocks = [lax.dynamic_slice_in_dim(values, order[at] * size, size, 1) for at in range(count)]
    return jnp.concatenate(blocks, 1)


def pack_kernel(place_ref, gate_ref, up_ref, down_ref, own_ref, sibling_ref):
    width = gate_ref.shape[2]
    for out_ref, core in ((own_ref, place_ref[1]), (sibling_ref, 1 - place_ref[1])):
        out_ref[0, :, :width] = gate_ref[core].astype(BF16)
        out_ref[0, :, width : 2 * width] = up_ref[core].astype(BF16)
        out_ref[0, :, 2 * width :] = down_ref[core].T.astype(BF16)


def pack_experts(place, gate_weight, up_weight, down_weight):
    count, shard, width = gate_weight.shape
    side_in = pl.BlockSpec((2, shard, width), lambda k, p: (p[0] ^ k, 0, 0))
    down_in = pl.BlockSpec((2, width, shard), lambda k, p: (p[0] ^ k, 0, 0))
    out = pl.BlockSpec((1, shard, 3 * width), lambda k, p: (k, 0, 0))
    return pl.pallas_call(
        pack_kernel,
        grid_spec=pltpu.PrefetchScalarGridSpec(
            num_scalar_prefetch=1,
            grid=(count // 2,),
            in_specs=[side_in, side_in, down_in],
            out_specs=[out, out],
        ),
        out_shape=[jax.ShapeDtypeStruct((count // 2, shard, 3 * width), BF16)] * 2,
    )(place, gate_weight, up_weight, down_weight)


def merge_kernel(place_ref, own_ref, sibling_ref, out_ref):
    size = own_ref.shape[1]
    for part_ref, core in ((own_ref, place_ref[1]), (sibling_ref, 1 - place_ref[1])):
        out_ref[0, pl.ds(pl.multiple_of(core * size, size), size)] = part_ref[0]


def merge_cores(place, own, sibling):
    chips, size, width = own.shape
    part = pl.BlockSpec((1, size, width), lambda k, p: (k, 0, 0))
    return pl.pallas_call(
        merge_kernel,
        grid_spec=pltpu.PrefetchScalarGridSpec(
            num_scalar_prefetch=1,
            grid=(chips,),
            in_specs=[part, part],
            out_specs=pl.BlockSpec((1, 2 * size, width), lambda k, p: (k, 0, 0)),
        ),
        out_shape=jax.ShapeDtypeStruct((chips, 2 * size, width), own.dtype),
    )(place, own, sibling)


def unpack_kernel(place_ref, own_ref, sibling_ref, gate_ref, up_ref, down_ref):
    width = gate_ref.shape[2]
    own_core = place_ref[pl.num_programs(0)]
    for chunk, core in ((own_ref[0, 0], own_core), (sibling_ref[0], 1 - own_core)):
        chunk = chunk.astype(F32)
        gate_ref[core] = chunk[:, :width]
        up_ref[core] = chunk[:, width : 2 * width]
        down_ref[core] = chunk[:, 2 * width :].T


def unpack_experts(place, own, sibling):
    chips, _, shard, width = own.shape
    width = width // 3
    side_out = pl.BlockSpec((2, shard, width), lambda k, p: (p[k], 0, 0))
    down_out = pl.BlockSpec((2, width, shard), lambda k, p: (p[k], 0, 0))
    sides = jax.ShapeDtypeStruct((2 * chips, shard, width), F32)
    return pl.pallas_call(
        unpack_kernel,
        grid_spec=pltpu.PrefetchScalarGridSpec(
            num_scalar_prefetch=1,
            grid=(chips,),
            in_specs=[
                pl.BlockSpec((1, 1, shard, 3 * width), lambda k, p: (k, p[chips], 0, 0)),
                pl.BlockSpec((1, shard, 3 * width), lambda k, p: (k, 0, 0)),
            ],
            out_specs=[side_out, side_out, down_out],
        ),
        out_shape=[sides, sides, jax.ShapeDtypeStruct((2 * chips, width, shard), F32)],
    )(place, own, sibling)


ROW_VMEM = 48 * 1024 * 1024
LIGHT = pl.CostEstimate(flops=1024, bytes_accessed=1024, transcendentals=0)


def mix_grads(front, active_grad, width):
    gate_pre, up_pre = front[:, :width], front[:, width:]
    sigmoid_gate = 1.0 / (1.0 + jnp.exp(-gate_pre))
    active = (gate_pre * sigmoid_gate * up_pre).astype(BF16)
    gate_grad = active_grad * up_pre * sigmoid_gate * (1.0 + gate_pre * (1.0 - sigmoid_gate))
    up_grad = active_grad * gate_pre * sigmoid_gate
    return active, jnp.concatenate([gate_grad.astype(BF16), up_grad.astype(BF16)], 1)


def rows_kernel(
    expert_ref, rows_ref, cot_ref, use_ref, router_ref, own_ref, peer_ref, *out_refs
):
    grad_ref, active_ref, front_grad_ref, cells_ref, gate_ref = out_refs
    width = own_ref.shape[1] // 3
    logits = mm(rows_ref[...], router_ref[...])
    powered = jnp.exp(logits - jnp.max(logits, -1, keepdims=True))
    router_probs = powered / jnp.sum(powered, -1, keepdims=True)
    numbers = lax.broadcasted_iota(jnp.int32, router_probs.shape, 1)
    gate = jnp.sum(jnp.where(numbers == expert_ref[0], router_probs, 0.0), -1, keepdims=True)
    gate = gate * use_ref[...]
    gate_ref[...] = gate
    cells = (cot_ref[...].astype(F32) * gate).astype(BF16)
    cells_ref[...] = cells
    total = None
    for half, weights_ref in enumerate((own_ref, peer_ref)):
        front = mm(rows_ref[...], weights_ref[:, : 2 * width])
        active_grad = mm(cells, weights_ref[:, 2 * width :])
        active, front_grad = mix_grads(front, active_grad, width)
        active_ref[:, half * width : (half + 1) * width] = active
        front_grad_ref[:, 2 * half * width : 2 * (half + 1) * width] = front_grad
        part = outer_cols(front_grad, weights_ref[:, : 2 * width])
        total = part if total is None else total + part
    grad_ref[...] = total.astype(BF16)


def expert_rows(expert, rows, cot_rows, uses, router, own, peer, tile):
    count, model_width = rows.shape
    width = own.shape[1] // 3
    part = lambda columns: pl.BlockSpec((tile, columns), lambda i, e: (i, 0))
    whole = lambda values: pl.BlockSpec(
        values.shape, lambda i, e: (0, 0), pipeline_mode=pl.Buffered(1)
    )
    outs = (model_width, 2 * width, 4 * width, model_width)
    return pl.pallas_call(
        rows_kernel,
        grid_spec=pltpu.PrefetchScalarGridSpec(
            num_scalar_prefetch=1,
            grid=(count // tile,),
            in_specs=[part(model_width), part(model_width), part(1)]
            + [whole(values) for values in (router, own, peer)],
            out_specs=[part(columns) for columns in outs + (1,)],
        ),
        out_shape=[jax.ShapeDtypeStruct((count, columns), BF16) for columns in outs]
        + [jax.ShapeDtypeStruct((count, 1), F32)],
        compiler_params=pltpu.CompilerParams(vmem_limit_bytes=ROW_VMEM),
        cost_estimate=LIGHT,
    )(expert, rows, cot_rows, uses, router, own, peer)


def mixture_kernel(active_ref, cot_ref, gate_ref, own_ref, peer_ref, mixed_ref, mixing_ref):
    width = own_ref.shape[1]
    produced = outer_cols(active_ref[:, :width], own_ref[...])
    produced = produced + outer_cols(active_ref[:, width:], peer_ref[...])
    mixing_ref[...] = jnp.sum(produced * cot_ref[...].astype(F32), -1, keepdims=True)
    mixed_ref[...] = (produced * gate_ref[...]).astype(BF16)


def expert_mixture(active, cot_rows, gates, own, peer, tile):
    count, model_width = cot_rows.shape
    width = own.shape[1] // 3
    wide = pl.BlockSpec((tile, model_width), lambda i: (i, 0))
    single = pl.BlockSpec((tile, 1), lambda i: (i, 0))
    down = pl.BlockSpec((model_width, width), lambda i: (0, 2), pipeline_mode=pl.Buffered(1))
    return pl.pallas_call(
        mixture_kernel,
        grid=(count // tile,),
        in_specs=[pl.BlockSpec((tile, 2 * width), lambda i: (i, 0)), wide, single, down, down],
        out_specs=[wide, single],
        out_shape=[
            jax.ShapeDtypeStruct((count, model_width), BF16),
            jax.ShapeDtypeStruct((count, 1), F32),
        ],
        compiler_params=pltpu.CompilerParams(vmem_limit_bytes=ROW_VMEM),
        cost_estimate=LIGHT,
    )(active, cot_rows, gates, own, peer)


PARTS = 4


def wgrad_kernel(order_ref, rows_ref, cells_ref, front_grad_ref, active_ref, *out_refs):
    number, many = pl.program_id(0), pl.num_programs(0) // PARTS
    width = active_ref.shape[1] // 2
    front = mm(rows_ref[...].T, front_grad_ref[...]).astype(BF16)
    down = mm(cells_ref[...].T, active_ref[...]).astype(BF16)
    for part in range(PARTS):

        @pl.when((number >= part * many) & (number < (part + 1) * many))
        def _():
            own_ref, peer_ref = out_refs[part], out_refs[PARTS + part]
            own_ref[0, :, : 2 * width] = front[:, : 2 * width]
            own_ref[0, :, 2 * width :] = down[:, :width]
            peer_ref[0, :, : 2 * width] = front[:, 2 * width :]
            peer_ref[0, :, 2 * width :] = down[:, width:]


def expert_wgrads(order, rows, cells, front_grad, active):
    count, model_width = rows.shape
    blocks = order.shape[0]
    many = blocks // PARTS
    size, width = model_width // blocks, active.shape[1] // 2
    columns = pl.BlockSpec((count, size), lambda i, o: (0, o[i]))
    whole = lambda values: pl.BlockSpec(
        values.shape, lambda i, o: (0, 0), pipeline_mode=pl.Buffered(1)
    )
    block = (1, size, 3 * width)

    def of_part(part):
        return pl.BlockSpec(block, lambda i, o: (jnp.clip(i - part * many, 0, many - 1), 0, 0))

    found = pl.pallas_call(
        wgrad_kernel,
        grid_spec=pltpu.PrefetchScalarGridSpec(
            num_scalar_prefetch=1,
            grid=(blocks,),
            in_specs=[columns, columns, whole(front_grad), whole(active)],
            out_specs=[of_part(part) for part in range(PARTS)] * 2,
        ),
        out_shape=[jax.ShapeDtypeStruct((many,) + block[1:], BF16)] * (2 * PARTS),
        compiler_params=pltpu.CompilerParams(vmem_limit_bytes=ROW_VMEM),
        cost_estimate=LIGHT,
    )(order, rows, cells, front_grad, active)
    return found[:PARTS], found[PARTS:]


def attention_kernel(
    query_ref, key_ref, value_ref, scale_ref, gain_ref, turn_ref, mask_ref, *out_refs
):
    rotated_query_ref, rotated_key_ref, context_ref, log_ref = out_refs
    cosine, sine = turn_ref[0], turn_ref[1]
    rotated = []
    for number, (raw_ref, out_ref) in enumerate(
        ((query_ref, rotated_query_ref), (key_ref, rotated_key_ref))
    ):
        normed = raw_ref[...] * scale_ref[number] * gain_ref[number : number + 1]
        turned = normed * cosine + pltpu.roll(normed, HEAD_DIM // 2, 1) * sine
        rotated.append(turned.astype(BF16))
        out_ref[...] = rotated[number]
    scores = outer_cols(rotated[0], rotated[1]) * HEAD_DIM ** (-0.5)
    scores = jnp.where(mask_ref[...] > 0, scores, MASKED)
    peak_value = jnp.max(scores, -1, keepdims=True)
    powered = jnp.exp(scores - peak_value)
    total_weight = jnp.sum(powered, -1, keepdims=True)
    probs = (powered / total_weight).astype(BF16)
    log_ref[0] = peak_value + jnp.log(total_weight)
    context_ref[...] = mm(probs, value_ref[...].astype(BF16)).astype(BF16)


def attention_grad_kernel(
    query_ref,
    key_ref,
    value_ref,
    scale_ref,
    gain_ref,
    turn_ref,
    mask_ref,
    rotated_query_ref,
    rotated_key_ref,
    log_ref,
    context_grad_ref,
    query_grad_ref,
    key_grad_ref,
    value_grad_ref,
    gain_grad_ref,
    inner_ref,
):
    head_scale = HEAD_DIM ** (-0.5)
    cosine, sine = turn_ref[0], turn_ref[1]
    query, key = rotated_query_ref[...], rotated_key_ref[...]
    scores = outer_cols(query, key) * head_scale
    scores = jnp.where(mask_ref[...] > 0, scores, MASKED)
    probs = jnp.exp(scores - log_ref[0])
    context_grad = context_grad_ref[...]
    probs_grad = outer_cols(context_grad, value_ref[...].astype(BF16))
    value_grad_ref[...] = mm(probs.astype(BF16).T, context_grad).astype(BF16)
    scores_grad = probs * (probs_grad - jnp.sum(probs * probs_grad, -1, keepdims=True))
    scores_grad = scores_grad.astype(BF16)

    @pl.when(pl.program_id(0) == 0)
    def _():
        inner_ref[...] = jnp.zeros_like(inner_ref)

    for number, (raw_ref, grad, out_ref) in enumerate(
        (
            (query_ref, mm(scores_grad, key), query_grad_ref),
            (key_ref, mm(scores_grad.T, query), key_grad_ref),
        )
    ):
        grad = grad * head_scale
        grad = grad * cosine - pltpu.roll(grad, HEAD_DIM // 2, 1) * sine
        out_ref[...] = grad
        raw = raw_ref[...]
        gain_grad_ref[number : number + 1] = jnp.sum(
            grad * raw * scale_ref[number], 0, keepdims=True
        )
        inner_ref[number] += jnp.sum(
            grad * gain_ref[number : number + 1] * raw, -1, keepdims=True
        )


def by_heads(kernel, rows, heads, inputs, extra, outs, log_out):
    column = pl.BlockSpec((rows, HEAD_DIM), lambda h: (0, h))
    at = lambda part: pl.BlockSpec((rows, HEAD_DIM), lambda h: (0, part * heads + h))
    logs = pl.BlockSpec((1, rows, 1), lambda h: (h, 0, 0))
    pair = pl.BlockSpec((2, HEAD_DIM), lambda h: (0, h))
    whole = lambda *shape: pl.BlockSpec(shape, lambda h: (0,) * len(shape))
    in_specs = [at(0), at(1), at(2), whole(2, rows, 1), pair]
    in_specs += [whole(2, rows, HEAD_DIM), whole(rows, rows)]
    in_specs += [logs if values.ndim == 3 else column for values in extra]
    out_shape = [jax.ShapeDtypeStruct((rows, heads * HEAD_DIM), kind) for kind in outs]
    out_specs = [column] * len(outs)
    if log_out:
        out_shape += [jax.ShapeDtypeStruct((heads, rows, 1), F32)]
        out_specs += [logs]
    else:
        out_shape += [
            jax.ShapeDtypeStruct((2, heads * HEAD_DIM), F32),
            jax.ShapeDtypeStruct((2, rows, 1), F32),
        ]
        out_specs += [pair, whole(2, rows, 1)]
    return pl.pallas_call(
        kernel,
        grid=(heads,),
        in_specs=in_specs,
        out_specs=out_specs,
        out_shape=out_shape,
        cost_estimate=LIGHT,
    )(*inputs, *extra)


def body(
    tokens,
    cotangent,
    dealing,
    lengths,
    routes,
    attention_gain,
    query_weight,
    key_weight,
    value_weight,
    output_weight,
    query_gain,
    key_gain,
    ffn_gain,
    router_weight,
    gate_weight,
    up_weight,
    down_weight,
):
    groups = lax.axis_size("dp")
    me = lax.axis_index("dp")
    side = lax.axis_index("tensor")
    rows_here, model_width = tokens.shape
    per_peer = rows_here // groups
    half_peer = per_peer // 2
    half_rows = rows_here // 2
    chips = groups // 2
    moe_chips = EXPERTS // 2
    replicas = groups // EXPERTS
    expert = lax.rem(me, EXPERTS)
    expert_chip, core = expert // 2, core_index()
    expert_place = jnp.stack([expert_chip, core]).astype(jnp.int32)

    dealt = dealing.reshape(groups, rows_here)
    places = jnp.arange(rows_here, dtype=jnp.int32)
    source_block = dealt // rows_here
    own_sources = lax.dynamic_slice_in_dim(source_block, me, 1, 0)
    numbers = jnp.arange(groups, dtype=jnp.int32)[:, None]
    chosen = jnp.concatenate([source_block == me, own_sources == numbers], 0).astype(BF16)
    earlier = (places[:, None] < places[None, :]).astype(BF16)
    rank = mm(chosen, earlier).astype(jnp.int32)
    turns = jnp.arange(per_peer, dtype=jnp.int32)[None, :, None]
    listed = (rank[:, None, :] == turns) & (chosen[:, None, :] > 0)
    leaving = jnp.sum(jnp.where(listed[:groups], lax.rem(dealt, rows_here)[:, None, :], 0), -1)
    own_order = jnp.sum(jnp.where(listed[groups:], places[None, None, :], 0), -1)
    leaving = leaving.reshape(groups, 2, half_peer)
    own_order = own_order.reshape(groups, 2, half_peer)

    def by_side(table):
        first, second = table[:, 0].reshape(-1), table[:, 1].reshape(-1)
        return jnp.concatenate(
            [jnp.where(side == 0, first, second), jnp.where(side == 0, second, first)]
        )

    leaving = by_side(leaving)
    own_order = by_side(own_order)
    expert_ids = jnp.arange(EXPERTS, dtype=jnp.int32)
    uses = jnp.sum((routes[:, :, None] == expert_ids[None, None, :]).astype(F32), 1)
    reorder = (own_order[:half_rows, None] == places[None, :]).astype(BF16)
    used = mm(reorder, uses.astype(BF16))

    told = jnp.tile(used.T.astype(BF16), (groups // EXPERTS, 1)).reshape(groups, per_peer, -1)

    small = jnp.concatenate(
        [
            attention_gain,
            ffn_gain,
            query_gain.reshape(-1),
            key_gain.reshape(-1),
            router_weight.reshape(-1),
        ]
    ).astype(BF16)
    small = jnp.broadcast_to(small.reshape(1, per_peer, -1), (groups, per_peer, small.size // per_peer))
    pick = (leaving[:half_rows, None] == places[None, :]).astype(BF16)
    sent = jnp.concatenate(
        [
            mm(pick, tokens).astype(BF16).reshape(groups, half_peer, model_width),
            mm(pick, cotangent).astype(BF16).reshape(groups, half_peer, model_width),
        ],
        1,
    )
    sent = jnp.concatenate([sent, small, told], 2)
    got = lax.all_to_all(sent, "dp", split_axis=0, concat_axis=0, tiled=True)

    packed_own, packed_sibling = pack_experts(expert_place, gate_weight, up_weight, down_weight)
    packed_experts = merge_cores(expert_place, packed_own, to_sibling(packed_sibling))
    got = after(got, packed_experts)
    rows = got[:, :half_peer, :model_width].reshape(half_rows, model_width).astype(F32)
    cot_rows = got[:, half_peer:, :model_width].reshape(half_rows, model_width)
    small = got[:, :, model_width : model_width + small.shape[2]].reshape(groups, -1)
    told = got[:, :, got.shape[2] - told.shape[2] :].reshape(groups, -1)
    told = lax.dynamic_slice_in_dim(told, me // EXPERTS * EXPERTS, EXPERTS, 0)
    uses_all = told.reshape(-1, 1).astype(F32)

    shard = attention_gain.shape[0]
    gain_shard = query_gain.shape[1]
    first_gain = small[:, :shard].reshape(-1).astype(F32)
    second_gain = small[:, shard : 2 * shard].reshape(-1).astype(F32)
    at = 2 * shard
    query_scale_gain = small[:, at : at + gain_shard].reshape(-1).astype(F32)
    key_scale_gain = small[:, at + gain_shard : at + 2 * gain_shard].reshape(-1).astype(F32)
    router_full = small[:, at + 2 * gain_shard :].reshape(model_width, EXPERTS)

    norm_one = row_scale(rows)
    normed_own = (rows * norm_one * first_gain).astype(BF16)
    normed_peer = to_peer(normed_own)

    hidden_half = gate_weight.shape[2]
    across = [list(range(at, groups, EXPERTS)) for at in range(EXPERTS)]
    own_chunks = [packed_experts[0]] + [None] * (moe_chips - 1)
    peer_chunks = [None] * moe_chips

    def chip_pairs(step):
        return [(index, index ^ (2 * step)) for index in range(groups)]

    def fetch_experts(steps):
        for step in steps:
            if step > 0:
                own_chunks[step] = lax.ppermute(packed_experts[step], "dp", chip_pairs(step))

    def share_experts(steps):
        for step in steps:
            peer_chunks[step] = to_peer(own_chunks[step])

    qkv_block = jnp.concatenate([query_weight, key_weight, value_weight], 1).astype(BF16)
    qkv_full = lax.all_gather(qkv_block, "dp", axis=0, tiled=True)
    output_full = lax.all_gather(output_weight.T.astype(BF16), "dp", axis=0, tiled=True)
    within = [list(range(at, at + EXPERTS)) for at in range(0, groups, EXPERTS)]
    in_group = {} if replicas == 1 else {"axis_index_groups": within}
    fetch_experts([4, 6, 1, 2, 3])
    packed_experts = list(packed_experts)
    for step in (5, 7):
        packed_experts[step] = after(packed_experts[step], output_full)
    fetch_experts([5, 7])
    own_chunks[0] = after(own_chunks[0], normed_peer)
    share_experts([0, 1, 2, 3])
    heads_width = query_weight.shape[1]
    order = ring_order(chips)

    finish_at = jnp.cumsum(lengths[0])
    start_at = finish_at - lengths[0]
    segment_ids = jnp.sum((own_order[:, None] >= finish_at[None, :]).astype(jnp.int32), -1)
    numbers = jnp.arange(lengths.shape[1], dtype=jnp.int32)
    begins = jnp.sum(jnp.where(segment_ids[:, None] == numbers[None, :], start_at[None, :], 0), -1)
    turn_tables = rope_tables((own_order - begins).astype(F32), HEAD_DIM)
    allowed = (segment_ids[:, None] == segment_ids[None, :]) & (
        own_order[None, :] <= own_order[:, None]
    )

    normed_one = jnp.concatenate([normed_own, normed_peer], 0)
    normed_one = after(normed_one, *[own_chunks[step] for step in (1, 2, 3, 4, 6)])
    qkv = mm(normed_one, qkv_full)
    query_raw, key_raw = qkv[:, :heads_width], qkv[:, heads_width : 2 * heads_width]

    def over_sides(values):
        theirs = to_peer(values)
        return values + jnp.concatenate([theirs[:, half_rows:], theirs[:, :half_rows]], 1)

    squares = over_sides(
        jnp.stack([jnp.sum(query_raw * query_raw, -1), jnp.sum(key_raw * key_raw, -1)])
    )
    scales = lax.rsqrt(squares / model_width + EPS)[:, :, None]
    for step in (4, 6):
        own_chunks[step] = after(own_chunks[step], squares)
    share_experts([4, 6])
    heads_here = heads_width // HEAD_DIM
    head_inputs = (
        qkv,
        qkv,
        qkv,
        scales,
        jnp.stack([query_scale_gain, key_scale_gain]),
        turn_tables,
        allowed.astype(F32),
    )
    query_heads, key_heads, context, log_total = by_heads(
        attention_kernel, rows_here, heads_here, head_inputs, (), (BF16,) * 3, True
    )
    attention = outer_cols(context, output_full)
    attention = after(attention, peer_chunks[4], peer_chunks[6])
    attention = attention[:half_rows] + to_peer(
        attention[half_rows:].astype(BF16)
    ).astype(F32)
    for step in (5, 7):
        own_chunks[step] = after(own_chunks[step], attention)
    share_experts([5, 7])
    hidden = rows + attention

    norm_two = row_scale(hidden)
    normed_two = (hidden * norm_two * second_gain).astype(BF16)
    logits = mm(normed_two, router_full)
    powered_two = jnp.exp(logits - jnp.max(logits, -1, keepdims=True))
    router_probs = powered_two / jnp.sum(powered_two, -1, keepdims=True)

    def to_experts(table):
        return lax.all_to_all(table, "dp", split_axis=0, concat_axis=0, tiled=True, **in_group)


    def placed(chunks):
        size, width = chunks[0].shape
        whole = jnp.zeros((moe_chips * size, width), chunks[0].dtype)
        for step, chunk in enumerate(chunks):
            at = (expert_chip ^ step) * size
            whole = lax.dynamic_update_slice_in_dim(whole, chunk, at, 0)
        return whole

    expert_own, expert_peer = placed(own_chunks), placed(peer_chunks)
    if replicas > 1:
        expert_own, expert_peer = (
            lax.all_gather(part, "dp", axis=0, tiled=True, axis_index_groups=across)
            for part in (expert_own, expert_peer)
        )
    inputs_all = lax.all_gather(after(normed_two, own_chunks[7]), "dp", axis=0, tiled=True, **in_group)
    cot_all = lax.all_gather(cot_rows, "dp", axis=0, tiled=True, **in_group)
    input_grad, active, front_grad, cells, gates = expert_rows(
        expert[None].astype(jnp.int32),
        inputs_all,
        cot_all,
        uses_all,
        router_full,
        expert_own,
        expert_peer,
        rows_here,
    )

    def sum_experts(values):
        return lax.psum_scatter(values, "dp", scatter_dimension=0, tiled=True, **in_group)

    steps_back = [4, 1, 6, 2, 5, 3, 7, 0]
    chips_back = jnp.stack([expert_chip ^ step for step in steps_back]).astype(jnp.int32)
    block_order = chips_back if replicas == 1 else jnp.arange(moe_chips, dtype=jnp.int32)
    wgrad_own, wgrad_peer = expert_wgrads(block_order, inputs_all, cells, front_grad, active)
    normed_two_grad = after(sum_experts(input_grad), wgrad_own[0])
    mixed, mixing = expert_mixture(active, cot_all, gates, expert_own, expert_peer, rows_here)
    normed_two_grad = normed_two_grad.astype(F32)
    mixing_table = to_experts(mixing.reshape(EXPERTS, -1))
    mixture = sum_experts(after(mixed, normed_two_grad)).astype(F32)
    out_rows = (hidden + mixture).astype(BF16)

    if replicas > 1:

        def over_replicas(values):
            values = lax.psum_scatter(
                values.reshape(model_width, -1),
                "dp",
                scatter_dimension=0,
                tiled=True,
                axis_index_groups=across,
            )
            return jnp.take(values.reshape(moe_chips, -1, values.shape[1]), chips_back, axis=0)

        wgrad_own, wgrad_peer = (
            pieces_of(over_replicas(jnp.concatenate(parts, 0)), PARTS)
            for parts in (wgrad_own, wgrad_peer)
        )
    summed, wgrad_chunks, exchanged = [], [], []

    def return_wgrads(part, *others):
        exchanged.append(to_peer(after(wgrad_peer[part], *others)))
        chunks = wgrad_own[part].astype(F32) + exchanged[part].astype(F32)
        for chunk in chunks.astype(BF16):
            step = steps_back[len(summed)]
            summed.append(chunk)
            wgrad_chunks.append(
                lax.ppermute(chunk, "dp", chip_pairs(step)) if step > 0 else chunk
            )

    for part in range(PARTS - 1):
        return_wgrads(part)

    prob_grad = mixing_table.T * used
    logit_grad = (
        router_probs * (prob_grad - jnp.sum(router_probs * prob_grad, -1, keepdims=True))
    ).astype(BF16)
    router_wgrad = inner_rows(normed_two, logit_grad)
    normed_two_grad = normed_two_grad + outer_cols(logit_grad, router_full)
    ffn_gain_grad = jnp.sum(normed_two_grad * hidden * norm_two, 0)
    scaled_two = normed_two_grad * second_gain
    hidden_grad = cot_rows.astype(F32) + norm_two * (
        scaled_two - hidden * norm_two * norm_two * jnp.mean(scaled_two * hidden, -1, keepdims=True)
    )

    attn_own = hidden_grad.astype(BF16)
    attn_peer = to_peer(attn_own)
    attn_grad = jnp.concatenate([attn_own, attn_peer], 0)
    attn_grad = after(attn_grad, wgrad_chunks[0], summed[2], summed[4])
    context_grad = mm(attn_grad, output_full).astype(BF16)
    query_norm_grad, key_norm_grad, value_grad, gain_grads, inner_parts = by_heads(
        attention_grad_kernel,
        rows_here,
        heads_here,
        head_inputs,
        (query_heads, key_heads, log_total, context_grad),
        (F32, F32, BF16),
        False,
    )
    output_wgrad = inner_rows(attn_grad, context).astype(BF16)
    query_gain_grad, key_gain_grad = gain_grads
    inners = over_sides(inner_parts[:, :, 0])
    query_scale, key_scale = scales
    output_wgrad = lax.psum_scatter(output_wgrad, "dp", scatter_dimension=0, tiled=True)
    return_wgrads(PARTS - 1, attn_peer)
    query_raw_grad = (
        query_scale * query_scale_gain * query_norm_grad
        - query_raw * query_scale**3 * inners[0][:, None] / model_width
    ).astype(BF16)
    key_raw_grad = (
        key_scale * key_scale_gain * key_norm_grad
        - key_raw * key_scale**3 * inners[1][:, None] / model_width
    ).astype(BF16)
    qkv_grad = jnp.concatenate([query_raw_grad, key_raw_grad, value_grad], 1)
    ring_rows = columns_in(normed_one, order, chips)
    qkv_wgrad = inner_rows(ring_rows, qkv_grad).astype(BF16)
    normed_one_grad = outer_cols(qkv_grad, qkv_full)
    normed_one_grad = normed_one_grad[:half_rows] + to_peer(
        normed_one_grad[half_rows:].astype(BF16)
    ).astype(F32)
    attention_gain_grad = jnp.sum(normed_one_grad * rows * norm_one, 0)
    scaled_one = normed_one_grad * first_gain
    rows_grad = hidden_grad + norm_one * (
        scaled_one - rows * norm_one * norm_one * jnp.mean(scaled_one * rows, -1, keepdims=True)
    )

    small_grad = jnp.concatenate(
        [
            query_gain_grad.reshape(groups, -1),
            key_gain_grad.reshape(groups, -1),
            attention_gain_grad.reshape(groups, -1),
            ffn_gain_grad.reshape(groups, -1),
            router_wgrad.reshape(groups, -1),
        ],
        1,
    )
    small_grad = jnp.sum(
        lax.all_to_all(small_grad, "dp", split_axis=0, concat_axis=0, tiled=True), 0
    )
    at = 2 * gain_shard
    by_rows = small_grad[at:]
    by_rows = by_rows + to_peer(by_rows)

    place_back = (places[:, None] == leaving[None, :]).astype(BF16)

    def send_back(values):
        back = values.reshape(groups, half_peer, model_width)
        back = lax.all_to_all(back, "dp", split_axis=0, concat_axis=0, tiled=True)
        back = back.reshape(half_rows, model_width)
        return mm(place_back, jnp.concatenate([back, to_peer(back)], 0)).astype(BF16)

    block_out = send_back(after(out_rows, qkv_grad))
    token_grad = send_back(rows_grad.astype(BF16))
    qkv_wgrad = after(qkv_wgrad, wgrad_chunks[0], wgrad_chunks[2], summed[6])
    qkv_wgrad = ring_scatter(pieces_of(qkv_wgrad, chips), chips, BF16, ((by_rows, wgrad_chunks[4]), (token_grad, wgrad_chunks[6]), block_out))
    returned = jnp.stack(wgrad_chunks).reshape(moe_chips, 2, -1, 3 * hidden_half)
    of_sibling = to_sibling(lax.dynamic_index_in_dim(returned, 1 - core, 1, keepdims=False))
    gate_weight_grad, up_weight_grad, down_weight_grad = unpack_experts(
        jnp.append(chips_back, core).astype(jnp.int32), returned, of_sibling
    )
    return (
        block_out,
        token_grad,
        by_rows[:shard],
        qkv_wgrad[:, :heads_width],
        qkv_wgrad[:, heads_width : 2 * heads_width],
        qkv_wgrad[:, 2 * heads_width :],
        output_wgrad.T.astype(F32),
        small_grad[:gain_shard][None],
        small_grad[gain_shard:at][None],
        by_rows[shard : 2 * shard],
        by_rows[2 * shard :].reshape(router_weight.shape),
        gate_weight_grad,
        up_weight_grad,
        down_weight_grad,
    )


def solution(mesh):
    rows = P("dp", None)
    columns = P("tensor", "dp")
    inputs = (rows, rows, P(), rows, rows, P("dp"))
    inputs += (P("dp", "tensor"),) * 3 + (columns,) * 3 + (P("dp"), rows)
    inputs += (P(None, "dp", "tensor"),) * 2 + (P(None, "tensor", "dp"),)
    outputs = (rows, rows, P("dp")) + (P("dp", "tensor"),) * 3 + (columns,) * 3
    outputs += (P("dp"), rows) + (P(None, "dp", "tensor"),) * 2 + (P(None, "tensor", "dp"),)
    return jax.shard_map(body, mesh=mesh, in_specs=inputs, out_specs=outputs, check_vma=False)
```
